32 devices in a mesh: fsdp: 16 (over z, x, core), tp: 2 (over y).
Axes of the slice: x: 2, y: 2, z: 4, core: 2. Of those that a mesh axis runs over, the one named last changes fastest.
Arguments:
- tokens: bfloat16 [2, 2048, 1792], P(None, ('fsdp', 'tp')), may hold values from -6 to 6
- doc_starts: int32 [2, 2048], P(None, 'fsdp'), may hold values from 0 to 1, as said below
- w_qkv: bfloat16 [3, 1792, 1792], P(None, 'fsdp', 'tp'), may hold values from -0.125 to 0.125
- w_out: bfloat16 [1792, 1792], P('tp', 'fsdp'), may hold values from -0.375 to 0.375
- w_gate_up: bfloat16 [2, 1792, 4864], P(None, 'fsdp', 'tp'), may hold values from -0.125 to 0.125
- w_down: bfloat16 [4864, 1792], P('tp', 'fsdp'), may hold values from -0.078125 to 0.078125
- gains: bfloat16 [2, 1792], P(None, 'fsdp'), may hold values from 0.5 to 1.5
- cotangent: bfloat16 [2, 2048, 1792], P(None, ('fsdp', 'tp')), may hold values from -6 to 6
Outputs:
- output: bfloat16 [2, 2048, 1792], P(None, ('fsdp', 'tp'))
- input_grad: float32 [2, 2048, 1792], P(None, ('fsdp', 'tp'))
- grad_qkv: float32 [3, 1792, 1792], P(None, 'fsdp', 'tp')
- grad_out: float32 [1792, 1792], P('tp', 'fsdp')
- grad_gate_up: float32 [2, 1792, 4864], P(None, 'fsdp', 'tp')
- grad_down: float32 [4864, 1792], P('tp', 'fsdp')
- grad_gains: float32 [2, 1792], P(None, 'fsdp')
The draws below stay inside these ranges and needn't reach their ends.
Inputs may be any that keep to these rules, and one draw needn't show every extreme that they name: `doc_starts`: each micro-batch's first position starts a document. In one micro-batch drawn from the seed a single document starts at position 64 and runs to position 1984 or beyond.
All inputs are finite; a program needn't handle non-finite values.
Results may differ from the reference program's by a relative error of at most 0.015.
Values may be sent and summed in bfloat16 or wider, within the bound.
A program may use at most 320 MiB of HBM per device.

```python
import jax
import jax.numpy as jnp
from jax import lax

D = 1792
H = 16
DH = 112
FF = 4864
WINDOW = 64
MB = 2
TOK_DEV = 128
TOKENS = 2048


def draw_doc_starts(key, part):
    key = jax.random.fold_in(key, 7)
    key_power, key_length, key_pick = jax.random.split(key, 3)
    number_docs = TOKENS // 4 + 1
    powers = jax.random.randint(key_power, (MB, number_docs), 2, 12)
    least = jnp.left_shift(jnp.ones_like(powers), powers)
    lengths = jax.random.randint(key_length, (MB, number_docs), least, 2 * least)
    starts = jnp.minimum(jnp.cumsum(lengths, axis=1) - lengths, TOKENS)
    batch_index = jnp.broadcast_to(jnp.arange(MB)[:, None], starts.shape)
    marks = jnp.zeros((MB, TOKENS + 1), jnp.int32).at[batch_index, starts].set(1)[:, :TOKENS]
    chosen = jax.random.randint(key_pick, (), 0, MB)
    position = jnp.arange(TOKENS)
    inside = (position >= TOK_DEV // 2) & (position < TOKENS - TOK_DEV // 2)
    single = (position == TOK_DEV // 2).astype(jnp.int32)
    spanning = jnp.where(inside[None, :], single[None, :], marks)
    return jnp.where(jnp.arange(MB)[:, None] == chosen, spanning, marks).astype(jnp.int32)


def with_spikes(values, key, source, target, blocks, factor):
    owner, partner = [(jnp.arange(values.shape[dim]) // (values.shape[dim] // blocks)).reshape([-1 if axis == dim else 1 for axis in range(values.ndim)]) for dim in (source, target)]
    chosen = jax.random.permutation(key, blocks)[partner]
    strong = (owner == chosen) | (owner == (partner + blocks // 2) % blocks)
    return jnp.where(strong, factor * values, values)


def steps_of(key, dims, cuts, low, high):
    loudness, own = 1.0, jax.random.fold_in(key, 6)
    for dim, blocks in cuts:
        steps = jnp.exp(jax.random.uniform(jax.random.fold_in(own, dim), (blocks,), jnp.float32, low / len(cuts), high / len(cuts)))
        loudness = loudness * jnp.repeat(steps, dims[dim] // blocks).reshape([-1 if axis == dim else 1 for axis in range(len(dims))])
    return loudness


def gaussian(stream_key, shape, spread, bound, cuts=(), kind=jnp.bfloat16):
    loudness = steps_of(stream_key, shape, cuts, -0.22, 0.18) if cuts else 1.0
    values = jax.random.normal(stream_key, shape, jnp.float32) * spread * loudness
    return jnp.minimum(jnp.maximum(values, -bound), bound).astype(kind)


def bell_draw_with(own_key, extent, spread, bound, cuts, heavy, kind=jnp.bfloat16):
    values = spread * jax.random.normal(own_key, extent, jnp.float32)
    if cuts:
        values = values * steps_of(own_key, extent, cuts, -0.22, 0.18)
    return jnp.clip(with_spikes(values, jax.random.fold_in(own_key, 3), *heavy), -bound, bound).astype(kind)


def setup_inputs(seed: int = 0) -> dict:
    seeds = jax.random.split(jax.random.key(seed), 9)
    tokens = gaussian(seeds[0], (MB, TOKENS, D), 1.0, 6.0, ((1, 32),))
    doc_starts = draw_doc_starts(jax.random.fold_in(seeds[8], 71), 0)
    w_qkv = gaussian(seeds[2], (3, D, H * DH), D ** -0.5, 0.125, ((1, 16), (2, 2)))
    w_out = gaussian(seeds[3], (H * DH, D), (H * DH // 8) ** -0.5, 0.375, ((0, 2), (1, 16)))
    w_gate_up = gaussian(seeds[4], (2, D, FF), D ** -0.5, 0.125, ((1, 16), (2, 2)))
    w_down = gaussian(seeds[5], (FF, D), FF ** -0.5, 0.078125, ((0, 2), (1, 16)))
    gains = jnp.clip(1.0 + 0.1 * jax.random.normal(seeds[6], (2, D), jnp.float32), 0.5, 1.5).astype(jnp.bfloat16)
    cotangent = bell_draw_with(seeds[7], (MB, TOKENS, D), 1.0, 6.0, ((1, 32),), (1, 2, 32, 2.75))
    return {"tokens": tokens, "doc_starts": doc_starts, "w_qkv": w_qkv, "w_out": w_out, "w_gate_up": w_gate_up, "w_down": w_down, "gains": gains, "cotangent": cotangent}


@jax.custom_vjp
def low(v):
    return lax.optimization_barrier(v.astype(jnp.bfloat16)).astype(jnp.float32)

@jax.custom_vjp
def low_back(v):
    return v

def low_keep(v):
    return (low(v), None)

def low_pass(kept, grad):
    return (grad,)

def back_keep(v):
    return (v, None)

def back_low(kept, grad):
    return (low(grad),)
low.defvjp(low_keep, low_pass)
low_back.defvjp(back_keep, back_low)
EPSILON = 1e-06
query_block = 512

def matmul(left, right):
    return jnp.dot(left, right, precision=lax.Precision.HIGHEST)

def normalize(rows, gain):
    scale = lax.rsqrt(lax.optimization_barrier(jnp.mean(rows * rows, axis=-1, keepdims=True)) + EPSILON)
    return rows * scale * gain

def block_attend(queries, keys, values, query_counts, key_counts):
    scores = jnp.einsum('ihd,jhd->hij', queries, keys, precision=lax.Precision.HIGHEST) * DH ** (-0.5)
    scores = low_back(scores)
    offset = jnp.arange(query_block)[:, None] + WINDOW - jnp.arange(query_block + WINDOW)[None, :]
    allowed = (offset >= 0) & (offset < WINDOW) & (query_counts[:, None] == key_counts[None, :])
    scores = jnp.where(allowed[None], scores, -1e+30)
    top = lax.optimization_barrier(jnp.max(scores, axis=-1, keepdims=True))
    weights = jnp.exp(scores - top)
    probs = weights / lax.optimization_barrier(jnp.sum(weights, axis=-1, keepdims=True))
    return jnp.einsum('hij,jhd->ihd', low(probs), values, precision=lax.Precision.HIGHEST)

def attend(queries, keys, values, counts):
    blocks = TOKENS // query_block

    def split(array):
        return array.reshape((blocks, query_block) + array.shape[1:])

    def with_rim(array, fill):
        parts = split(array)
        first = jnp.full((1, WINDOW) + array.shape[1:], fill, array.dtype)
        rim = jnp.concatenate([first, parts[:-1, query_block - WINDOW:]], axis=0)
        return jnp.concatenate([rim, parts], axis=1)
    checked = jax.checkpoint(block_attend)
    results = lax.map(lambda bundle: checked(*bundle), (split(queries), with_rim(keys, 0.0), with_rim(values, 0.0), split(counts), with_rim(counts, -1)))
    return results.reshape(TOKENS, H * DH)

def layer(tokens_in, gains, w_qkv, w_out, w_gate_up, w_down, counts):
    normed = low(normalize(tokens_in, gains[0]))
    projected = [low(low_back(matmul(normed, w_qkv[index]))).reshape(TOKENS, H, DH) for index in range(3)]
    heads_out = low(low_back(attend(projected[0], projected[1], projected[2], counts)))
    resid = tokens_in + low_back(matmul(heads_out, w_out))
    normed_two = low(normalize(resid, gains[1]))
    gate = low_back(matmul(normed_two, w_gate_up[0]))
    upward = low_back(matmul(normed_two, w_gate_up[1]))
    hidden = low(jax.nn.silu(gate) * upward)
    return resid + low_back(matmul(hidden, w_down))

def reference(tokens, doc_starts, w_qkv, w_out, w_gate_up, w_down, gains, cotangent):
    weights = tuple((array.astype(jnp.float32) for array in (gains, w_qkv, w_out, w_gate_up, w_down)))
    totals = tuple((jnp.zeros(array.shape, jnp.float32) for array in weights))
    outputs = []
    input_grads = []
    for batch in range(MB):
        counts = jnp.cumsum(doc_starts[batch]).astype(jnp.int32)

        def forward(tokens_in, gain_rows, qkv_rows, out_rows, gate_rows, down_rows):
            return layer(tokens_in, gain_rows, qkv_rows, out_rows, gate_rows, down_rows, counts)
        result, pullback = jax.vjp(forward, tokens[batch].astype(jnp.float32), *weights)
        grads = pullback(cotangent[batch].astype(jnp.float32))
        outputs.append(result.astype(jnp.bfloat16))
        input_grads.append(grads[0])
        totals = tuple((total + grad for total, grad in zip(totals, grads[1:])))
    return (jnp.stack(outputs), jnp.stack(input_grads), totals[1], totals[2], totals[3], totals[4], totals[0])
```

```python
import functools

import jax
import jax.numpy as jnp
from jax import lax
from jax.experimental import pallas as pl
from jax.experimental.pallas import tpu as pltpu
from jax.sharding import PartitionSpec as P

DH = 112
HP = 128
WINDOW = 64
EPSILON = 1e-06
SUB = 4
BF = jnp.bfloat16
F32 = jnp.float32
NN = (((1,), (0,)), ((), ()))
NT = (((1,), (1,)), ((), ()))
TN = (((0,), (0,)), ((), ()))


def dot(a, b, dims):
    return lax.dot_general(a, b, dims, preferred_element_type=F32)


def flat(value):
    return value.reshape(-1, value.shape[-1])


def half_of(cols):
    return (cols // 256) * 128


class Kernel:
    def __init__(self, cfg, refs):
        self.cfg = cfg
        self.__dict__.update(refs)
        f = lax.axis_index("fsdp")
        self.y = lax.axis_index("tp")
        self.r = f // SUB
        self.s = f % SUB
        core = self.s % 2
        self.sib = self.s + 1 - 2 * core
        self.xn = (self.s + 2) % SUB
        self.diag = (self.sib + 2) % SUB
        self.yn = 1 - self.y
        self.up = (self.r + 1) % cfg["R"]
        self.down = (self.r + cfg["R"] - 1) % cfg["R"]
        self.count = 0
        self.local_count = 0
        self.sends = []
        self.gathered = []

    def dev(self, r, s, y):
        return {"fsdp": r * SUB + s, "tp": y}

    def barrier(self):
        sem = pltpu.get_barrier_semaphore()
        partners = [self.dev(self.r, s, self.y) for s in (self.sib, self.xn, self.diag)]
        partners += [self.dev(self.r, self.s, self.yn)]
        partners += [self.dev(r, self.s, self.y) for r in (self.up, self.down)]
        for partner in partners:
            pl.semaphore_signal(sem, inc=1, device_id=partner, device_id_type=pl.DeviceIdType.MESH)
        pl.semaphore_wait(sem, len(partners))

    def remote(self, src, dst, device):
        k = self.count
        self.count += 1
        copy = pltpu.make_async_remote_copy(
            src_ref=src,
            dst_ref=dst,
            send_sem=self.send_sems.at[k],
            recv_sem=self.recv_sems.at[k],
            device_id=device,
            device_id_type=pl.DeviceIdType.MESH,
        )
        copy.start()
        self.sends.append(copy)
        return copy

    def to_sib(self, src, dst):
        return self.remote(src, dst, self.dev(self.r, self.sib, self.y))

    def to_x(self, src, dst):
        return self.remote(src, dst, self.dev(self.r, self.xn, self.y))

    def to_y(self, src, dst):
        return self.remote(src, dst, self.dev(self.r, self.s, self.yn))

    def to_up(self, src, dst):
        return self.remote(src, dst, self.dev(self.up, self.s, self.y))

    def to_down(self, src, dst):
        return self.remote(src, dst, self.dev(self.down, self.s, self.y))

    def local(self, src, dst):
        k = self.local_count
        self.local_count += 1
        copy = pltpu.make_async_copy(src, dst, self.local_sems.at[k])
        copy.start()
        return copy


    def block(self, ref, b, cols=slice(None)):
        rows = self.cfg["BR"]
        return ref.at[pl.ds(pl.multiple_of(b * rows, 16), rows), cols]

    def share_rows(self, ref, s):
        db = self.cfg["DB"]
        return ref.at[pl.ds(pl.multiple_of(self.r * self.cfg["BR"] + s * db, 16), db), :]

    def columns_out(self, shares, full):
        if self.cfg["exchanged"]:
            copies = [self.local(shares, self.block(full, self.r))]
            return lambda: [c.wait() for c in copies]
        mine = self.share_rows(full, self.s)
        copies = [
            self.remote(shares.at[s], mine, self.dev(self.r, s, self.y))
            for s in (self.xn, self.diag, self.sib)
        ]
        own = self.local(shares.at[self.s], mine)

        def wait():
            for c in copies:
                c.wait_recv()
            own.wait()

        return wait

    def columns_back(self, full, result):
        if self.cfg["exchanged"]:
            own = self.local(self.block(full, self.r), result)
            return own.wait
        copies = [
            self.remote(self.share_rows(full, s), result.at[self.s], self.dev(self.r, s, self.y))
            for s in (self.xn, self.diag, self.sib)
        ]
        own = self.local(self.share_rows(full, self.s), result.at[self.s])

        def wait():
            for c in copies:
                c.wait_recv()
            own.wait()

        return wait

    def ring_gather(self, full, step):
        ring, cols = self.cfg["R"], full.shape[1]
        low, high = slice(None), slice(None)
        if step == ring // 2:
            low, high = slice(0, half_of(cols)), slice(half_of(cols), cols)
        ahead = (self.r + ring - step + 1) % ring
        back = (self.r + step - 1) % ring
        a = self.block(full, ahead, low)
        b = self.block(full, back, high)
        pair = (self.to_up(a, a), self.to_down(b, b))
        self.gathered += pair

        def wait():
            for c in pair:
                c.wait_recv()

        return wait

    def ring_gather_rest(self, full, wait):
        for step in range(2, self.cfg["R"] // 2 + 1):
            wait()
            wait = self.ring_gather(full, step)
        return wait

    def ring_scatter(self, grad, slots, step):
        ring, cols = self.cfg["R"], grad.shape[1]
        first_up, first_down, rest_up, rest_down = slots
        low, high = slice(None), slice(None)
        if step == 1:
            low, high = slice(0, half_of(cols)), slice(half_of(cols), cols)
            to_up, to_down = first_up, first_down
        else:
            to_up, to_down = rest_up.at[step - 2], rest_down.at[step - 2]
        width = cols
        if step == 1:
            to_up = to_up.at[:, : half_of(cols)]
            to_down = to_down.at[:, : cols - half_of(cols)]
        else:
            to_up, to_down = to_up.at[:, :width], to_down.at[:, :width]
        distance = ring // 2 - step + 1
        ahead = (self.r + distance) % ring
        back = (self.r + ring - distance) % ring
        pair = (
            self.to_up(self.block(grad, ahead, low), to_up),
            self.to_down(self.block(grad, back, high), to_down),
        )

        def add():
            for c in pair:
                c.wait_recv()
            near = ring // 2 - step
            targets = [((self.r + near) % ring, low, to_up), ((self.r + ring - near) % ring, high, to_down)]
            tile = next(t for t in (112, 64, 16) if self.cfg["BR"] % t == 0)
            for i in range(self.cfg["BR"] // tile):
                if near == 0:
                    rows = pl.ds(pl.multiple_of(self.r * self.cfg["BR"] + i * tile, 16), tile)
                    part = slice(i * tile, (i + 1) * tile)
                    total = grad[rows, :].astype(F32) + to_up[part, :].astype(F32) + to_down[part, :].astype(F32)
                    grad[rows, :] = total.astype(BF)
                else:
                    for b, span, ref in targets:
                        rows = pl.ds(pl.multiple_of(b * self.cfg["BR"] + i * tile, 16), tile)
                        part = slice(i * tile, (i + 1) * tile)
                        total = grad[rows, span].astype(F32) + ref[part, :].astype(F32)
                        grad[rows, span] = total.astype(BF)

        return pair, add


    def gather_start(self, buf):
        own = buf.at[self.s, self.y]
        return {"x": self.to_x(own, own), "y": self.to_y(own, own), "own": self.to_sib(own, own), "buf": buf}

    def gather_relay(self, g):
        buf, cut = g["buf"], self.cfg["cut"]
        g["x"].wait_recv()
        part = buf.at[self.xn, self.y, :, slice(0, cut)]
        g["d0"] = self.to_y(part, part)
        whole = buf.at[self.xn, self.y]
        g["fx"] = self.to_sib(whole, whole)
        g["y"].wait_recv()
        part = buf.at[self.s, self.yn, :, slice(cut, self.cfg["D"])]
        g["d1"] = self.to_x(part, part)
        whole = buf.at[self.s, self.yn]
        g["fy"] = self.to_sib(whole, whole)

    def gather_finish(self, g):
        buf, cut = g["buf"], self.cfg["cut"]
        g["d0"].wait_recv()
        part = buf.at[self.xn, self.yn, :, slice(0, cut)]
        f0 = self.to_sib(part, part)
        g["d1"].wait_recv()
        part = buf.at[self.xn, self.yn, :, slice(cut, self.cfg["D"])]
        f1 = self.to_sib(part, part)
        for c in (g["own"], g["fx"], g["fy"], f0, f1):
            c.wait_recv()
        g["copies"] = [g[n] for n in ("own", "x", "y", "d0", "d1", "fx", "fy")] + [f0, f1]

    def scatter_pair(self, st, partial):
        sc, rc = st["sc"], st["rc"]
        copies = []
        for k, pair in enumerate(((self.sib + 2) % SUB, self.sib)):
            sc[k] = partial(pair).astype(BF).reshape(sc.shape[1:])
            copies.append(self.to_sib(sc.at[k], rc.at[k]))
        return {"pair": copies, "st": st}

    def scatter_send(self, g, partial):
        st, cut, d = g["st"], self.cfg["cut"], self.cfg["D"]
        so, rc = st["so"], st["rc"]
        lo, hi = slice(0, cut), slice(cut, d)
        value = partial(self.xn)
        g["pair"][0].wait_recv()
        so[0] = (value + flat(rc[0].astype(F32))).astype(BF).reshape(so.shape[1:])
        g["d0"] = self.to_x(so.at[0, self.yn, :, lo], st["rd0"])
        g["d1"] = self.to_y(so.at[0, self.yn, :, hi], st["rd1"])
        g["x0"] = self.to_x(so.at[0, self.y, :, lo], st["rx"].at[:, lo])
        value = partial(self.s)
        g["pair"][1].wait_recv()
        so[1] = (value + flat(rc[1].astype(F32))).astype(BF).reshape(so.shape[1:])
        g["y1"] = self.to_y(so.at[1, self.yn, :, hi], st["ry"].at[:, hi])

    def scatter_relay(self, g):
        st, cut, d = g["st"], self.cfg["cut"], self.cfg["D"]
        so = st["so"]
        lo, hi = slice(0, cut), slice(cut, d)
        g["d1"].wait_recv()
        so[0, self.y, :, hi] = (so[0, self.y, :, hi].astype(F32) + st["rd1"][...].astype(F32)).astype(BF)
        g["x1"] = self.to_x(so.at[0, self.y, :, hi], st["rx"].at[:, hi])
        g["d0"].wait_recv()
        so[1, self.yn, :, lo] = (so[1, self.yn, :, lo].astype(F32) + st["rd0"][...].astype(F32)).astype(BF)
        g["y0"] = self.to_y(so.at[1, self.yn, :, lo], st["ry"].at[:, lo])

    def scatter_finish(self, g):
        st = g["st"]
        for name in ("x0", "x1", "y0", "y1"):
            g[name].wait_recv()
        total = st["so"][1, self.y].astype(F32) + st["rx"][...].astype(F32) + st["ry"][...].astype(F32)
        self.settle(g["pair"] + [g[n] for n in ("d0", "d1", "x0", "x1", "y0", "y1")])
        return total


    def project(self, w):
        def step(i, _):
            rows = flat(self.u1[i])
            out = dot(rows, w[...], NN).astype(BF)
            self.qkv[pl.ds(1 + 2 * i, 2)] = out.reshape(2, 2 * WINDOW, out.shape[1])
            return 0

        lax.fori_loop(0, SUB, step, 0)

    def masks(self, quad):
        before, own = self.starts[quad], self.starts[quad + 1]
        lane = lax.broadcasted_iota(jnp.int32, before.shape, 1)
        even = jnp.where(lane < WINDOW, pltpu.roll(before, WINDOW, 1), pltpu.roll(own, WINDOW, 1))
        shape = (WINDOW, 2 * WINDOW)
        i = lax.broadcasted_iota(jnp.int32, shape, 0)
        j = lax.broadcasted_iota(jnp.int32, shape, 1)
        square = (2 * WINDOW, 2 * WINDOW)
        later = lax.broadcasted_iota(jnp.int32, square, 0) > lax.broadcasted_iota(jnp.int32, square, 1)
        later = later.astype(F32).astype(BF)
        band = (j <= i + WINDOW) & (j > i)
        result = []
        for rows in (even, own):
            per_batch = []
            for batch in range(2):
                line = jnp.broadcast_to(rows[batch : batch + 1, :], shape)
                line = jnp.where(j <= i + WINDOW, line, 0.0).astype(BF)
                between = dot(line, later, NN)
                per_batch.append(band & (between < 0.5))
            result.append(per_batch)
        return result

    def tile(self, index, batch, part, head):
        cols = slice(part * 2 * HP + head * HP, part * 2 * HP + (head + 1) * HP)
        return self.qkv[index, batch * WINDOW : (batch + 1) * WINDOW, cols]

    def attend(self):
        def step(n, _):
            quad = SUB - 1 - n
            allowed = self.masks(quad)
            for half in range(2):
                p = 2 * quad + half
                for batch in range(2):
                    for head in range(2):
                        q = self.tile(p + 1, batch, 0, head)
                        k = jnp.concatenate([self.tile(p, batch, 1, head), self.tile(p + 1, batch, 1, head)], axis=0)
                        v = jnp.concatenate([self.tile(p, batch, 2, head), self.tile(p + 1, batch, 2, head)], axis=0)
                        scores = dot(q, k, NT) * DH ** (-0.5)
                        scores = jnp.where(allowed[half][batch], scores, -1e30)
                        top = jnp.max(scores, axis=-1, keepdims=True)
                        weights = jnp.exp(scores - top)
                        probs = weights / jnp.sum(weights, axis=-1, keepdims=True)
                        self.probs[p, 2 * batch + head] = probs
                        out = dot(probs.astype(BF), v, NN).astype(BF)
                        self.heads[quad, half, batch * WINDOW : (batch + 1) * WINDOW, head * HP : (head + 1) * HP] = out
            return 0

        lax.fori_loop(0, SUB, step, 0)

    def attend_back_quad(self, quad):
        for half in range(2):
            p = 2 * quad + half
            for batch in range(2):
                rows = slice(batch * WINDOW, (batch + 1) * WINDOW)
                for head in range(2):
                    cols = slice(head * HP, (head + 1) * HP)
                    q = self.tile(p + 1, batch, 0, head)
                    k = jnp.concatenate([self.tile(p, batch, 1, head), self.tile(p + 1, batch, 1, head)], axis=0)
                    v = jnp.concatenate([self.tile(p, batch, 2, head), self.tile(p + 1, batch, 2, head)], axis=0)
                    probs = self.probs[p, 2 * batch + head]
                    d_out = self.d_heads[quad, half, rows, cols]
                    d_probs = dot(d_out, v, NT)
                    inner = jnp.sum(probs * d_probs, axis=-1, keepdims=True)
                    d_scores = (probs * (d_probs - inner)).astype(BF)
                    d_q = dot(d_scores, k, NN) * DH ** (-0.5)
                    d_k = dot(d_scores, q, TN) * DH ** (-0.5)
                    d_v = dot(probs.astype(BF), d_out, TN)
                    self.qkv[p + 1, rows, head * HP : (head + 1) * HP] = d_q.astype(BF)
                    for part, grad in ((1, d_k), (2, d_v)):
                        slot = slice((part - 1) * 2 * HP + head * HP, (part - 1) * 2 * HP + (head + 1) * HP)
                        place = slice(part * 2 * HP + head * HP, part * 2 * HP + (head + 1) * HP)
                        done = self.carry[rows, slot] + grad[:WINDOW]
                        self.qkv[p, rows, place] = done.astype(BF)
                        self.carry[rows, slot] = grad[WINDOW:]

    def grad_into(self, target, left, right):
        width = 256

        def step(m, _):
            cols = pl.ds(pl.multiple_of(m * width, width), width)
            a = flat(left[:, :, :, cols])
            target[cols, :] = dot(a, right(), TN).astype(BF)
            return 0

        lax.fori_loop(0, self.cfg["D"] // width, step, 0)

    def feed_forward(self):
        ff = self.w_dn.shape[1]

        def step(i, _):
            rows = flat(self.u2[i])
            gate = dot(rows, self.w_gu[:, :ff], NN)
            upward = dot(rows, self.w_gu[:, ff:], NN)
            d_hidden = dot(flat(self.g[i]), self.w_dn[...], NN)
            sig = jax.nn.sigmoid(gate)
            silu = gate * sig
            shape = (2, 2 * WINDOW, ff)
            self.hidden[i] = (silu * upward).astype(BF).reshape(shape)
            d_gate = d_hidden * upward * sig * (1.0 + gate * (1.0 - sig))
            self.d_gu[i, :, :, :ff] = d_gate.astype(BF).reshape(shape)
            self.d_gu[i, :, :, ff:] = (d_hidden * silu).astype(BF).reshape(shape)
            return 0

        lax.fori_loop(0, SUB, step, 0)

    def run(self):
        cfg = self.cfg
        me = (self.s, self.y)
        norm = lambda v: lax.rsqrt(jnp.mean(v * v, axis=-1, keepdims=True) + EPSILON)
        steps = cfg["R"] // 2

        self.barrier()
        qkv_here = self.columns_out(self.sh_qkv, self.w_qkv)
        start_copies = [
            self.remote(self.starts_in, self.starts.at[self.s + 1], self.dev(self.r, s, self.y))
            for s in (self.sib, self.xn, self.diag)
        ]
        self.starts[self.s + 1] = self.starts_in[...]

        x = self.x[...].astype(F32)
        self.u1[me] = (x * norm(x)).astype(BF)
        gather_one = self.gather_start(self.u1)
        out_here = self.columns_out(self.sh_out, self.w_out)
        qkv_here()
        ring_qkv = self.ring_gather(self.w_qkv, 1)
        gu_here = self.columns_out(self.sh_gu, self.w_gu)
        for c in start_copies:
            c.wait_recv()
        rim_starts = self.to_up(self.starts.at[SUB], self.starts.at[0])
        self.gather_relay(gather_one)
        out_here()
        ring_qkv = self.ring_gather_rest(self.w_qkv, ring_qkv)
        ring_out = self.ring_gather(self.w_out, 1)
        gu_here()
        ring_gu = self.ring_gather(self.w_gu, 1)
        self.gather_finish(gather_one)
        self.g[me] = self.g_in[...]
        gather_g = self.gather_start(self.g)
        dn_here = self.columns_out(self.sh_dn, self.w_dn)
        ring_qkv()

        self.project(self.w_qkv)
        rims = [
            self.to_up(self.qkv.at[2 * SUB, :, part], self.qkv.at[0, :, part])
            for part in (slice(2 * HP, 4 * HP), slice(4 * HP, 6 * HP))
        ]
        ring_out = self.ring_gather_rest(self.w_out, ring_out)
        self.gather_relay(gather_g)
        rim_starts.wait_recv()
        for c in rims:
            c.wait_recv()
        self.attend()
        self.gather_finish(gather_g)
        dn_here()
        ring_out()

        partial = lambda pair: dot(flat(self.heads[pair]), self.w_out[...], NT)
        stage = {n: getattr(self, n) for n in ("sc", "rc", "so", "rd0", "rd1", "rx", "ry")}
        scatter = self.scatter_pair(stage, partial)
        self.scatter_send(scatter, partial)
        self.scatter_relay(scatter)
        ring_gu = self.ring_gather_rest(self.w_gu, ring_gu)
        ring_dn = self.ring_gather(self.w_dn, 1)
        self.resid[...] = self.x[...].astype(F32) + self.scatter_finish(scatter)
        resid = self.resid[...]
        self.u2[me] = (resid * norm(resid)).astype(BF)
        gather_two = self.gather_start(self.u2)
        self.gather_relay(gather_two)
        self.gather_finish(gather_two)
        ring_gu()
        ring_dn = self.ring_gather_rest(self.w_dn, ring_dn)
        ring_dn()

        self.feed_forward()
        partial = lambda pair: dot(flat(self.d_gu[pair]), self.w_gu[...], NT)
        scatter = self.scatter_pair(stage, partial)
        self.scatter_send(scatter, partial)
        self.grad_into(self.g_dn, self.g, lambda: flat(self.hidden[...]))
        dn_add = self.ring_scatter(self.g_dn, self.slots_dn, 1)[1]
        self.scatter_relay(scatter)
        self.settle(self.gathered)
        self.grad_into(self.w_gu, self.u2, lambda: flat(self.d_gu[...]))
        gu_add = self.ring_scatter(self.w_gu, self.slots_gu, 1)[1]
        d_unit = self.scatter_finish(scatter)
        resid = self.resid[...]
        scale = norm(resid)
        unit = resid * scale
        inner = jnp.mean(d_unit * unit, axis=-1, keepdims=True)
        self.d_resid[...] = self.g_in[...].astype(F32) + scale * (d_unit - unit * inner)
        self.d_r[me] = self.d_resid[...].astype(BF)
        self.settle(gather_g["copies"] + gather_two["copies"] + rims)
        gather_d = self.gather_start(self.d_r)
        dn_add = self.ring_scatter_rest(self.g_dn, self.slots_dn, dn_add)
        self.gather_relay(gather_d)
        gu_add = self.ring_scatter_rest(self.w_gu, self.slots_gu, gu_add)
        self.gather_finish(gather_d)

        def heads_back(i, _):
            value = dot(flat(self.d_r[i]), self.w_out[...], NN).astype(BF)
            self.d_heads[i] = value.reshape(2, 2 * WINDOW, 2 * HP)
            return 0

        lax.fori_loop(0, SUB, heads_back, 0)

        view = {
            "sc": self.u2.at[0:2],
            "so": self.u2.at[2:4],
            "rc": self.g.at[0:2],
            "rd0": self.g.at[2, 0, :, slice(0, cfg["cut"])],
            "rd1": self.g.at[2, 0, :, slice(cfg["cut"], cfg["D"])],
            "rx": self.g.at[2, 1],
            "ry": self.g.at[3, 0],
        }
        partial = lambda pair: dot(flat(self.hidden[pair]), self.w_dn[...], NT)
        mlp = self.scatter_pair(view, partial)
        self.scatter_send(mlp, partial)

        self.carry[...] = jnp.zeros_like(self.carry)
        self.attend_back_quad(0)
        rim_back = [
            self.to_down(self.qkv.at[0, :, part], self.rim.at[:, slice(k * 2 * HP, (k + 1) * 2 * HP)])
            for k, part in enumerate((slice(2 * HP, 4 * HP), slice(4 * HP, 6 * HP)))
        ]
        self.scatter_relay(mlp)

        def back(quad, _):
            self.attend_back_quad(quad)
            return 0

        lax.fori_loop(1, SUB, back, 0)
        for c in rim_back:
            c.wait_recv()
        done = self.carry[...] + self.rim[...].astype(F32)
        self.qkv[2 * SUB, :, 2 * HP :] = done.astype(BF)

        d_qkv = lambda: flat(self.qkv[1:])
        self.grad_into(self.g_qkv, self.u1, d_qkv)
        dn_add()
        dn_back = self.columns_back(self.g_dn, self.o_dn)
        gu_add()
        gu_back = self.columns_back(self.w_gu, self.o_gu)
        qkv_add = self.ring_scatter(self.g_qkv, self.slots_qkv, 1)[1]
        partial = lambda pair: dot(flat(self.qkv[pl.ds(1 + 2 * pair, 2)]), self.w_qkv[...], NT)
        scatter = self.scatter_pair(stage, partial)
        self.scatter_send(scatter, partial)
        self.grad_into(self.w_out, self.d_r, lambda: flat(self.heads[...]))
        qkv_add = self.ring_scatter_rest(self.g_qkv, self.slots_qkv, qkv_add)
        out_add = self.ring_scatter(self.w_out, self.slots_out, 1)[1]
        self.scatter_relay(scatter)
        self.out[...] = (self.resid[...] + self.scatter_finish(mlp)).astype(BF)
        out_add = self.ring_scatter_rest(self.w_out, self.slots_out, out_add)
        d_unit = self.scatter_finish(scatter)
        x = self.x[...].astype(F32)
        scale = norm(x)
        unit = x * scale
        inner = jnp.mean(d_unit * unit, axis=-1, keepdims=True)
        self.in_grad[...] = self.d_resid[...] + scale * (d_unit - unit * inner)
        qkv_add()
        qkv_back = self.columns_back(self.g_qkv, self.o_qkv)
        out_add()
        out_back = self.columns_back(self.w_out, self.o_out)
        for wait in (dn_back, gu_back, qkv_back, out_back):
            wait()
        self.settle()

    def ring_scatter_rest(self, grad, slots, add):
        for step in range(2, self.cfg["R"] // 2 + 1):
            add()
            add = self.ring_scatter(grad, slots, step)[1]
        return add

    def settle(self, copies=None):
        for c in self.sends:
            if copies is None or any(c is other for other in copies):
                c.wait_send()
        if copies is None:
            self.sends = []
        else:
            self.sends = [c for c in self.sends if not any(c is other for other in copies)]


def fused(cfg, cols, shares, starts, x, g):
    n_qkv, n_out, n_gu, n_dn = cols
    d, ring, br, db = cfg["D"], cfg["R"], cfg["BR"], cfg["DB"]
    rows = 2 * WINDOW
    cut = cfg["cut"]
    steps = ring // 2
    anywhere = pl.BlockSpec(memory_space=pl.ANY)
    vmem = pl.BlockSpec(memory_space=pltpu.VMEM)
    result = (br,) if cfg["exchanged"] else (SUB, db)
    outs = [
        ("out", (rows, d), BF, vmem),
        ("in_grad", (rows, d), F32, vmem),
        ("o_qkv", result + (n_qkv,), BF, anywhere),
        ("o_out", result + (n_out,), BF, anywhere),
        ("o_gu", result + (n_gu,), BF, anywhere),
        ("o_dn", result + (n_dn,), BF, anywhere),
    ]
    ins = [
        ("sh_qkv", anywhere),
        ("sh_out", anywhere),
        ("sh_gu", anywhere),
        ("sh_dn", anywhere),
        ("starts_in", vmem),
        ("x", vmem),
        ("g_in", vmem),
    ]
    plane = (SUB, 2, rows)
    wide = max(n_gu, n_qkv)
    scratch = [
        ("w_qkv", (d, n_qkv), BF),
        ("w_out", (d, n_out), BF),
        ("w_gu", (d, n_gu), BF),
        ("w_dn", (d, n_dn), BF),
        ("g_qkv", (d, n_qkv), BF),
        ("g_dn", (d, n_dn), BF),
        ("u1", plane + (d,), BF),
        ("u2", plane + (d,), BF),
        ("g", plane + (d,), BF),
        ("d_r", plane + (d,), BF),
        ("starts", (SUB + 1, 8, rows), F32),
        ("qkv", (2 * SUB + 1, rows, n_qkv), BF),
        ("probs", (2 * SUB, 4, WINDOW, 2 * WINDOW), F32),
        ("heads", plane + (n_out,), BF),
        ("d_heads", plane + (n_out,), BF),
        ("hidden", plane + (n_dn,), BF),
        ("d_gu", plane + (n_gu,), BF),
        ("carry", (rows, 4 * HP), F32),
        ("rim", (rows, 4 * HP), BF),
        ("resid", (rows, d), F32),
        ("d_resid", (rows, d), F32),
        ("sc", (2, 2, rows, d), BF),
        ("rc", (2, 2, rows, d), BF),
        ("so", (2, 2, rows, d), BF),
        ("rd0", (rows, cut), BF),
        ("rd1", (rows, d - cut), BF),
        ("rx", (rows, d), BF),
        ("ry", (rows, d), BF),
    ]
    for name, width in (("wide", wide), ("dn", n_dn), ("out", n_out)):
        high = width - half_of(width)
        scratch += [
            ("first_up_" + name, (br, high), BF),
            ("first_down_" + name, (br, high), BF),
            ("rest_up_" + name, (steps - 1, br, width), BF),
            ("rest_down_" + name, (steps - 1, br, width), BF),
        ]
    number = 110 + 4 * (6 + 4 * ring)
    names = [n for n, _ in ins] + [n for n, *_ in outs] + [n for n, *_ in scratch]
    names += ["send_sems", "recv_sems", "local_sems"]

    def kernel(*refs):
        table = dict(zip(names, refs, strict=True))
        for name, key in (("qkv", "wide"), ("gu", "wide"), ("dn", "dn"), ("out", "out")):
            table["slots_" + name] = tuple(
                table[part + key] for part in ("first_up_", "first_down_", "rest_up_", "rest_down_")
            )
        Kernel(cfg, table).run()

    results = pl.pallas_call(
        kernel,
        out_shape=[jax.ShapeDtypeStruct(shape, kind) for _, shape, kind, _ in outs],
        in_specs=[spec for _, spec in ins],
        out_specs=[spec for *_, spec in outs],
        scratch_shapes=[pltpu.VMEM(shape, kind) for _, shape, kind in scratch]
        + [
            pltpu.SemaphoreType.DMA((number,)),
            pltpu.SemaphoreType.DMA((number,)),
            pltpu.SemaphoreType.DMA((8,)),
        ],
        compiler_params=pltpu.CompilerParams(
            collective_id=0, has_side_effects=True, vmem_limit_bytes=63 * 2**20
        ),
    )(*shares, starts, x, g)
    return results


def padded(value, size):
    pads = [(0, 0)] * (value.ndim - 1) + [(0, size - value.shape[-1])]
    return jnp.pad(value, pads)


def body(ring, tokens, doc_starts, w_qkv, w_out, w_gate_up, w_down, gains, cotangent):
    batches, rows, d = tokens.shape
    db = w_qkv.shape[1]
    ff = w_gate_up.shape[2] // SUB
    ffp = -(-ff // HP) * HP
    heads = w_qkv.shape[2] // (SUB * DH)
    gain = gains.astype(F32)

    exchanged = db % 16 != 0
    groups = [[r * SUB + s for s in range(SUB)] for r in range(ring)]
    cfg = {
        "D": d,
        "R": ring,
        "DB": db,
        "BR": SUB * db,
        "cut": d // 256 * 128,
        "exchanged": exchanged,
    }

    sh_qkv = (w_qkv.astype(F32) * gain[0][None, :, None]).astype(BF).reshape(3, db, SUB, heads, DH)
    sh_qkv = padded(sh_qkv, HP).transpose(2, 1, 0, 3, 4).reshape(SUB, db, 3 * heads * HP)
    sh_out = w_out.T.reshape(db, SUB, heads, DH)
    sh_out = padded(sh_out, HP).transpose(1, 0, 2, 3).reshape(SUB, db, heads * HP)
    sh_gu = (w_gate_up.astype(F32) * gain[1][None, :, None]).astype(BF).reshape(2, db, SUB, ff)
    sh_gu = padded(sh_gu, ffp).transpose(2, 1, 0, 3).reshape(SUB, db, 2 * ffp)
    sh_dn = padded(w_down.T.reshape(db, SUB, ff), ffp).transpose(1, 0, 2)
    shares = [sh_qkv, sh_out, sh_gu, sh_dn]
    cols = [v.shape[2] for v in shares]

    def swapped(v):
        return lax.all_to_all(v, "fsdp", 0, 0, axis_index_groups=groups, tiled=True)

    if exchanged:
        shares = [swapped(v).reshape(SUB * db, v.shape[2]) for v in shares]
    starts = jnp.pad(doc_starts.astype(F32), ((0, 8 - batches), (0, 0)))
    out, in_grad, *grads = fused(
        cfg, cols, shares, starts, tokens.reshape(batches * rows, d), cotangent.reshape(batches * rows, d)
    )
    if exchanged:
        grads = [swapped(v.reshape(SUB, db, v.shape[1])) for v in grads]
    g_qkv, g_out, g_gu, g_dn = [v.astype(F32) for v in grads]
    g_qkv = g_qkv.reshape(SUB, db, 3, heads, HP)[..., :DH].transpose(2, 1, 0, 3, 4).reshape(w_qkv.shape)
    g_out = g_out.reshape(SUB, db, heads, HP)[..., :DH].transpose(0, 2, 3, 1).reshape(w_out.shape)
    g_gu = g_gu.reshape(SUB, db, 2, ffp)[..., :ff].transpose(2, 1, 0, 3).reshape(w_gate_up.shape)
    g_dn = g_dn[..., :ff].transpose(0, 2, 1).reshape(w_down.shape)
    gain_sums = jnp.stack(
        [
            jnp.sum(g_qkv * w_qkv.astype(F32), axis=(0, 2)),
            jnp.sum(g_gu * w_gate_up.astype(F32), axis=(0, 2)),
        ]
    )
    gain_sums = gain_sums + lax.ppermute(gain_sums, "tp", [(0, 1), (1, 0)])
    return (
        out.reshape(tokens.shape),
        in_grad.reshape(tokens.shape),
        g_qkv * gain[0][None, :, None],
        g_out,
        g_gu * gain[1][None, :, None],
        g_dn,
        gain_sums,
    )


def solution(mesh):
    in_specs = (
        P(None, ("fsdp", "tp"), None),
        P(None, "fsdp"),
        P(None, "fsdp", "tp"),
        P("tp", "fsdp"),
        P(None, "fsdp", "tp"),
        P("tp", "fsdp"),
        P(None, "fsdp"),
        P(None, ("fsdp", "tp"), None),
    )
    out_specs = (
        P(None, ("fsdp", "tp"), None),
        P(None, ("fsdp", "tp"), None),
        P(None, "fsdp", "tp"),
        P("tp", "fsdp"),
        P(None, "fsdp", "tp"),
        P("tp", "fsdp"),
        P(None, "fsdp"),
    )
    ring = mesh.shape["fsdp"] // SUB
    return jax.shard_map(
        functools.partial(body, ring), mesh=mesh, in_specs=in_specs, out_specs=out_specs, check_vma=False
    )
```

```python
import functools

import jax
import jax.numpy as jnp
from jax import lax
from jax.experimental import pallas as pl
from jax.experimental.pallas import tpu as pltpu
from jax.sharding import PartitionSpec as P

DH = 112
HP = 128
WINDOW = 64
EPSILON = 1e-06
SUB = 4
BF = jnp.bfloat16
F32 = jnp.float32
NN = (((1,), (0,)), ((), ()))
NT = (((1,), (1,)), ((), ()))
TN = (((0,), (0,)), ((), ()))


def dot(a, b, dims):
    return lax.dot_general(a, b, dims, preferred_element_type=F32)


def flat(value):
    return value.reshape(-1, value.shape[-1])


class Kernel:
    def __init__(self, cfg, refs):
        self.cfg = cfg
        self.__dict__.update(refs)
        self.f = lax.axis_index("fsdp")
        self.y = lax.axis_index("tp")
        core = self.f % 2
        self.x = (self.f // 2) % 2
        self.hi = self.f // 8
        self.s = (self.f // 4) % 2 * 2 + core
        self.sib = self.s + 1 - 2 * core
        self.zn = (self.s + 2) % SUB
        self.diag = (self.sib + 2) % SUB
        self.yn = 1 - self.y
        self.next_hi = (self.hi + 1) % cfg["NH"]
        self.last_hi = (self.hi + cfg["NH"] - 1) % cfg["NH"]
        self.count = 0
        self.local_count = 0
        self.sends = []
        self.gathered = []

    def index(self, hi, s, x):
        return hi * 8 + s // 2 * 4 + x * 2 + s % 2

    def mate(self, s):
        return {"fsdp": self.index(self.hi, s, self.x), "tp": self.y}

    def peer(self, hi, x):
        return {"fsdp": self.index(hi, self.s, x), "tp": self.y}

    def barrier(self):
        sem = pltpu.get_barrier_semaphore()
        partners = [self.mate(s) for s in (self.sib, self.zn, self.diag)]
        partners += [{"fsdp": self.f, "tp": self.yn}, self.peer(self.hi, 1 - self.x)]
        partners += [self.peer(self.next_hi, self.x), self.peer(self.next_hi, 1 - self.x)]
        if self.cfg["NH"] > 2:
            partners += [self.peer(self.last_hi, self.x), self.peer(self.last_hi, 1 - self.x)]
        for partner in partners:
            pl.semaphore_signal(sem, inc=1, device_id=partner, device_id_type=pl.DeviceIdType.MESH)
        pl.semaphore_wait(sem, len(partners))

    def remote(self, src, dst, device):
        k = self.count
        self.count += 1
        copy = pltpu.make_async_remote_copy(
            src_ref=src,
            dst_ref=dst,
            send_sem=self.send_sems.at[k],
            recv_sem=self.recv_sems.at[k],
            device_id=device,
            device_id_type=pl.DeviceIdType.MESH,
        )
        copy.start()
        self.sends.append(copy)
        return copy

    def to_sib(self, src, dst):
        return self.remote(src, dst, self.mate(self.sib))

    def to_z(self, src, dst):
        return self.remote(src, dst, self.mate(self.zn))

    def to_y(self, src, dst):
        return self.remote(src, dst, {"fsdp": self.f, "tp": self.yn})

    def to_x(self, src, dst):
        return self.remote(src, dst, self.peer(self.hi, 1 - self.x))

    def to_half(self, src, dst):
        return self.remote(src, dst, self.peer(self.next_hi, self.x))

    def local(self, src, dst):
        k = self.local_count
        self.local_count += 1
        copy = pltpu.make_async_copy(src, dst, self.local_sems.at[k])
        copy.start()
        return copy


    def rows(self, hi, z, x):
        size = 2 * self.cfg["DB"]
        return pl.ds(pl.multiple_of(((hi * 2 + z) * 2 + x) * size, 16), size)

    def share(self, ref, s):
        db = self.cfg["DB"]
        return ref.at[pl.ds(pl.multiple_of(self.index(self.hi, s, self.x) * db, 16), db), :]

    def columns_out(self, shares, full):
        if self.cfg["whole"]:
            return self.local(shares, full).wait
        mine = self.share(full, self.s)
        copies = [self.remote(shares.at[s], mine, self.mate(s)) for s in (self.zn, self.diag, self.sib)]
        own = self.local(shares.at[self.s], mine)

        def wait():
            for c in copies:
                c.wait_recv()
            own.wait()

        return wait

    def columns_back(self, full, result):
        if self.cfg["whole"]:
            return self.local(full, result).wait
        copies = [
            self.remote(self.share(full, s), result.at[self.s], self.mate(s)) for s in (self.zn, self.diag, self.sib)
        ]
        own = self.local(self.share(full, self.s), result.at[self.s])

        def wait():
            for c in copies:
                c.wait_recv()
            own.wait()

        return wait

    def spread(self, full):
        if self.cfg["whole"]:
            return None
        parts = [full.at[self.rows(self.hi, z, self.x), :] for z in range(2)]
        far = [self.to_half(part, part) for part in parts]
        near = [self.to_x(part, part) for part in parts]
        self.gathered += far + near
        return {"full": full, "far": far, "near": near}

    def spread_on(self, g):
        if g is None:
            return
        for z, c in enumerate(g["far"]):
            c.wait_recv()
            part = g["full"].at[self.rows(self.next_hi, z, self.x), :]
            onward = self.to_x(part, part)
            g["near"].append(onward)
            self.gathered.append(onward)

    def spread_done(self, g):
        if g is not None:
            for c in g["near"]:
                c.wait_recv()

    def add_rows(self, grad, rows, parts):
        size, tile = 2 * self.cfg["DB"], 2 * self.cfg["DB"]
        tile = next(t for t in (112, 32, 16) if size % t == 0)
        for i in range(size // tile):
            place = pl.ds(pl.multiple_of(rows.start + i * tile, 16), tile)
            total = grad[place, :].astype(F32)
            for part in parts:
                total = total + part[i * tile : (i + 1) * tile, :].astype(F32)
            grad[place, :] = total.astype(BF)

    def collect(self, grad, slots):
        if self.cfg["whole"]:
            return None
        near = []
        for k, hi in enumerate((self.next_hi, self.hi)):
            for z in range(2):
                near.append(self.to_x(grad.at[self.rows(hi, z, 1 - self.x), :], slots.at[2 * k + z]))
        return {"grad": grad, "slots": slots, "near": near}

    def collect_on(self, g):
        if g is None:
            return
        g["far"] = []
        for z in range(2):
            g["near"][z].wait_recv()
            rows = self.rows(self.next_hi, z, self.x)
            self.add_rows(g["grad"], rows, [g["slots"].at[z]])
            g["far"].append(self.to_half(g["grad"].at[rows, :], g["slots"].at[4 + z]))

    def collect_done(self, g):
        if g is None:
            return
        for z in range(2):
            g["near"][2 + z].wait_recv()
            g["far"][z].wait_recv()
            rows = self.rows(self.hi, z, self.x)
            self.add_rows(g["grad"], rows, [g["slots"].at[2 + z], g["slots"].at[4 + z]])


    def rim_out(self, ends, slots):
        after = self.peer((self.hi + self.x) % self.cfg["NH"], 1 - self.x)
        return [self.to_x(ends[0], slots(self.x)), self.remote(ends[1], slots(1 - self.x), after)]

    def rim_home(self, slots, ends):
        before = self.peer((self.hi + self.cfg["NH"] - 1 + self.x) % self.cfg["NH"], 1 - self.x)
        return [self.to_x(slots(1 - self.x), ends[0]), self.remote(slots(self.x), ends[1], before)]


    def gather_start(self, buf):
        own = buf.at[self.s, self.y]
        return {"x": self.to_z(own, own), "y": self.to_y(own, own), "own": self.to_sib(own, own), "buf": buf}

    def gather_relay(self, g):
        buf, cut = g["buf"], self.cfg["cut"]
        g["x"].wait_recv()
        part = buf.at[self.zn, self.y, :, slice(0, cut)]
        g["d0"] = self.to_y(part, part)
        whole = buf.at[self.zn, self.y]
        g["fx"] = self.to_sib(whole, whole)
        g["y"].wait_recv()
        part = buf.at[self.s, self.yn, :, slice(cut, self.cfg["D"])]
        g["d1"] = self.to_z(part, part)
        whole = buf.at[self.s, self.yn]
        g["fy"] = self.to_sib(whole, whole)

    def gather_finish(self, g):
        buf, cut = g["buf"], self.cfg["cut"]
        g["d0"].wait_recv()
        part = buf.at[self.zn, self.yn, :, slice(0, cut)]
        f0 = self.to_sib(part, part)
        g["d1"].wait_recv()
        part = buf.at[self.zn, self.yn, :, slice(cut, self.cfg["D"])]
        f1 = self.to_sib(part, part)
        for c in (g["own"], g["fx"], g["fy"], f0, f1):
            c.wait_recv()
        g["copies"] = [g[n] for n in ("own", "x", "y", "d0", "d1", "fx", "fy")] + [f0, f1]

    def scatter_pair(self, st, partial):
        sc, rc = st["sc"], st["rc"]
        copies = []
        for k, pair in enumerate(((self.sib + 2) % SUB, self.sib)):
            sc[k] = partial(pair).astype(BF).reshape(sc.shape[1:])
            copies.append(self.to_sib(sc.at[k], rc.at[k]))
        return {"pair": copies, "st": st}

    def scatter_send(self, g, partial):
        st, cut, d = g["st"], self.cfg["cut"], self.cfg["D"]
        so, rc = st["so"], st["rc"]
        lo, hi = slice(0, cut), slice(cut, d)
        value = partial(self.zn)
        g["pair"][0].wait_recv()
        so[0] = (value + flat(rc[0].astype(F32))).astype(BF).reshape(so.shape[1:])
        g["d0"] = self.to_z(so.at[0, self.yn, :, lo], st["rd0"])
        g["d1"] = self.to_y(so.at[0, self.yn, :, hi], st["rd1"])
        g["x0"] = self.to_z(so.at[0, self.y, :, lo], st["rx"].at[:, lo])
        value = partial(self.s)
        g["pair"][1].wait_recv()
        so[1] = (value + flat(rc[1].astype(F32))).astype(BF).reshape(so.shape[1:])
        g["y1"] = self.to_y(so.at[1, self.yn, :, hi], st["ry"].at[:, hi])

    def scatter_relay(self, g):
        st, cut, d = g["st"], self.cfg["cut"], self.cfg["D"]
        so = st["so"]
        lo, hi = slice(0, cut), slice(cut, d)
        g["d1"].wait_recv()
        so[0, self.y, :, hi] = (so[0, self.y, :, hi].astype(F32) + st["rd1"][...].astype(F32)).astype(BF)
        g["x1"] = self.to_z(so.at[0, self.y, :, hi], st["rx"].at[:, hi])
        g["d0"].wait_recv()
        so[1, self.yn, :, lo] = (so[1, self.yn, :, lo].astype(F32) + st["rd0"][...].astype(F32)).astype(BF)
        g["y0"] = self.to_y(so.at[1, self.yn, :, lo], st["ry"].at[:, lo])

    def scatter_finish(self, g):
        st = g["st"]
        for name in ("x0", "x1", "y0", "y1"):
            g[name].wait_recv()
        total = st["so"][1, self.y].astype(F32) + st["rx"][...].astype(F32) + st["ry"][...].astype(F32)
        self.settle(g["pair"] + [g[n] for n in ("d0", "d1", "x0", "x1", "y0", "y1")])
        return total


    def place(self, s):
        return 1 + 2 * s + s // 2

    def project(self, w):
        def step(i, _):
            rows = flat(self.u1[i])
            out = dot(rows, w[...], NN).astype(BF)
            self.qkv[pl.ds(self.place(i), 2)] = out.reshape(2, 2 * WINDOW, out.shape[1])
            return 0

        lax.fori_loop(0, SUB, step, 0)

    def masks(self, s):
        at = 1 + s + s // 2
        before, own = self.starts[at - 1], self.starts[at]
        lane = lax.broadcasted_iota(jnp.int32, before.shape, 1)
        even = jnp.where(lane < WINDOW, pltpu.roll(before, WINDOW, 1), pltpu.roll(own, WINDOW, 1))
        shape = (WINDOW, 2 * WINDOW)
        i = lax.broadcasted_iota(jnp.int32, shape, 0)
        j = lax.broadcasted_iota(jnp.int32, shape, 1)
        square = (2 * WINDOW, 2 * WINDOW)
        later = lax.broadcasted_iota(jnp.int32, square, 0) > lax.broadcasted_iota(jnp.int32, square, 1)
        later = later.astype(F32).astype(BF)
        band = (j <= i + WINDOW) & (j > i)
        result = []
        for rows in (even, own):
            per_batch = []
            for batch in range(2):
                line = jnp.broadcast_to(rows[batch : batch + 1, :], shape)
                line = jnp.where(j <= i + WINDOW, line, 0.0).astype(BF)
                between = dot(line, later, NN)
                per_batch.append(band & (between < 0.5))
            result.append(per_batch)
        return result

    def tile(self, index, batch, part, head):
        cols = slice(part * 2 * HP + head * HP, part * 2 * HP + (head + 1) * HP)
        return self.qkv[index, batch * WINDOW : (batch + 1) * WINDOW, cols]

    def attend(self):
        def step(n, _):
            s = SUB - 1 - n
            allowed = self.masks(s)
            for half in range(2):
                p = self.place(s) + half
                for batch in range(2):
                    for head in range(2):
                        q = self.tile(p, batch, 0, head)
                        k = jnp.concatenate([self.tile(p - 1, batch, 1, head), self.tile(p, batch, 1, head)], axis=0)
                        v = jnp.concatenate([self.tile(p - 1, batch, 2, head), self.tile(p, batch, 2, head)], axis=0)
                        scores = dot(q, k, NT) * DH ** (-0.5)
                        scores = jnp.where(allowed[half][batch], scores, -1e30)
                        top = jnp.max(scores, axis=-1, keepdims=True)
                        weights = jnp.exp(scores - top)
                        probs = weights / jnp.sum(weights, axis=-1, keepdims=True)
                        self.probs[2 * s + half, 2 * batch + head] = probs
                        out = dot(probs.astype(BF), v, NN).astype(BF)
                        self.heads[s, half, batch * WINDOW : (batch + 1) * WINDOW, head * HP : (head + 1) * HP] = out
            return 0

        lax.fori_loop(0, SUB, step, 0)

    def attend_back(self, s):
        run = s // 2
        for half in range(2):
            p = self.place(s) + half
            for batch in range(2):
                rows = slice(batch * WINDOW, (batch + 1) * WINDOW)
                for head in range(2):
                    cols = slice(head * HP, (head + 1) * HP)
                    q = self.tile(p, batch, 0, head)
                    k = jnp.concatenate([self.tile(p - 1, batch, 1, head), self.tile(p, batch, 1, head)], axis=0)
                    v = jnp.concatenate([self.tile(p - 1, batch, 2, head), self.tile(p, batch, 2, head)], axis=0)
                    probs = self.probs[2 * s + half, 2 * batch + head]
                    d_out = self.d_heads[s, half, rows, cols]
                    d_probs = dot(d_out, v, NT)
                    inner = jnp.sum(probs * d_probs, axis=-1, keepdims=True)
                    d_scores = (probs * (d_probs - inner)).astype(BF)
                    d_q = dot(d_scores, k, NN) * DH ** (-0.5)
                    d_k = dot(d_scores, q, TN) * DH ** (-0.5)
                    d_v = dot(probs.astype(BF), d_out, TN)
                    self.qkv[p, rows, head * HP : (head + 1) * HP] = d_q.astype(BF)
                    for part, grad in ((1, d_k), (2, d_v)):
                        slot = slice((part - 1) * 2 * HP + head * HP, (part - 1) * 2 * HP + (head + 1) * HP)
                        place = slice(part * 2 * HP + head * HP, part * 2 * HP + (head + 1) * HP)
                        done = self.carry[run, rows, slot] + grad[:WINDOW]
                        self.qkv[p - 1, rows, place] = done.astype(BF)
                        self.carry[run, rows, slot] = grad[WINDOW:]

    def grad_into(self, target, left, right):
        width = 256

        def step(m, _):
            cols = pl.ds(pl.multiple_of(m * width, width), width)
            parts = right()
            each = SUB // len(parts)
            total = 0.0
            for k, part in enumerate(parts):
                total = total + dot(flat(left[k * each : (k + 1) * each, :, :, cols]), part, TN)
            target[cols, :] = total.astype(BF)
            return 0

        lax.fori_loop(0, self.cfg["D"] // width, step, 0)

    def feed_forward(self):
        ff = self.w_dn.shape[1]

        def step(i, _):
            rows = flat(self.u2[i])
            gate = dot(rows, self.w_ga[...], NN)
            upward = dot(rows, self.w_up[...], NN)
            d_hidden = dot(flat(self.g[i]), self.w_dn[...], NN)
            sig = jax.nn.sigmoid(gate)
            silu = gate * sig
            shape = (2, 2 * WINDOW, ff)
            self.hidden[i] = (silu * upward).astype(BF).reshape(shape)
            d_gate = d_hidden * upward * sig * (1.0 + gate * (1.0 - sig))
            self.d_ga[i] = d_gate.astype(BF).reshape(shape)
            self.d_up[i] = (d_hidden * silu).astype(BF).reshape(shape)
            return 0

        lax.fori_loop(0, SUB, step, 0)

    def run(self):
        cfg = self.cfg
        me = (self.s, self.y)
        norm = lambda v: lax.rsqrt(jnp.mean(v * v, axis=-1, keepdims=True) + EPSILON)
        whole = lambda ref: [flat(ref[...])]

        self.barrier()
        qkv_here = self.columns_out(self.sh_qkv, self.w_qkv)
        line = 1 + self.s + self.s // 2
        start_copies = [
            self.remote(self.starts_in, self.starts.at[line], self.mate(s)) for s in (self.sib, self.zn, self.diag)
        ]
        self.starts[line] = self.starts_in[...]

        x = self.x_in[...].astype(F32)
        self.u1[me] = (x * norm(x)).astype(BF)
        gather_one = self.gather_start(self.u1)
        out_here = self.columns_out(self.sh_out, self.w_out)
        qkv_here()
        go_qkv = self.spread(self.w_qkv)
        ga_here = self.columns_out(self.sh_ga, self.w_ga)
        for c in start_copies:
            c.wait_recv()
        rim_starts = self.rim_out([self.starts.at[2], self.starts.at[5]], lambda run: self.starts.at[3 * run])
        self.gather_relay(gather_one)
        out_here()
        go_out = self.spread(self.w_out)
        self.g[me] = self.g_in[...]
        self.gather_finish(gather_one)
        self.spread_on(go_qkv)
        up_here = self.columns_out(self.sh_up, self.w_up)
        gather_g = self.gather_start(self.g)
        dn_here = self.columns_out(self.sh_dn, self.w_dn)
        self.spread_done(go_qkv)

        self.project(self.w_qkv)
        rims = self.rim_out(
            [self.qkv.at[4, :, slice(2 * HP, 6 * HP)], self.qkv.at[9, :, slice(2 * HP, 6 * HP)]],
            lambda run: self.qkv.at[5 * run, :, slice(2 * HP, 6 * HP)],
        )
        self.spread_on(go_out)
        ga_here()
        go_ga = self.spread(self.w_ga)
        self.gather_relay(gather_g)
        for c in rim_starts + rims:
            c.wait_recv()
        self.attend()
        self.gather_finish(gather_g)
        self.spread_done(go_out)

        partial = lambda pair: dot(flat(self.heads[pair]), self.w_out[...], NT)
        stage = {n: getattr(self, n) for n in ("sc", "rc", "so", "rd0", "rd1", "rx", "ry")}
        scatter = self.scatter_pair(stage, partial)
        self.scatter_send(scatter, partial)
        self.scatter_relay(scatter)
        up_here()
        go_up = self.spread(self.w_up)
        self.spread_on(go_ga)
        self.resid[...] = self.x_in[...].astype(F32) + self.scatter_finish(scatter)
        resid = self.resid[...]
        self.u2[me] = (resid * norm(resid)).astype(BF)
        gather_two = self.gather_start(self.u2)
        dn_here()
        go_dn = self.spread(self.w_dn)
        self.gather_relay(gather_two)
        self.spread_on(go_up)
        self.gather_finish(gather_two)
        self.spread_on(go_dn)
        for go in (go_ga, go_up, go_dn):
            self.spread_done(go)

        self.feed_forward()
        partial = lambda pair: dot(flat(self.d_ga[pair]), self.w_ga[...], NT) + dot(
            flat(self.d_up[pair]), self.w_up[...], NT
        )
        scatter = self.scatter_pair(stage, partial)
        self.scatter_send(scatter, partial)
        self.grad_into(self.g_dn, self.g, lambda: whole(self.hidden))
        sum_dn = self.collect(self.g_dn, self.slots_dn)
        self.scatter_relay(scatter)
        self.settle(self.gathered)
        self.grad_into(self.w_ga, self.u2, lambda: whole(self.d_ga))
        sum_ga = self.collect(self.w_ga, self.slots_ga)
        self.grad_into(self.w_up, self.u2, lambda: whole(self.d_up))
        sum_up = self.collect(self.w_up, self.slots_up)
        d_unit = self.scatter_finish(scatter)
        resid = self.resid[...]
        scale = norm(resid)
        unit = resid * scale
        inner = jnp.mean(d_unit * unit, axis=-1, keepdims=True)
        self.d_resid[...] = self.g_in[...].astype(F32) + scale * (d_unit - unit * inner)
        self.d_r[me] = self.d_resid[...].astype(BF)
        self.settle(gather_g["copies"] + gather_two["copies"] + rims)
        gather_d = self.gather_start(self.d_r)
        self.collect_on(sum_dn)
        self.gather_relay(gather_d)
        self.gather_finish(gather_d)

        def heads_back(i, _):
            value = dot(flat(self.d_r[i]), self.w_out[...], NN).astype(BF)
            self.d_heads[i] = value.reshape(2, 2 * WINDOW, 2 * HP)
            return 0

        lax.fori_loop(0, SUB, heads_back, 0)

        view = {
            "sc": self.u2.at[0:2],
            "so": self.u2.at[2:4],
            "rc": self.g.at[0:2],
            "rd0": self.g.at[2, 0, :, slice(0, cfg["cut"])],
            "rd1": self.g.at[2, 0, :, slice(cfg["cut"], cfg["D"])],
            "rx": self.g.at[2, 1],
            "ry": self.g.at[3, 0],
        }
        partial = lambda pair: dot(flat(self.hidden[pair]), self.w_dn[...], NT)
        mlp = self.scatter_pair(view, partial)
        self.scatter_send(mlp, partial)
        self.collect_on(sum_ga)

        self.carry[...] = jnp.zeros_like(self.carry)

        def first(run, _):
            self.attend_back(2 * run)
            return 0

        def second(run, _):
            self.attend_back(2 * run + 1)
            return 0

        lax.fori_loop(0, 2, first, 0)
        rim_back = self.rim_home(
            lambda run: self.qkv.at[5 * run, :, slice(2 * HP, 6 * HP)], [self.rim.at[0], self.rim.at[1]]
        )
        self.scatter_relay(mlp)
        lax.fori_loop(0, 2, second, 0)
        self.collect_on(sum_up)
        for c in rim_back:
            c.wait_recv()
        for run in range(2):
            done = self.carry[run] + self.rim[run].astype(F32)
            self.qkv[5 * run + 4, :, 2 * HP :] = done.astype(BF)

        self.grad_into(self.g_qkv, self.u1, lambda: [flat(self.qkv[1:5]), flat(self.qkv[6:10])])
        sum_qkv = self.collect(self.g_qkv, self.slots_qkv)
        partial = lambda pair: dot(flat(self.qkv[pl.ds(self.place(pair), 2)]), self.w_qkv[...], NT)
        scatter = self.scatter_pair(stage, partial)
        self.scatter_send(scatter, partial)
        self.grad_into(self.w_out, self.d_r, lambda: whole(self.heads))
        sum_out = self.collect(self.w_out, self.slots_out)
        self.scatter_relay(scatter)
        self.out[...] = (self.resid[...] + self.scatter_finish(mlp)).astype(BF)
        self.collect_done(sum_dn)
        dn_back = self.columns_back(self.g_dn, self.o_dn)
        self.collect_done(sum_ga)
        ga_back = self.columns_back(self.w_ga, self.o_ga)
        d_unit = self.scatter_finish(scatter)
        x = self.x_in[...].astype(F32)
        scale = norm(x)
        unit = x * scale
        inner = jnp.mean(d_unit * unit, axis=-1, keepdims=True)
        self.in_grad[...] = self.d_resid[...] + scale * (d_unit - unit * inner)
        self.collect_on(sum_qkv)
        self.collect_on(sum_out)
        self.collect_done(sum_up)
        up_back = self.columns_back(self.w_up, self.o_up)
        self.collect_done(sum_qkv)
        qkv_back = self.columns_back(self.g_qkv, self.o_qkv)
        self.collect_done(sum_out)
        out_back = self.columns_back(self.w_out, self.o_out)
        for wait in (dn_back, ga_back, up_back, qkv_back, out_back):
            wait()
        self.settle()

    def settle(self, copies=None):
        for c in self.sends:
            if copies is None or any(c is other for other in copies):
                c.wait_send()
        if copies is None:
            self.sends = []
        else:
            self.sends = [c for c in self.sends if not any(c is other for other in copies)]


def fused(cfg, shares, starts, x, g):
    d, db = cfg["D"], cfg["DB"]
    rows = 2 * WINDOW
    cut = cfg["cut"]
    anywhere = pl.BlockSpec(memory_space=pl.ANY)
    vmem = pl.BlockSpec(memory_space=pltpu.VMEM)
    keys = ("qkv", "out", "ga", "up", "dn")
    width = {key: share.shape[-1] for key, share in zip(keys, shares, strict=True)}
    result = (d,) if cfg["whole"] else (SUB, db)
    outs = [("out", (rows, d), BF, vmem), ("in_grad", (rows, d), F32, vmem)]
    outs += [("o_" + key, result + (width[key],), BF, anywhere) for key in keys]
    ins = [("sh_" + key, anywhere) for key in keys] + [("starts_in", vmem), ("x_in", vmem), ("g_in", vmem)]
    plane = (SUB, 2, rows)
    scratch = [("w_" + key, (d, width[key]), BF) for key in keys]
    scratch += [("g_" + key, (d, width[key]), BF) for key in ("qkv", "dn")]
    slot = 16 if cfg["whole"] else 2 * db
    scratch += [("slots_" + key, (6, slot, width[key]), BF) for key in keys]
    scratch += [(name, plane + (d,), BF) for name in ("u1", "u2", "g", "d_r")]
    scratch += [(name, plane + (width["out"],), BF) for name in ("heads", "d_heads")]
    scratch += [(name, plane + (width["dn"],), BF) for name in ("hidden", "d_ga", "d_up")]
    scratch += [(name, (2, 2, rows, d), BF) for name in ("sc", "rc", "so")]
    scratch += [
        ("starts", (SUB + 2, 8, rows), F32),
        ("qkv", (2 * SUB + 2, rows, width["qkv"]), BF),
        ("probs", (2 * SUB, 4, WINDOW, 2 * WINDOW), F32),
        ("carry", (2, rows, 4 * HP), F32),
        ("rim", (2, rows, 4 * HP), BF),
        ("resid", (rows, d), F32),
        ("d_resid", (rows, d), F32),
        ("rd0", (rows, cut), BF),
        ("rd1", (rows, d - cut), BF),
        ("rx", (rows, d), BF),
        ("ry", (rows, d), BF),
    ]
    number = 190
    names = [n for n, _ in ins] + [n for n, *_ in outs] + [n for n, *_ in scratch]
    names += ["send_sems", "recv_sems", "local_sems"]

    def kernel(*refs):
        Kernel(cfg, dict(zip(names, refs, strict=True))).run()

    return pl.pallas_call(
        kernel,
        out_shape=[jax.ShapeDtypeStruct(shape, kind) for _, shape, kind, _ in outs],
        in_specs=[spec for _, spec in ins],
        out_specs=[spec for *_, spec in outs],
        scratch_shapes=[pltpu.VMEM(shape, kind) for _, shape, kind in scratch]
        + [
            pltpu.SemaphoreType.DMA((number,)),
            pltpu.SemaphoreType.DMA((number,)),
            pltpu.SemaphoreType.DMA((10,)),
        ],
        compiler_params=pltpu.CompilerParams(
            collective_id=0, has_side_effects=True, vmem_limit_bytes=63 * 2**20
        ),
    )(*shares, starts, x, g)


def padded(value, size):
    pads = [(0, 0)] * (value.ndim - 1) + [(0, size - value.shape[-1])]
    return jnp.pad(value, pads)


def body(size, tokens, doc_starts, w_qkv, w_out, w_gate_up, w_down, gains, cotangent):
    batches, rows, d = tokens.shape
    db = w_qkv.shape[1]
    ff = w_gate_up.shape[2] // SUB
    ffp = -(-ff // HP) * HP
    heads = w_qkv.shape[2] // (SUB * DH)
    gain = gains.astype(F32)
    whole = size != 16 or db % 16 != 0
    cfg = {"D": d, "NH": size // 8, "DB": db, "cut": d // 256 * 128, "whole": whole}

    sh_qkv = (w_qkv.astype(F32) * gain[0][None, :, None]).astype(BF).reshape(3, db, SUB, heads, DH)
    sh_qkv = padded(sh_qkv, HP).transpose(2, 1, 0, 3, 4).reshape(SUB, db, 3 * heads * HP)
    sh_out = w_out.T.reshape(db, SUB, heads, DH)
    sh_out = padded(sh_out, HP).transpose(1, 0, 2, 3).reshape(SUB, db, heads * HP)
    scaled = (w_gate_up.astype(F32) * gain[1][None, :, None]).astype(BF).reshape(2, db, SUB, ff)
    sh_ga, sh_up = [padded(scaled[k], ffp).transpose(1, 0, 2) for k in range(2)]
    sh_dn = padded(w_down.T.reshape(db, SUB, ff), ffp).transpose(1, 0, 2)
    shares = [sh_qkv, sh_out, sh_ga, sh_up, sh_dn]

    if whole:
        f = lax.axis_index("fsdp")
        s = (f // 4) % 2 * 2 + f % 2
        everyone = [lax.all_gather(v, "fsdp", axis=1, tiled=True) for v in shares]
        shares = [lax.dynamic_index_in_dim(v, s, 0, keepdims=False) for v in everyone]
    starts = jnp.pad(doc_starts.astype(F32), ((0, 8 - batches), (0, 0)))
    out, in_grad, *grads = fused(
        cfg, shares, starts, tokens.reshape(batches * rows, d), cotangent.reshape(batches * rows, d)
    )
    if whole:
        mine = (jnp.arange(SUB) == s)[:, None, None]
        grads = [
            lax.psum_scatter(jnp.where(mine, v[None], 0).astype(BF), "fsdp", scatter_dimension=1, tiled=True)
            for v in grads
        ]
    g_qkv, g_out, g_ga, g_up, g_dn = [v.astype(F32) for v in grads]
    g_qkv = g_qkv.reshape(SUB, db, 3, heads, HP)[..., :DH].transpose(2, 1, 0, 3, 4).reshape(w_qkv.shape)
    g_out = g_out.reshape(SUB, db, heads, HP)[..., :DH].transpose(0, 2, 3, 1).reshape(w_out.shape)
    g_gu = jnp.stack([v[..., :ff].transpose(1, 0, 2).reshape(w_gate_up.shape[1:]) for v in (g_ga, g_up)])
    g_dn = g_dn[..., :ff].transpose(0, 2, 1).reshape(w_down.shape)
    gain_sums = jnp.stack(
        [
            jnp.sum(g_qkv * w_qkv.astype(F32), axis=(0, 2)),
            jnp.sum(g_gu * w_gate_up.astype(F32), axis=(0, 2)),
        ]
    )
    gain_sums = gain_sums + lax.ppermute(gain_sums, "tp", [(0, 1), (1, 0)])
    return (
        out.reshape(tokens.shape),
        in_grad.reshape(tokens.shape),
        g_qkv * gain[0][None, :, None],
        g_out,
        g_gu * gain[1][None, :, None],
        g_dn,
        gain_sums,
    )


def solution(mesh):
    in_specs = (
        P(None, ("fsdp", "tp"), None),
        P(None, "fsdp"),
        P(None, "fsdp", "tp"),
        P("tp", "fsdp"),
        P(None, "fsdp", "tp"),
        P("tp", "fsdp"),
        P(None, "fsdp"),
        P(None, ("fsdp", "tp"), None),
    )
    out_specs = (
        P(None, ("fsdp", "tp"), None),
        P(None, ("fsdp", "tp"), None),
        P(None, "fsdp", "tp"),
        P("tp", "fsdp"),
        P(None, "fsdp", "tp"),
        P("tp", "fsdp"),
        P(None, "fsdp"),
    )
    return jax.shard_map(
        functools.partial(body, mesh.shape["fsdp"]), mesh=mesh, in_specs=in_specs, out_specs=out_specs, check_vma=False
    )
```

```python
import functools

import jax
import jax.numpy as jnp
from jax import lax
from jax.experimental import pallas as pl
from jax.experimental.pallas import tpu as pltpu
from jax.sharding import PartitionSpec as P

DH = 112
HP = 128
WINDOW = 64
EPSILON = 1e-06
SUB = 4
BF = jnp.bfloat16
F32 = jnp.float32
NN = (((1,), (0,)), ((), ()))
NT = (((1,), (1,)), ((), ()))
TN = (((0,), (0,)), ((), ()))


def dot(a, b, dims):
    return lax.dot_general(a, b, dims, preferred_element_type=F32)


def flat(value):
    return value.reshape(-1, value.shape[-1])


def eye(size):
    shape = (size, size)
    return lax.broadcasted_iota(jnp.int32, shape, 0) == lax.broadcasted_iota(jnp.int32, shape, 1)


def padded(value, size):
    extra = size - value.shape[-1]
    if not extra:
        return value
    return jnp.concatenate([value, jnp.zeros(value.shape[:-1] + (extra,), value.dtype)], axis=-1)


class Conditional:
    def __init__(self, copy, sent, received):
        self.copy, self.sent, self.received = copy, sent, received

    def wait_send(self):
        pl.when(self.sent)(self.copy.wait_send)

    def wait_recv(self):
        pl.when(self.received)(self.copy.wait_recv)


class Kernel:
    def __init__(self, cfg, refs):
        self.cfg = cfg
        self.__dict__.update(refs)
        self.f = lax.axis_index("fsdp")
        self.y = lax.axis_index("tp")
        core = self.f % 2
        self.x = (self.f // 2) % 2
        self.hi = self.f // 8
        self.z = (self.f // 4) % 2
        self.is_middle = self.hi + self.z == 1
        self.is_end = self.hi + self.z != 1
        self.s = (self.f // 4) % 2 * 2 + core
        self.sib = self.s + 1 - 2 * core
        self.zn = (self.s + 2) % SUB
        self.diag = (self.sib + 2) % SUB
        self.yn = 1 - self.y
        self.next_hi = (self.hi + 1) % cfg["NH"]
        self.last_hi = (self.hi + cfg["NH"] - 1) % cfg["NH"]
        self.count = 0
        self.local_count = 0
        self.sends = []
        self.gathered = []
        self.given = []
        middle = cfg["D"] // 256 * 128
        self.halves = (slice(0, middle), slice(middle, cfg["D"]))

    def index(self, hi, s, x):
        return hi * 8 + s // 2 * 4 + x * 2 + s % 2

    def mate(self, s):
        return {"fsdp": self.index(self.hi, s, self.x), "tp": self.y}

    def other(self, s):
        return {"fsdp": self.index(self.next_hi, s, self.x), "tp": self.y}

    def peer(self, hi, x):
        return {"fsdp": self.index(hi, self.s, x), "tp": self.y}

    def barrier(self):
        sem = pltpu.get_barrier_semaphore()
        partners = [self.mate(s) for s in (self.sib, self.zn, self.diag)]
        partners += [{"fsdp": self.f, "tp": self.yn}, self.peer(self.hi, 1 - self.x)]
        partners += [self.peer(self.next_hi, 1 - self.x)]
        if self.cfg["whole"]:
            partners += [self.peer(self.last_hi, 1 - self.x)]
        else:
            partners += [self.other(s) for s in (self.s, self.sib, self.zn, self.diag)]
        for partner in partners:
            pl.semaphore_signal(sem, inc=1, device_id=partner, device_id_type=pl.DeviceIdType.MESH)
        pl.semaphore_wait(sem, len(partners))

    def remote(self, src, dst, device, sent=None, received=None):
        k = self.count
        self.count += 1
        copy = pltpu.make_async_remote_copy(
            src_ref=src,
            dst_ref=dst,
            send_sem=self.send_sems.at[k],
            recv_sem=self.recv_sems.at[k],
            device_id=device,
            device_id_type=pl.DeviceIdType.MESH,
        )
        if sent is None:
            copy.start()
        else:
            pl.when(sent)(copy.start)
            copy = Conditional(copy, sent, received)
        self.sends.append(copy)
        return copy

    def to_sib(self, src, dst):
        return self.remote(src, dst, self.mate(self.sib))

    def to_z(self, src, dst):
        return self.remote(src, dst, self.mate(self.zn))

    def to_y(self, src, dst):
        return self.remote(src, dst, {"fsdp": self.f, "tp": self.yn})

    def to_x(self, src, dst):
        return self.remote(src, dst, self.peer(self.hi, 1 - self.x))

    def to_half(self, src, dst):
        return self.remote(src, dst, self.peer(self.next_hi, self.x))

    def local(self, src, dst):
        k = self.local_count
        self.local_count += 1
        copy = pltpu.make_async_copy(src, dst, self.local_sems.at[k])
        copy.start()
        return copy


    def rows(self, hi, z, x):
        size = 2 * self.cfg["DB"]
        return pl.ds(pl.multiple_of(((hi * 2 + z) * 2 + x) * size, 16), size)

    def share(self, ref, s):
        db = self.cfg["DB"]
        return ref.at[pl.ds(pl.multiple_of(self.index(self.hi, s, self.x) * db, 16), db), :]

    def columns_out(self, key):
        full = getattr(self, "w_" + key)
        if self.cfg["whole"]:
            return {"full": full, "own": self.local(getattr(self, "sh_" + key), full), "here": []}
        self.prepare(key)
        shares = functools.partial(self.prepared, key)
        mine = self.share(full, self.s)
        here = [self.remote(shares(s), mine, self.mate(s)) for s in (self.zn, self.diag, self.sib)]
        self.given += here
        return {"full": full, "shares": shares, "own": self.local(shares(self.s), mine), "here": here}

    def prepared(self, key, s):
        db = self.cfg["DB"]
        rows = pl.ds(pl.multiple_of(s % 2 * db, 16), db)
        return getattr(self, "slots_" + key).at[s // 2, rows, :]

    def gain_column(self, k):
        db = self.cfg["DB"]
        line = jnp.broadcast_to(self.gains[...].astype(F32)[k : k + 1, :], (db, db))
        return jnp.sum(jnp.where(eye(db), line, 0.0), axis=1, keepdims=True)

    def prepare(self, key):
        db, ff = self.cfg["DB"], self.cfg["FF"]
        slots = getattr(self, "slots_" + key)
        if key in ("qkv", "ga", "up"):
            gain = self.gain_column(0 if key == "qkv" else 1)
        for s in range(SUB):
            if key == "qkv":
                blocks = [(k, 2 * s + h) for k in range(3) for h in range(2)]
                parts = [self.raw_qkv[k, :, n * DH : (n + 1) * DH].astype(F32) * gain for k, n in blocks]
            elif key == "out":
                parts = [self.raw_out[:, n * DH : (n + 1) * DH].astype(F32) for n in (2 * s, 2 * s + 1)]
            elif key == "dn":
                parts = [self.raw_dn[:, s * ff : (s + 1) * ff].astype(F32)]
            else:
                parts = [self.raw_gu[int(key == "up"), :, s * ff : (s + 1) * ff].astype(F32) * gain]
            value = jnp.concatenate([padded(part, -(-part.shape[1] // HP) * HP) for part in parts], axis=1)
            slots[s // 2, s % 2 * db : (s % 2 + 1) * db, :] = value.astype(BF)

    def columns_far(self, g):
        if self.cfg["whole"]:
            return
        mine = self.share(g["full"], self.s)
        g["far"], g["middle"] = [], []
        for s in (self.s, self.sib):
            g["far"].append(self.remote(g["shares"](s), mine, self.other(s)))
        for s in (self.zn, self.diag):
            g["middle"].append(self.remote(g["shares"](s), mine, self.other(s), self.is_middle, self.is_middle))
        self.given += g["far"] + g["middle"]

    def spread(self, g):
        for c in g["here"]:
            c.wait_recv()
        g["own"].wait()
        if self.cfg["whole"]:
            return
        part = g["full"].at[self.rows(self.hi, 1 - self.z, self.x), :]
        g["passed"] = self.remote(part, part, self.other(self.s), self.is_middle, self.is_end)
        parts = [g["full"].at[self.rows(self.hi, z, self.x), :] for z in range(2)]
        g["near"] = [self.to_x(part, part) for part in parts]
        self.gathered += [g["passed"]] + g["near"]

    def onward(self, g, z):
        part = g["full"].at[self.rows(self.next_hi, z, self.x), :]
        copy = self.to_x(part, part)
        g["near"].append(copy)
        self.gathered.append(copy)

    def spread_same(self, g):
        if self.cfg["whole"]:
            return
        for c in g["far"]:
            c.wait_recv()
        self.onward(g, self.z)

    def spread_rest(self, g):
        if self.cfg["whole"]:
            return
        for c in g["middle"] + [g["passed"]]:
            c.wait_recv()
        self.onward(g, 1 - self.z)

    def spread_done(self, g):
        if not self.cfg["whole"]:
            for c in g["near"]:
                c.wait_recv()

    def columns_back(self, full, result):
        if self.cfg["whole"]:
            return self.local(full, result).wait
        copies = [
            self.remote(self.share(full, s), result.at[self.s], self.mate(s)) for s in (self.zn, self.diag, self.sib)
        ]
        own = self.local(self.share(full, self.s), result.at[self.s])

        def wait():
            for c in copies:
                c.wait_recv()
            own.wait()

        return wait

    def add_rows(self, grad, rows, parts):
        size, tile = 2 * self.cfg["DB"], 2 * self.cfg["DB"]
        tile = next(t for t in (112, 32, 16) if size % t == 0)
        for i in range(size // tile):
            place = pl.ds(pl.multiple_of(rows.start + i * tile, 16), tile)
            total = grad[place, :].astype(F32)
            for part in parts:
                total = total + part[i * tile : (i + 1) * tile, :].astype(F32)
            grad[place, :] = total.astype(BF)

    def collect(self, grad, slots):
        if self.cfg["whole"]:
            return None
        near = []
        for k, hi in enumerate((self.next_hi, self.hi)):
            for z in range(2):
                near.append(self.to_x(grad.at[self.rows(hi, z, 1 - self.x), :], slots.at[2 * k + z]))
        return {"grad": grad, "slots": slots, "near": near}

    def collect_on(self, g):
        if g is None:
            return
        g["far"] = []
        for z in range(2):
            g["near"][z].wait_recv()
            rows = self.rows(self.next_hi, z, self.x)
            self.add_rows(g["grad"], rows, [g["slots"].at[z]])
            g["far"].append(self.to_half(g["grad"].at[rows, :], g["slots"].at[4 + z]))

    def collect_done(self, g):
        if g is None:
            return
        for z in range(2):
            g["near"][2 + z].wait_recv()
            g["far"][z].wait_recv()
            rows = self.rows(self.hi, z, self.x)
            self.add_rows(g["grad"], rows, [g["slots"].at[2 + z], g["slots"].at[4 + z]])


    def rim_out(self, ends, slots):
        after = self.peer((self.hi + self.x) % self.cfg["NH"], 1 - self.x)
        return [self.to_x(ends[0], slots(self.x)), self.remote(ends[1], slots(1 - self.x), after)]

    def rim_home(self, slots, ends):
        before = self.peer((self.hi + self.cfg["NH"] - 1 + self.x) % self.cfg["NH"], 1 - self.x)
        return [self.to_x(slots(1 - self.x), ends[0]), self.remote(slots(self.x), ends[1], before)]


    def gather_start(self, buf):
        own = buf.at[self.s, self.y]
        return {"z": self.to_z(own, own), "y": self.to_y(own, own), "own": self.to_sib(own, own), "buf": buf}

    def gather_relay(self, g):
        buf = g["buf"]
        g["z"].wait_recv()
        part = buf.at[self.zn, self.y]
        g["d"] = self.to_y(part, part)
        g["fz"] = self.to_sib(part, part)
        g["y"].wait_recv()
        part = buf.at[self.s, self.yn]
        g["fy"] = self.to_sib(part, part)

    def gather_finish(self, g):
        g["d"].wait_recv()
        part = g["buf"].at[self.zn, self.yn]
        g["fd"] = self.to_sib(part, part)
        for name in ("own", "fz", "fy", "fd"):
            g[name].wait_recv()
        g["copies"] = [g[n] for n in ("own", "z", "y", "d", "fz", "fy", "fd")]

    def scatter_pair(self, st, partial):
        sc, rc = st["sc"], st["rc"]
        copies = []
        for k, pair in enumerate((self.diag, self.sib)):
            sc[k] = partial(pair).astype(BF).reshape(sc.shape[1:])
            copies.append(self.to_sib(sc.at[k], rc.at[k]))
        return {"pair": copies, "st": st}

    def scatter_send(self, g, partial):
        st = g["st"]
        so, rc = st["so"], st["rc"]
        value = partial(self.zn)
        g["pair"][0].wait_recv()
        so[0] = (value + flat(rc[0].astype(F32))).astype(BF).reshape(so.shape[1:])
        g["d"] = [self.to_y(so.at[0, self.yn, :, h], st["rd"].at[:, h]) for h in self.halves]
        value = partial(self.s)
        g["pair"][1].wait_recv()
        so[1] = (value + flat(rc[1].astype(F32))).astype(BF).reshape(so.shape[1:])
        g["y"] = self.to_y(so.at[1, self.yn], st["ry"])

    def scatter_relay(self, g):
        st = g["st"]
        so = st["so"]
        g["z"] = []
        for c, h in zip(g["d"], self.halves, strict=True):
            c.wait_recv()
            so[0, self.y, :, h] = (so[0, self.y, :, h].astype(F32) + st["rd"][:, h].astype(F32)).astype(BF)
            g["z"].append(self.to_z(so.at[0, self.y, :, h], st["rz"].at[:, h]))

    def scatter_finish(self, g):
        st = g["st"]
        for c in g["z"] + [g["y"]]:
            c.wait_recv()
        total = st["so"][1, self.y].astype(F32) + st["rz"][...].astype(F32) + st["ry"][...].astype(F32)
        self.settle(g["pair"] + g["d"] + g["z"] + [g["y"]])
        return total


    def place(self, s):
        return 1 + 2 * s + s // 2

    def project(self, w):
        def step(i, _):
            rows = flat(self.u1[i])
            out = dot(rows, w[...], NN).astype(BF)
            self.qkv[pl.ds(self.place(i), 2)] = out.reshape(2, 2 * WINDOW, out.shape[1])
            return 0

        lax.fori_loop(0, SUB, step, 0)

    def masks(self, s):
        at = 1 + s + s // 2
        before, own = self.starts[at - 1], self.starts[at]
        lane = lax.broadcasted_iota(jnp.int32, before.shape, 1)
        even = jnp.where(lane < WINDOW, pltpu.roll(before, WINDOW, 1), pltpu.roll(own, WINDOW, 1))
        shape = (WINDOW, 2 * WINDOW)
        i = lax.broadcasted_iota(jnp.int32, shape, 0)
        j = lax.broadcasted_iota(jnp.int32, shape, 1)
        square = (2 * WINDOW, 2 * WINDOW)
        later = lax.broadcasted_iota(jnp.int32, square, 0) > lax.broadcasted_iota(jnp.int32, square, 1)
        later = later.astype(F32).astype(BF)
        band = (j <= i + WINDOW) & (j > i)
        result = []
        for rows in (even, own):
            per_batch = []
            for batch in range(2):
                line = jnp.broadcast_to(rows[batch : batch + 1, :], shape)
                line = jnp.where(j <= i + WINDOW, line, 0.0).astype(BF)
                between = dot(line, later, NN)
                per_batch.append(band & (between < 0.5))
            result.append(per_batch)
        return result

    def tile(self, index, batch, part, head):
        cols = slice(part * 2 * HP + head * HP, part * 2 * HP + (head + 1) * HP)
        return self.qkv[index, batch * WINDOW : (batch + 1) * WINDOW, cols]

    def attend(self):
        def step(n, _):
            s = SUB - 1 - n
            allowed = self.masks(s)
            for half in range(2):
                p = self.place(s) + half
                for batch in range(2):
                    for head in range(2):
                        q = self.tile(p, batch, 0, head)
                        k = jnp.concatenate([self.tile(p - 1, batch, 1, head), self.tile(p, batch, 1, head)], axis=0)
                        v = jnp.concatenate([self.tile(p - 1, batch, 2, head), self.tile(p, batch, 2, head)], axis=0)
                        scores = dot(q, k, NT) * DH ** (-0.5)
                        scores = jnp.where(allowed[half][batch], scores, -1e30)
                        top = jnp.max(scores, axis=-1, keepdims=True)
                        weights = jnp.exp(scores - top)
                        probs = weights / jnp.sum(weights, axis=-1, keepdims=True)
                        self.probs[2 * s + half, 2 * batch + head] = probs
                        out = dot(probs.astype(BF), v, NN).astype(BF)
                        self.heads[s, half, batch * WINDOW : (batch + 1) * WINDOW, head * HP : (head + 1) * HP] = out
            return 0

        lax.fori_loop(0, SUB, step, 0)

    def attend_back(self, s):
        run = s // 2
        for half in range(2):
            p = self.place(s) + half
            for batch in range(2):
                rows = slice(batch * WINDOW, (batch + 1) * WINDOW)
                for head in range(2):
                    cols = slice(head * HP, (head + 1) * HP)
                    q = self.tile(p, batch, 0, head)
                    k = jnp.concatenate([self.tile(p - 1, batch, 1, head), self.tile(p, batch, 1, head)], axis=0)
                    v = jnp.concatenate([self.tile(p - 1, batch, 2, head), self.tile(p, batch, 2, head)], axis=0)
                    probs = self.probs[2 * s + half, 2 * batch + head]
                    d_out = self.d_heads[s, half, rows, cols]
                    d_probs = dot(d_out, v, NT)
                    inner = jnp.sum(probs * d_probs, axis=-1, keepdims=True)
                    d_scores = (probs * (d_probs - inner)).astype(BF)
                    d_q = dot(d_scores, k, NN) * DH ** (-0.5)
                    d_k = dot(d_scores, q, TN) * DH ** (-0.5)
                    d_v = dot(probs.astype(BF), d_out, TN)
                    self.qkv[p, rows, head * HP : (head + 1) * HP] = d_q.astype(BF)
                    for part, grad in ((1, d_k), (2, d_v)):
                        slot = slice((part - 1) * 2 * HP + head * HP, (part - 1) * 2 * HP + (head + 1) * HP)
                        place = slice(part * 2 * HP + head * HP, part * 2 * HP + (head + 1) * HP)
                        done = self.carry[run, rows, slot] + grad[:WINDOW]
                        self.qkv[p - 1, rows, place] = done.astype(BF)
                        self.carry[run, rows, slot] = grad[WINDOW:]

    def grad_into(self, target, left, right):
        width = 256

        def step(m, _):
            cols = pl.ds(pl.multiple_of(m * width, width), width)
            parts = right()
            each = SUB // len(parts)
            total = 0.0
            for k, part in enumerate(parts):
                total = total + dot(flat(left[k * each : (k + 1) * each, :, :, cols]), part, TN)
            target[cols, :] = total.astype(BF)
            return 0

        lax.fori_loop(0, self.cfg["D"] // width, step, 0)

    def feed_forward(self):
        ff = self.w_dn.shape[1]

        def step(i, _):
            rows = flat(self.u2[i])
            gate = dot(rows, self.w_ga[...], NN)
            upward = dot(rows, self.w_up[...], NN)
            d_hidden = dot(flat(self.g[i]), self.w_dn[...], NN)
            sig = jax.nn.sigmoid(gate)
            silu = gate * sig
            shape = (2, 2 * WINDOW, ff)
            self.hidden[i] = (silu * upward).astype(BF).reshape(shape)
            d_gate = d_hidden * upward * sig * (1.0 + gate * (1.0 - sig))
            self.d_ga[i] = d_gate.astype(BF).reshape(shape)
            self.d_up[i] = (d_hidden * silu).astype(BF).reshape(shape)
            return 0

        lax.fori_loop(0, SUB, step, 0)

    def run(self):
        cfg = self.cfg
        me = (self.s, self.y)
        norm = lambda v: lax.rsqrt(jnp.mean(v * v, axis=-1, keepdims=True) + EPSILON)
        whole = lambda ref: [flat(ref[...])]

        self.barrier()
        line = 1 + self.s + self.s // 2
        own_starts = self.doc_starts[...].astype(F32)
        fill = jnp.zeros((self.starts.shape[1] - own_starts.shape[0], own_starts.shape[1]), F32)
        self.starts[line] = jnp.concatenate([own_starts, fill], axis=0)
        own_line = self.starts.at[line]
        start_copies = [self.remote(own_line, own_line, self.mate(s)) for s in (self.sib, self.zn, self.diag)]
        qkv = self.columns_out("qkv")
        x = self.x_in[...].astype(F32)
        self.u1[me] = (x * norm(x)).astype(BF)
        gather_one = self.gather_start(self.u1)
        self.columns_far(qkv)
        out = self.columns_out("out")
        self.columns_far(out)
        self.spread(qkv)
        for c in start_copies:
            c.wait_recv()
        rim_starts = self.rim_out([self.starts.at[2], self.starts.at[5]], lambda run: self.starts.at[3 * run])
        self.gather_relay(gather_one)
        self.spread(out)
        ga = self.columns_out("ga")
        self.g[me] = self.g_in[...]
        self.spread_same(qkv)
        self.gather_finish(gather_one)
        self.spread_rest(qkv)
        self.spread_done(qkv)

        self.project(self.w_qkv)
        rims = self.rim_out(
            [self.qkv.at[4, :, slice(2 * HP, 6 * HP)], self.qkv.at[9, :, slice(2 * HP, 6 * HP)]],
            lambda run: self.qkv.at[5 * run, :, slice(2 * HP, 6 * HP)],
        )
        self.columns_far(ga)
        self.spread(ga)
        up = self.columns_out("up")
        self.columns_far(up)
        self.spread_same(out)
        self.spread_rest(out)
        for c in rim_starts + rims:
            c.wait_recv()
        self.attend()
        self.spread(up)
        dn = self.columns_out("dn")
        self.spread_done(out)

        partial = lambda pair: dot(flat(self.heads[pair]), self.w_out[...], NT)
        stage = {n: getattr(self, n) for n in ("sc", "rc", "so", "rd", "rz", "ry")}
        scatter = self.scatter_pair(stage, partial)
        self.scatter_send(scatter, partial)
        self.spread_same(ga)
        self.scatter_relay(scatter)
        gather_g = self.gather_start(self.g)
        self.columns_far(dn)
        self.spread(dn)
        self.spread_rest(ga)
        self.resid[...] = self.x_in[...].astype(F32) + self.scatter_finish(scatter)
        resid = self.resid[...]
        self.u2[me] = (resid * norm(resid)).astype(BF)
        gather_two = self.gather_start(self.u2)
        self.gather_relay(gather_g)
        self.spread_same(up)
        self.spread_rest(up)
        self.gather_relay(gather_two)
        self.gather_finish(gather_g)
        self.spread_same(dn)
        self.gather_finish(gather_two)
        self.settle(self.given)
        self.spread_rest(dn)
        for g in (ga, up, dn):
            self.spread_done(g)

        self.feed_forward()
        self.grad_into(self.g_dn, self.g, lambda: whole(self.hidden))
        sum_dn = self.collect(self.g_dn, self.slots_dn)
        partial = lambda pair: dot(flat(self.d_ga[pair]), self.w_ga[...], NT) + dot(
            flat(self.d_up[pair]), self.w_up[...], NT
        )
        scatter = self.scatter_pair(stage, partial)
        self.scatter_send(scatter, partial)
        self.settle(self.gathered)
        self.grad_into(self.w_ga, self.u2, lambda: whole(self.d_ga))
        sum_ga = self.collect(self.w_ga, self.slots_ga)
        self.scatter_relay(scatter)
        self.collect_on(sum_dn)
        self.grad_into(self.w_up, self.u2, lambda: whole(self.d_up))
        sum_up = self.collect(self.w_up, self.slots_up)
        d_unit = self.scatter_finish(scatter)
        resid = self.resid[...]
        scale = norm(resid)
        unit = resid * scale
        inner = jnp.mean(d_unit * unit, axis=-1, keepdims=True)
        self.in_grad[...] = self.g_in[...].astype(F32) + scale * (d_unit - unit * inner)
        self.d_r[me] = self.in_grad[...].astype(BF)
        self.settle(gather_g["copies"] + gather_two["copies"] + rims)
        gather_d = self.gather_start(self.d_r)
        self.gather_relay(gather_d)
        self.collect_on(sum_ga)
        self.gather_finish(gather_d)

        def heads_back(i, _):
            value = dot(flat(self.d_r[i]), self.w_out[...], NN).astype(BF)
            self.d_heads[i] = value.reshape(2, 2 * WINDOW, 2 * HP)
            return 0

        lax.fori_loop(0, SUB, heads_back, 0)

        self.carry[...] = jnp.zeros_like(self.carry)

        def first(run, _):
            self.attend_back(2 * run)
            return 0

        def second(run, _):
            self.attend_back(2 * run + 1)
            return 0

        lax.fori_loop(0, 2, first, 0)
        rim_back = self.rim_home(
            lambda run: self.qkv.at[5 * run, :, slice(2 * HP, 6 * HP)], [self.rim.at[0], self.rim.at[1]]
        )
        self.grad_into(self.w_out, self.d_r, lambda: whole(self.heads))
        sum_out = self.collect(self.w_out, self.slots_out)
        self.collect_done(sum_dn)
        backs = [self.columns_back(self.g_dn, self.o_dn)]
        self.collect_on(sum_up)
        lax.fori_loop(0, 2, second, 0)
        of_q, of_kv = slice(0, 2 * HP), slice(2 * HP, 6 * HP)
        g_q, g_kv = self.g_qkv.at[:, of_q], self.g_qkv.at[:, of_kv]
        self.grad_into(g_q, self.u1, lambda: [flat(self.qkv[1:5, :, of_q]), flat(self.qkv[6:10, :, of_q])])
        sum_q = self.collect(g_q, self.slots_qkv.at[:, :, of_q])
        for c in rim_back:
            c.wait_recv()
        for run in range(2):
            done = self.carry[run] + self.rim[run].astype(F32)
            self.qkv[5 * run + 4, :, 2 * HP :] = done.astype(BF)

        self.grad_into(g_kv, self.u1, lambda: [flat(self.qkv[1:5, :, of_kv]), flat(self.qkv[6:10, :, of_kv])])
        sum_kv = self.collect(g_kv, self.slots_qkv.at[:, :, of_kv])
        self.collect_done(sum_ga)
        backs.append(self.columns_back(self.w_ga, self.o_ga))
        partial = lambda pair: dot(flat(self.qkv[pl.ds(self.place(pair), 2)]), self.w_qkv[...], NT)
        scatter = self.scatter_pair(stage, partial)
        self.scatter_send(scatter, partial)
        self.collect_on(sum_out)
        self.scatter_relay(scatter)
        self.collect_on(sum_q)

        view = {
            "sc": self.u2.at[0:2],
            "so": self.u2.at[2:4],
            "rc": self.g.at[0:2],
            "rd": self.g.at[2, 0],
            "rz": self.g.at[2, 1],
            "ry": self.g.at[3, 0],
        }
        partial = lambda pair: dot(flat(self.hidden[pair]), self.w_dn[...], NT)
        mlp = self.scatter_pair(view, partial)
        self.scatter_send(mlp, partial)
        self.collect_done(sum_up)
        backs.append(self.columns_back(self.w_up, self.o_up))
        self.collect_on(sum_kv)
        self.collect_done(sum_out)
        backs.append(self.columns_back(self.w_out, self.o_out))
        self.scatter_relay(mlp)
        d_unit = self.scatter_finish(scatter)
        x = self.x_in[...].astype(F32)
        scale = norm(x)
        unit = x * scale
        inner = jnp.mean(d_unit * unit, axis=-1, keepdims=True)
        self.in_grad[...] += scale * (d_unit - unit * inner)
        self.collect_done(sum_q)
        back_to = lambda span: self.o_qkv.at[:, span] if cfg["whole"] else self.o_qkv.at[:, :, span]
        backs.append(self.columns_back(g_q, back_to(of_q)))
        self.out[...] = (self.resid[...] + self.scatter_finish(mlp)).astype(BF)
        self.collect_done(sum_kv)
        backs.append(self.columns_back(g_kv, back_to(of_kv)))
        for wait in backs:
            wait()
        self.settle()

    def settle(self, copies=None):
        for c in self.sends:
            if copies is None or any(c is other for other in copies):
                c.wait_send()
        if copies is None:
            self.sends = []
        else:
            self.sends = [c for c in self.sends if not any(c is other for other in copies)]


def fused(cfg, width, weights, starts, x, g):
    d, db = cfg["D"], cfg["DB"]
    rows = 2 * WINDOW
    anywhere = pl.BlockSpec(memory_space=pl.ANY)
    vmem = pl.BlockSpec(memory_space=pltpu.VMEM)
    keys = ("qkv", "out", "ga", "up", "dn")
    result = (d,) if cfg["whole"] else (SUB, db)
    outs = [("out", (rows, d), BF, vmem), ("in_grad", (rows, d), F32, vmem)]
    outs += [("o_" + key, result + (width[key],), BF, anywhere) for key in keys]
    if cfg["whole"]:
        ins = [("sh_" + key, anywhere) for key in keys]
    else:
        ins = [(name, vmem) for name in ("raw_qkv", "raw_out", "raw_gu", "raw_dn", "gains")]
    ins += [(name, vmem) for name in ("doc_starts", "x_in", "g_in")]
    plane = (SUB, 2, rows)
    scratch = [("w_" + key, (d, width[key]), BF) for key in keys]
    scratch += [("g_" + key, (d, width[key]), BF) for key in ("qkv", "dn")]
    slot = 16 if cfg["whole"] else 2 * db
    scratch += [("slots_" + key, (6, slot, width[key]), BF) for key in keys]
    scratch += [(name, plane + (d,), BF) for name in ("u1", "u2", "g", "d_r")]
    scratch += [(name, plane + (width["out"],), BF) for name in ("heads", "d_heads")]
    scratch += [(name, plane + (width["dn"],), BF) for name in ("hidden", "d_ga", "d_up")]
    scratch += [(name, (2, 2, rows, d), BF) for name in ("sc", "rc", "so")]
    scratch += [
        ("starts", (SUB + 2, 8, rows), F32),
        ("qkv", (2 * SUB + 2, rows, width["qkv"]), BF),
        ("probs", (2 * SUB, 4, WINDOW, 2 * WINDOW), F32),
        ("carry", (2, rows, 4 * HP), F32),
        ("rim", (2, rows, 4 * HP), BF),
        ("resid", (rows, d), F32),
        ("rd", (rows, d), BF),
        ("rz", (rows, d), BF),
        ("ry", (rows, d), BF),
    ]
    number = 200
    names = [n for n, _ in ins] + [n for n, *_ in outs] + [n for n, *_ in scratch]
    names += ["send_sems", "recv_sems", "local_sems"]

    def kernel(*refs):
        Kernel(cfg, dict(zip(names, refs, strict=True))).run()

    return pl.pallas_call(
        kernel,
        out_shape=[jax.ShapeDtypeStruct(shape, kind) for _, shape, kind, _ in outs],
        in_specs=[spec for _, spec in ins],
        out_specs=[spec for *_, spec in outs],
        scratch_shapes=[pltpu.VMEM(shape, kind) for _, shape, kind in scratch]
        + [
            pltpu.SemaphoreType.DMA((number,)),
            pltpu.SemaphoreType.DMA((number,)),
            pltpu.SemaphoreType.DMA((11,)),
        ],
        compiler_params=pltpu.CompilerParams(
            collective_id=0, has_side_effects=True, vmem_limit_bytes=63 * 2**20
        ),
    )(*weights, starts, x, g)


def assemble(ff, o_qkv, o_out, o_ga, o_up, o_dn, w_qkv, w_gu, gains, g_qkv, g_out, g_gu, g_dn, g_gain):
    db = w_qkv.shape[1]
    lines = gains[...].astype(F32)
    same = eye(db)

    def column(k):
        return jnp.sum(jnp.where(same, jnp.broadcast_to(lines[k : k + 1, :], (db, db)), 0.0), axis=1, keepdims=True)

    sums = []
    gain = column(0)
    total = jnp.zeros((db, 1), F32)
    for k in range(3):
        parts = []
        for s in range(SUB):
            for h in range(2):
                start = (2 * k + h) * HP
                parts.append(o_qkv[s, :, start : start + DH].astype(F32))
        value = jnp.concatenate(parts, axis=1)
        total = total + jnp.sum(value * w_qkv[k].astype(F32), axis=1, keepdims=True)
        g_qkv[k] = value * gain
    sums.append(total)
    gain = column(1)
    total = jnp.zeros((db, 1), F32)
    for k, ref in enumerate((o_ga, o_up)):
        value = jnp.concatenate([ref[s, :, :ff].astype(F32) for s in range(SUB)], axis=1)
        total = total + jnp.sum(value * w_gu[k].astype(F32), axis=1, keepdims=True)
        g_gu[k] = value * gain
    sums.append(total)
    for k, total in enumerate(sums):
        g_gain[k : k + 1, :] = jnp.sum(jnp.where(same, jnp.broadcast_to(total, (db, db)), 0.0), axis=0, keepdims=True)
    parts = [o_out[s, :, h * HP : h * HP + DH].astype(F32) for s in range(SUB) for h in range(2)]
    g_out[...] = jnp.concatenate(parts, axis=1)
    g_dn[...] = jnp.concatenate([o_dn[s, :, :ff].astype(F32) for s in range(SUB)], axis=1)


def body(size, tokens, doc_starts, w_qkv, w_out, w_gate_up, w_down, gains, cotangent):
    batches, rows, d = tokens.shape
    db = w_qkv.shape[1]
    ff = w_gate_up.shape[2] // SUB
    ffp = -(-ff // HP) * HP
    heads = w_qkv.shape[2] // (SUB * DH)
    whole = size != 16 or db % 16 != 0
    cfg = {"D": d, "NH": size // 8, "DB": db, "FF": ff, "whole": whole}
    width = {"qkv": 3 * heads * HP, "out": heads * HP, "ga": ffp, "up": ffp, "dn": ffp}
    acts = [doc_starts, tokens.reshape(batches * rows, d), cotangent.reshape(batches * rows, d)]

    def results(out, in_grad, g_qkv, g_out, g_gu, g_dn, gain_sums):
        gain_sums = gain_sums + lax.ppermute(gain_sums, "tp", [(0, 1), (1, 0)])
        return (out.reshape(tokens.shape), in_grad.reshape(tokens.shape), g_qkv, g_out, g_gu, g_dn, gain_sums)

    if not whole:
        out, in_grad, *grads = fused(cfg, width, [w_qkv, w_out.T, w_gate_up, w_down.T, gains], *acts)
        vmem = pl.BlockSpec(memory_space=pltpu.VMEM)
        grads = pl.pallas_call(
            functools.partial(assemble, ff),
            out_shape=[jax.ShapeDtypeStruct(v.shape, F32) for v in (w_qkv, w_out.T, w_gate_up, w_down.T, gains)],
            in_specs=[vmem] * 8,
            out_specs=[vmem] * 5,
            compiler_params=pltpu.CompilerParams(vmem_limit_bytes=40 * 2**20),
        )(*grads, w_qkv, w_gate_up, gains)
        g_qkv, g_out, g_gu, g_dn, gain_sums = grads
        return results(out, in_grad, g_qkv, g_out.T, g_gu, g_dn.T, gain_sums)

    gain = gains.astype(F32)
    sh_qkv = (w_qkv.astype(F32) * gain[0][None, :, None]).astype(BF).reshape(3, db, SUB, heads, DH)
    sh_qkv = padded(sh_qkv, HP).transpose(2, 1, 0, 3, 4).reshape(SUB, db, 3 * heads * HP)
    sh_out = w_out.T.reshape(db, SUB, heads, DH)
    sh_out = padded(sh_out, HP).transpose(1, 0, 2, 3).reshape(SUB, db, heads * HP)
    scaled = (w_gate_up.astype(F32) * gain[1][None, :, None]).astype(BF).reshape(2, db, SUB, ff)
    sh_ga, sh_up = [padded(scaled[k], ffp).transpose(1, 0, 2) for k in range(2)]
    sh_dn = padded(w_down.T.reshape(db, SUB, ff), ffp).transpose(1, 0, 2)
    f = lax.axis_index("fsdp")
    s = (f // 4) % 2 * 2 + f % 2
    everyone = [lax.all_gather(v, "fsdp", axis=1, tiled=True) for v in (sh_qkv, sh_out, sh_ga, sh_up, sh_dn)]
    shares = [lax.dynamic_index_in_dim(v, s, 0, keepdims=False) for v in everyone]
    out, in_grad, *grads = fused(cfg, width, shares, *acts)
    mine = (jnp.arange(SUB) == s)[:, None, None]
    g_qkv, g_out, g_ga, g_up, g_dn = [
        lax.psum_scatter(jnp.where(mine, v[None], 0).astype(BF), "fsdp", scatter_dimension=1, tiled=True).astype(F32)
        for v in grads
    ]
    g_qkv = g_qkv.reshape(SUB, db, 3, heads, HP)[..., :DH].transpose(2, 1, 0, 3, 4).reshape(w_qkv.shape)
    g_out = g_out.reshape(SUB, db, heads, HP)[..., :DH].transpose(0, 2, 3, 1).reshape(w_out.shape)
    g_gu = jnp.stack([v[..., :ff].transpose(1, 0, 2).reshape(w_gate_up.shape[1:]) for v in (g_ga, g_up)])
    g_dn = g_dn[..., :ff].transpose(0, 2, 1).reshape(w_down.shape)
    gain_sums = jnp.stack(
        [
            jnp.sum(g_qkv * w_qkv.astype(F32), axis=(0, 2)),
            jnp.sum(g_gu * w_gate_up.astype(F32), axis=(0, 2)),
        ]
    )
    g_qkv, g_gu = g_qkv * gain[0][None, :, None], g_gu * gain[1][None, :, None]
    return results(out, in_grad, g_qkv, g_out, g_gu, g_dn, gain_sums)


def solution(mesh):
    in_specs = (
        P(None, ("fsdp", "tp"), None),
        P(None, "fsdp"),
        P(None, "fsdp", "tp"),
        P("tp", "fsdp"),
        P(None, "fsdp", "tp"),
        P("tp", "fsdp"),
        P(None, "fsdp"),
        P(None, ("fsdp", "tp"), None),
    )
    out_specs = (
        P(None, ("fsdp", "tp"), None),
        P(None, ("fsdp", "tp"), None),
        P(None, "fsdp", "tp"),
        P("tp", "fsdp"),
        P(None, "fsdp", "tp"),
        P("tp", "fsdp"),
        P(None, "fsdp"),
    )
    return jax.shard_map(
        functools.partial(body, mesh.shape["fsdp"]), mesh=mesh, in_specs=in_specs, out_specs=out_specs, check_vma=False
    )
```

```python
import functools

import jax
import jax.numpy as jnp
from jax import lax
from jax.experimental import pallas as pl
from jax.experimental.pallas import tpu as pltpu
from jax.sharding import PartitionSpec as P

DH = 112
HP = 128
WINDOW = 64
EPSILON = 1e-06
SUB = 4
BF = jnp.bfloat16
F32 = jnp.float32
NN = (((1,), (0,)), ((), ()))
NT = (((1,), (1,)), ((), ()))
TN = (((0,), (0,)), ((), ()))


def dot(a, b, dims):
    return lax.dot_general(a, b, dims, preferred_element_type=F32)


def flat(value):
    return value.reshape(-1, value.shape[-1])


def eye(size):
    shape = (size, size)
    return lax.broadcasted_iota(jnp.int32, shape, 0) == lax.broadcasted_iota(jnp.int32, shape, 1)


def padded(value, size):
    extra = size - value.shape[-1]
    if not extra:
        return value
    return jnp.concatenate([value, jnp.zeros(value.shape[:-1] + (extra,), value.dtype)], axis=-1)


class Conditional:
    def __init__(self, copy, sent, received):
        self.copy, self.sent, self.received = copy, sent, received

    def wait_send(self):
        pl.when(self.sent)(self.copy.wait_send)

    def wait_recv(self):
        pl.when(self.received)(self.copy.wait_recv)


class Kernel:
    def __init__(self, cfg, refs):
        self.cfg = cfg
        self.__dict__.update(refs)
        self.f = lax.axis_index("fsdp")
        self.y = lax.axis_index("tp")
        core = self.f % 2
        self.x = (self.f // 2) % 2
        self.hi = self.f // 8
        self.z = (self.f // 4) % 2
        self.is_middle = self.hi + self.z == 1
        self.is_end = self.hi + self.z != 1
        self.s = (self.f // 4) % 2 * 2 + core
        self.sib = self.s + 1 - 2 * core
        self.zn = (self.s + 2) % SUB
        self.diag = (self.sib + 2) % SUB
        self.yn = 1 - self.y
        self.next_hi = (self.hi + 1) % cfg["NH"]
        self.last_hi = (self.hi + cfg["NH"] - 1) % cfg["NH"]
        self.count = 0
        self.local_count = 0
        self.sends = []
        self.gathered = []
        self.given = []
        middle = cfg["D"] // 256 * 128
        self.halves = (slice(0, middle), slice(middle, cfg["D"]))

    def index(self, hi, s, x):
        return hi * 8 + s // 2 * 4 + x * 2 + s % 2

    def mate(self, s):
        return {"fsdp": self.index(self.hi, s, self.x), "tp": self.y}

    def other(self, s):
        return {"fsdp": self.index(self.next_hi, s, self.x), "tp": self.y}

    def peer(self, hi, x):
        return {"fsdp": self.index(hi, self.s, x), "tp": self.y}

    def barrier(self):
        sem = pltpu.get_barrier_semaphore()
        partners = [self.mate(s) for s in (self.sib, self.zn, self.diag)]
        partners += [{"fsdp": self.f, "tp": self.yn}, self.peer(self.hi, 1 - self.x)]
        partners += [self.peer(self.next_hi, 1 - self.x)]
        if self.cfg["whole"]:
            partners += [self.peer(self.last_hi, 1 - self.x)]
        else:
            partners += [self.other(s) for s in (self.s, self.sib, self.zn, self.diag)]
        for partner in partners:
            pl.semaphore_signal(sem, inc=1, device_id=partner, device_id_type=pl.DeviceIdType.MESH)
        return lambda: pl.semaphore_wait(sem, len(partners))

    def remote(self, src, dst, device, sent=None, received=None):
        k = self.count
        self.count += 1
        copy = pltpu.make_async_remote_copy(
            src_ref=src,
            dst_ref=dst,
            send_sem=self.send_sems.at[k],
            recv_sem=self.recv_sems.at[k],
            device_id=device,
            device_id_type=pl.DeviceIdType.MESH,
        )
        if sent is None:
            copy.start()
        else:
            pl.when(sent)(copy.start)
            copy = Conditional(copy, sent, received)
        self.sends.append(copy)
        return copy

    def to_sib(self, src, dst):
        return self.remote(src, dst, self.mate(self.sib))

    def to_z(self, src, dst):
        return self.remote(src, dst, self.mate(self.zn))

    def to_y(self, src, dst):
        return self.remote(src, dst, {"fsdp": self.f, "tp": self.yn})

    def to_x(self, src, dst):
        return self.remote(src, dst, self.peer(self.hi, 1 - self.x))

    def to_half(self, src, dst):
        return self.remote(src, dst, self.peer(self.next_hi, self.x))

    def local(self, src, dst):
        k = self.local_count
        self.local_count += 1
        copy = pltpu.make_async_copy(src, dst, self.local_sems.at[k])
        copy.start()
        return copy


    def rows(self, hi, z, x):
        size = 2 * self.cfg["DB"]
        return pl.ds(pl.multiple_of(((hi * 2 + z) * 2 + x) * size, 16), size)

    def share(self, ref, s):
        db = self.cfg["DB"]
        return ref.at[pl.ds(pl.multiple_of(self.index(self.hi, s, self.x) * db, 16), db), :]

    def columns_out(self, key):
        full = getattr(self, "w_" + key)
        if self.cfg["whole"]:
            return {"full": full, "own": self.local(getattr(self, "sh_" + key), full), "here": []}
        if key != "qkv":
            self.prepare(key)
        shares = functools.partial(self.prepared, key)
        mine = self.share(full, self.s)
        here = [self.remote(shares(s), mine, self.mate(s)) for s in (self.zn, self.diag, self.sib)]
        self.given += here
        return {"full": full, "shares": shares, "own": self.local(shares(self.s), mine), "here": here}

    def prepared(self, key, s):
        db = self.cfg["DB"]
        rows = pl.ds(pl.multiple_of(s % 2 * db, 16), db)
        return getattr(self, "slots_" + key).at[s // 2, rows, :]

    def gain_column(self, k):
        db = self.cfg["DB"]
        line = jnp.broadcast_to(self.gains[...].astype(F32)[k : k + 1, :], (db, db))
        return jnp.sum(jnp.where(eye(db), line, 0.0), axis=1, keepdims=True)

    def prepare(self, key):
        db, ff = self.cfg["DB"], self.cfg["FF"]
        slots = getattr(self, "slots_" + key)
        if key in ("qkv", "ga", "up"):
            gain = self.gain_column(0 if key == "qkv" else 1)
        for s in range(SUB):
            if key == "qkv":
                blocks = [(k, 2 * s + h) for k in range(3) for h in range(2)]
                parts = [self.raw_qkv[k, :, n * DH : (n + 1) * DH].astype(F32) * gain for k, n in blocks]
            elif key == "out":
                parts = [self.raw_out[:, n * DH : (n + 1) * DH].astype(F32) for n in (2 * s, 2 * s + 1)]
            elif key == "dn":
                parts = [self.raw_dn[:, s * ff : (s + 1) * ff].astype(F32)]
            else:
                parts = [self.raw_gu[int(key == "up"), :, s * ff : (s + 1) * ff].astype(F32) * gain]
            value = jnp.concatenate([padded(part, -(-part.shape[1] // HP) * HP) for part in parts], axis=1)
            slots[s // 2, s % 2 * db : (s % 2 + 1) * db, :] = value.astype(BF)

    def columns_far(self, g):
        if self.cfg["whole"]:
            return
        mine = self.share(g["full"], self.s)
        g["far"], g["middle"] = [], []
        for s in (self.s, self.sib):
            g["far"].append(self.remote(g["shares"](s), mine, self.other(s)))
        for s in (self.zn, self.diag):
            g["middle"].append(self.remote(g["shares"](s), mine, self.other(s), self.is_middle, self.is_middle))
        self.given += g["far"] + g["middle"]

    def spread(self, g):
        for c in g["here"]:
            c.wait_recv()
        g["own"].wait()
        if self.cfg["whole"]:
            return
        part = g["full"].at[self.rows(self.hi, 1 - self.z, self.x), :]
        g["passed"] = self.remote(part, part, self.other(self.s), self.is_middle, self.is_end)
        parts = [g["full"].at[self.rows(self.hi, z, self.x), :] for z in range(2)]
        g["near"] = [self.to_x(part, part) for part in parts]
        self.gathered += [g["passed"]] + g["near"]

    def onward(self, g, z):
        part = g["full"].at[self.rows(self.next_hi, z, self.x), :]
        copy = self.to_x(part, part)
        g["near"].append(copy)
        self.gathered.append(copy)

    def spread_same(self, g):
        if self.cfg["whole"]:
            return
        for c in g["far"]:
            c.wait_recv()
        self.onward(g, self.z)

    def spread_rest(self, g):
        if self.cfg["whole"]:
            return
        for c in g["middle"] + [g["passed"]]:
            c.wait_recv()
        self.onward(g, 1 - self.z)

    def spread_done(self, g):
        if not self.cfg["whole"]:
            for c in g["near"]:
                c.wait_recv()

    def columns_back(self, full, result):
        if self.cfg["whole"]:
            return self.local(full, result).wait
        copies = [
            self.remote(self.share(full, s), result.at[self.s], self.mate(s)) for s in (self.zn, self.diag, self.sib)
        ]
        own = self.local(self.share(full, self.s), result.at[self.s])

        def wait():
            for c in copies:
                c.wait_recv()
            own.wait()

        return wait

    def add_rows(self, grad, rows, parts):
        size, tile = 2 * self.cfg["DB"], 2 * self.cfg["DB"]
        tile = next(t for t in (112, 32, 16) if size % t == 0)
        for i in range(size // tile):
            place = pl.ds(pl.multiple_of(rows.start + i * tile, 16), tile)
            total = grad[place, :].astype(F32)
            for part in parts:
                total = total + part[i * tile : (i + 1) * tile, :].astype(F32)
            grad[place, :] = total.astype(BF)

    def collect(self, grad, slots):
        if self.cfg["whole"]:
            return None
        near = []
        for k, hi in enumerate((self.next_hi, self.hi)):
            for z in range(2):
                near.append(self.to_x(grad.at[self.rows(hi, z, 1 - self.x), :], slots.at[2 * k + z]))
        return {"grad": grad, "slots": slots, "near": near, "far": []}

    def collect_on(self, g, planes=(0, 1)):
        if g is None:
            return
        for z in planes:
            g["near"][z].wait_recv()
            rows = self.rows(self.next_hi, z, self.x)
            self.add_rows(g["grad"], rows, [g["slots"].at[z]])
            g["far"].append(self.to_half(g["grad"].at[rows, :], g["slots"].at[4 + z]))

    def collect_done(self, g):
        if g is None:
            return
        for z in range(2):
            g["near"][2 + z].wait_recv()
            g["far"][z].wait_recv()
            rows = self.rows(self.hi, z, self.x)
            self.add_rows(g["grad"], rows, [g["slots"].at[2 + z], g["slots"].at[4 + z]])


    def rim_out(self, ends, slots):
        after = self.peer((self.hi + self.x) % self.cfg["NH"], 1 - self.x)
        return [self.to_x(ends[0], slots(self.x)), self.remote(ends[1], slots(1 - self.x), after)]

    def rim_home(self, slots, ends):
        before = self.peer((self.hi + self.cfg["NH"] - 1 + self.x) % self.cfg["NH"], 1 - self.x)
        return [self.to_x(slots(1 - self.x), ends[0]), self.remote(slots(self.x), ends[1], before)]


    def gather_start(self, buf):
        own = buf.at[self.s, self.y]
        halves = [own.at[:, h] for h in self.halves]
        z = [self.to_z(half, half) for half in halves]
        return {"z": z, "y": self.to_y(own, own), "own": self.to_sib(own, own), "buf": buf}

    def gather_relay(self, g):
        buf = g["buf"]
        g["d"], g["fz"] = [], []
        for c, h in zip(g["z"], self.halves, strict=True):
            c.wait_recv()
            part = buf.at[self.zn, self.y, :, h]
            g["d"].append(self.to_y(part, part))
            g["fz"].append(self.to_sib(part, part))
        g["y"].wait_recv()
        part = buf.at[self.s, self.yn]
        g["fy"] = self.to_sib(part, part)
        g["own"].wait_recv()

    def gather_near(self, g):
        g["fy"].wait_recv()

    def gather_finish(self, g, near=False):
        g["fd"] = []
        for c, h in zip(g["d"], self.halves, strict=True):
            c.wait_recv()
            part = g["buf"].at[self.zn, self.yn, :, h]
            g["fd"].append(self.to_sib(part, part))
        for c in ([] if near else [g["fy"]]) + g["fz"] + g["fd"]:
            c.wait_recv()
        g["copies"] = [g["own"], g["y"], g["fy"]] + g["z"] + g["d"] + g["fz"] + g["fd"]

    def scatter_pair(self, st, partial):
        sc, rc = st["sc"], st["rc"]
        copies = []
        for k, pair in enumerate((self.diag, self.sib)):
            sc[k] = partial(pair).astype(BF).reshape(sc.shape[1:])
            copies.append(self.to_sib(sc.at[k], rc.at[k]))
        return {"pair": copies, "st": st}

    def scatter_send(self, g, partial):
        st = g["st"]
        so, rc = st["so"], st["rc"]
        value = partial(self.zn)
        g["pair"][0].wait_recv()
        so[0] = (value + flat(rc[0].astype(F32))).astype(BF).reshape(so.shape[1:])
        g["d"] = [self.to_y(so.at[0, self.yn, :, h], st["rd"].at[:, h]) for h in self.halves]
        value = partial(self.s)
        g["pair"][1].wait_recv()
        so[1] = (value + flat(rc[1].astype(F32))).astype(BF).reshape(so.shape[1:])
        g["y"] = self.to_y(so.at[1, self.yn], st["ry"])

    def scatter_relay(self, g):
        st = g["st"]
        so = st["so"]
        g["z"] = []
        for c, h in zip(g["d"], self.halves, strict=True):
            c.wait_recv()
            so[0, self.y, :, h] = (so[0, self.y, :, h].astype(F32) + st["rd"][:, h].astype(F32)).astype(BF)
            g["z"].append(self.to_z(so.at[0, self.y, :, h], st["rz"].at[:, h]))

    def scatter_finish(self, g):
        st = g["st"]
        for c in g["z"] + [g["y"]]:
            c.wait_recv()
        total = st["so"][1, self.y].astype(F32) + st["rz"][...].astype(F32) + st["ry"][...].astype(F32)
        self.settle(g["pair"] + g["d"] + g["z"] + [g["y"]])
        return total


    def place(self, s):
        return 1 + 2 * s + s // 2

    def project(self, w):
        def step(i, _):
            rows = flat(self.u1[i])
            out = dot(rows, w[...], NN).astype(BF)
            self.qkv[pl.ds(self.place(i), 2)] = out.reshape(2, 2 * WINDOW, out.shape[1])
            return 0

        lax.fori_loop(0, SUB, step, 0)

    def masks(self, s):
        at = 1 + s + s // 2
        before, own = self.starts[at - 1], self.starts[at]
        lane = lax.broadcasted_iota(jnp.int32, before.shape, 1)
        even = jnp.where(lane < WINDOW, pltpu.roll(before, WINDOW, 1), pltpu.roll(own, WINDOW, 1))
        shape = (WINDOW, 2 * WINDOW)
        i = lax.broadcasted_iota(jnp.int32, shape, 0)
        j = lax.broadcasted_iota(jnp.int32, shape, 1)
        square = (2 * WINDOW, 2 * WINDOW)
        later = lax.broadcasted_iota(jnp.int32, square, 0) > lax.broadcasted_iota(jnp.int32, square, 1)
        later = later.astype(F32).astype(BF)
        band = (j <= i + WINDOW) & (j > i)
        result = []
        for rows in (even, own):
            per_batch = []
            for batch in range(2):
                line = jnp.broadcast_to(rows[batch : batch + 1, :], shape)
                line = jnp.where(j <= i + WINDOW, line, 0.0).astype(BF)
                between = dot(line, later, NN)
                per_batch.append(band & (between < 0.5))
            result.append(per_batch)
        return result

    def tile(self, index, batch, part, head):
        cols = slice(part * 2 * HP + head * HP, part * 2 * HP + (head + 1) * HP)
        return self.qkv[index, batch * WINDOW : (batch + 1) * WINDOW, cols]

    def attend(self):
        def step(n, _):
            s = SUB - 1 - n
            allowed = self.masks(s)
            for half in range(2):
                p = self.place(s) + half
                for batch in range(2):
                    for head in range(2):
                        q = self.tile(p, batch, 0, head)
                        k = jnp.concatenate([self.tile(p - 1, batch, 1, head), self.tile(p, batch, 1, head)], axis=0)
                        v = jnp.concatenate([self.tile(p - 1, batch, 2, head), self.tile(p, batch, 2, head)], axis=0)
                        scores = dot(q, k, NT) * DH ** (-0.5)
                        scores = jnp.where(allowed[half][batch], scores, -1e30)
                        top = jnp.max(scores, axis=-1, keepdims=True)
                        weights = jnp.exp(scores - top)
                        probs = weights / jnp.sum(weights, axis=-1, keepdims=True)
                        self.probs[2 * s + half, 2 * batch + head] = probs
                        out = dot(probs.astype(BF), v, NN).astype(BF)
                        self.heads[s, half, batch * WINDOW : (batch + 1) * WINDOW, head * HP : (head + 1) * HP] = out
            return 0

        lax.fori_loop(0, SUB, step, 0)

    def attend_back(self, s):
        run = s // 2
        for half in range(2):
            p = self.place(s) + half
            for batch in range(2):
                rows = slice(batch * WINDOW, (batch + 1) * WINDOW)
                for head in range(2):
                    cols = slice(head * HP, (head + 1) * HP)
                    q = self.tile(p, batch, 0, head)
                    k = jnp.concatenate([self.tile(p - 1, batch, 1, head), self.tile(p, batch, 1, head)], axis=0)
                    v = jnp.concatenate([self.tile(p - 1, batch, 2, head), self.tile(p, batch, 2, head)], axis=0)
                    probs = self.probs[2 * s + half, 2 * batch + head]
                    d_out = self.d_heads[s, half, rows, cols]
                    d_probs = dot(d_out, v, NT)
                    inner = jnp.sum(probs * d_probs, axis=-1, keepdims=True)
                    d_scores = (probs * (d_probs - inner)).astype(BF)
                    d_q = dot(d_scores, k, NN) * DH ** (-0.5)
                    d_k = dot(d_scores, q, TN) * DH ** (-0.5)
                    d_v = dot(probs.astype(BF), d_out, TN)
                    self.qkv[p, rows, head * HP : (head + 1) * HP] = d_q.astype(BF)
                    for part, grad in ((1, d_k), (2, d_v)):
                        slot = slice((part - 1) * 2 * HP + head * HP, (part - 1) * 2 * HP + (head + 1) * HP)
                        place = slice(part * 2 * HP + head * HP, part * 2 * HP + (head + 1) * HP)
                        done = self.carry[run, rows, slot] + grad[:WINDOW]
                        self.qkv[p - 1, rows, place] = done.astype(BF)
                        self.carry[run, rows, slot] = grad[WINDOW:]

    def grad_into(self, target, left, right):
        width = 256

        def step(m, _):
            cols = pl.ds(pl.multiple_of(m * width, width), width)
            parts = right()
            each = SUB // len(parts)
            total = 0.0
            for k, part in enumerate(parts):
                total = total + dot(flat(left[k * each : (k + 1) * each, :, :, cols]), part, TN)
            target[cols, :] = total.astype(BF)
            return 0

        lax.fori_loop(0, self.cfg["D"] // width, step, 0)

    def feed_forward(self, plane):
        ff = self.w_dn.shape[1]

        def step(k, _):
            i = 2 * plane + k
            rows = flat(self.u2[i])
            gate = dot(rows, self.w_ga[...], NN)
            upward = dot(rows, self.w_up[...], NN)
            d_hidden = dot(flat(self.g[i]), self.w_dn[...], NN)
            sig = jax.nn.sigmoid(gate)
            silu = gate * sig
            shape = (2, 2 * WINDOW, ff)
            self.hidden[i] = (silu * upward).astype(BF).reshape(shape)
            d_gate = d_hidden * upward * sig * (1.0 + gate * (1.0 - sig))
            self.d_ga[i] = d_gate.astype(BF).reshape(shape)
            self.d_up[i] = (d_hidden * silu).astype(BF).reshape(shape)
            return 0

        lax.fori_loop(0, 2, step, 0)

    def run(self):
        cfg = self.cfg
        me = (self.s, self.y)
        norm = lambda v: lax.rsqrt(jnp.mean(v * v, axis=-1, keepdims=True) + EPSILON)
        whole = lambda ref: [flat(ref[...])]

        everyone_here = self.barrier()
        line = 1 + self.s + self.s // 2
        own_starts = self.doc_starts[...].astype(F32)
        fill = jnp.zeros((self.starts.shape[1] - own_starts.shape[0], own_starts.shape[1]), F32)
        self.starts[line] = jnp.concatenate([own_starts, fill], axis=0)
        own_line = self.starts.at[line]
        x = self.x_in[...].astype(F32)
        self.u1[me] = (x * norm(x)).astype(BF)
        if not cfg["whole"]:
            self.prepare("qkv")
        everyone_here()
        start_copies = [self.remote(own_line, own_line, self.mate(s)) for s in (self.sib, self.zn, self.diag)]
        qkv = self.columns_out("qkv")
        gather_one = self.gather_start(self.u1)
        self.columns_far(qkv)
        self.spread(qkv)
        out = self.columns_out("out")
        self.columns_far(out)
        for c in start_copies:
            c.wait_recv()
        rim_starts = self.rim_out([self.starts.at[2], self.starts.at[5]], lambda run: self.starts.at[3 * run])
        self.gather_relay(gather_one)
        self.spread_same(qkv)
        self.spread(out)
        ga = self.columns_out("ga")
        self.spread_rest(qkv)
        self.gather_finish(gather_one)
        self.spread_done(qkv)

        self.project(self.w_qkv)
        rims = self.rim_out(
            [self.qkv.at[4, :, slice(2 * HP, 6 * HP)], self.qkv.at[9, :, slice(2 * HP, 6 * HP)]],
            lambda run: self.qkv.at[5 * run, :, slice(2 * HP, 6 * HP)],
        )
        self.columns_far(ga)
        self.spread(ga)
        up = self.columns_out("up")
        self.columns_far(up)
        self.spread_same(out)
        self.spread_rest(out)
        for c in rim_starts + rims:
            c.wait_recv()
        self.attend()
        self.spread(up)
        dn = self.columns_out("dn")
        self.spread_same(ga)
        self.spread_done(out)

        partial = lambda pair: dot(flat(self.heads[pair]), self.w_out[...], NT)
        stage = {n: getattr(self, n) for n in ("sc", "rc", "so", "rd", "rz", "ry")}
        scatter = self.scatter_pair(stage, partial)
        self.scatter_send(scatter, partial)
        self.spread_rest(ga)
        self.scatter_relay(scatter)
        self.g[me] = self.g_in[...]
        gather_g = self.gather_start(self.g)
        self.columns_far(dn)
        self.spread(dn)
        self.spread_same(up)
        self.spread_rest(up)
        self.resid[...] = self.x_in[...].astype(F32) + self.scatter_finish(scatter)
        resid = self.resid[...]
        self.u2[me] = (resid * norm(resid)).astype(BF)
        gather_two = self.gather_start(self.u2)
        self.gather_relay(gather_g)
        self.spread_same(dn)
        self.settle(self.given)
        self.spread_rest(dn)
        self.gather_relay(gather_two)
        self.gather_finish(gather_g)
        for g in (ga, up, dn):
            self.spread_done(g)
        self.gather_near(gather_two)
        self.feed_forward(self.s // 2)
        self.gather_finish(gather_two, near=True)
        self.feed_forward(1 - self.s // 2)
        self.grad_into(self.g_dn, self.g, lambda: whole(self.hidden))
        sum_dn = self.collect(self.g_dn, self.slots_dn)
        partial = lambda pair: dot(flat(self.d_ga[pair]), self.w_ga[...], NT) + dot(
            flat(self.d_up[pair]), self.w_up[...], NT
        )
        scatter = self.scatter_pair(stage, partial)
        self.scatter_send(scatter, partial)
        self.settle(self.gathered)
        self.grad_into(self.w_ga, self.u2, lambda: whole(self.d_ga))
        sum_ga = self.collect(self.w_ga, self.slots_ga)
        self.scatter_relay(scatter)
        self.collect_on(sum_dn, (0,))
        self.grad_into(self.w_up, self.u2, lambda: whole(self.d_up))
        sum_up = self.collect(self.w_up, self.slots_up)
        d_unit = self.scatter_finish(scatter)
        resid = self.resid[...]
        scale = norm(resid)
        unit = resid * scale
        inner = jnp.mean(d_unit * unit, axis=-1, keepdims=True)
        self.in_grad[...] = self.g_in[...].astype(F32) + scale * (d_unit - unit * inner)
        self.d_r[me] = self.in_grad[...].astype(BF)
        self.settle(gather_g["copies"] + gather_two["copies"] + rims)
        gather_d = self.gather_start(self.d_r)
        self.collect_on(sum_dn, (1,))
        self.gather_relay(gather_d)

        view = {
            "sc": self.u2.at[0:2],
            "so": self.u2.at[2:4],
            "rc": self.g.at[0:2],
            "rd": self.g.at[2, 0],
            "rz": self.g.at[2, 1],
            "ry": self.g.at[3, 0],
        }
        partial = lambda pair: dot(flat(self.hidden[pair]), self.w_dn[...], NT)
        mlp = self.scatter_pair(view, partial)
        self.scatter_send(mlp, partial)
        self.collect_on(sum_ga)
        self.gather_finish(gather_d)

        d_heads = self.d_heads = self.d_ga.at[:, :, :, slice(0, 2 * HP)]

        def heads_back(i, _):
            value = dot(flat(self.d_r[i]), self.w_out[...], NN).astype(BF)
            d_heads[i] = value.reshape(2, 2 * WINDOW, 2 * HP)
            return 0

        lax.fori_loop(0, SUB, heads_back, 0)
        self.collect_done(sum_dn)
        backs = [self.columns_back(self.g_dn, self.o_dn)]

        self.carry[...] = jnp.zeros_like(self.carry)

        def first(run, _):
            self.attend_back(2 * run)
            return 0

        def second(run, _):
            self.attend_back(2 * run + 1)
            return 0

        lax.fori_loop(0, 2, first, 0)
        rim_back = self.rim_home(
            lambda run: self.qkv.at[5 * run, :, slice(2 * HP, 6 * HP)], [self.rim.at[0], self.rim.at[1]]
        )
        self.scatter_relay(mlp)
        lax.fori_loop(0, 2, second, 0)
        of_q, of_kv = slice(0, 2 * HP), slice(2 * HP, 6 * HP)
        g_q, g_kv = self.g_qkv.at[:, of_q], self.g_qkv.at[:, of_kv]
        self.grad_into(g_q, self.u1, lambda: [flat(self.qkv[1:5, :, of_q]), flat(self.qkv[6:10, :, of_q])])
        sum_q = self.collect(g_q, self.slots_qkv.at[:, :, of_q])
        self.collect_on(sum_up)
        self.collect_done(sum_ga)
        backs.append(self.columns_back(self.w_ga, self.o_ga))
        for c in rim_back:
            c.wait_recv()
        for run in range(2):
            done = self.carry[run] + self.rim[run].astype(F32)
            self.qkv[5 * run + 4, :, 2 * HP :] = done.astype(BF)

        self.grad_into(g_kv, self.u1, lambda: [flat(self.qkv[1:5, :, of_kv]), flat(self.qkv[6:10, :, of_kv])])
        sum_kv = self.collect(g_kv, self.slots_qkv.at[:, :, of_kv])
        self.grad_into(self.w_out, self.d_r, lambda: whole(self.heads))
        sum_out = self.collect(self.w_out, self.slots_out)
        partial = lambda pair: dot(flat(self.qkv[pl.ds(self.place(pair), 2)]), self.w_qkv[...], NT)
        scatter = self.scatter_pair(stage, partial)
        self.scatter_send(scatter, partial)
        self.collect_on(sum_q)
        self.scatter_relay(scatter)
        self.collect_done(sum_up)
        backs.append(self.columns_back(self.w_up, self.o_up))
        self.collect_on(sum_kv)
        self.out[...] = (self.resid[...] + self.scatter_finish(mlp)).astype(BF)
        back_to = lambda span: self.o_qkv.at[:, span] if cfg["whole"] else self.o_qkv.at[:, :, span]
        self.collect_done(sum_q)
        backs.append(self.columns_back(g_q, back_to(of_q)))
        d_unit = self.scatter_finish(scatter)
        x = self.x_in[...].astype(F32)
        scale = norm(x)
        unit = x * scale
        inner = jnp.mean(d_unit * unit, axis=-1, keepdims=True)
        self.in_grad[...] += scale * (d_unit - unit * inner)
        self.collect_on(sum_out)
        self.collect_done(sum_kv)
        backs.append(self.columns_back(g_kv, back_to(of_kv)))
        self.collect_done(sum_out)
        backs.append(self.columns_back(self.w_out, self.o_out))
        for wait in backs:
            wait()
        self.settle()

    def settle(self, copies=None):
        for c in self.sends:
            if copies is None or any(c is other for other in copies):
                c.wait_send()
        if copies is None:
            self.sends = []
        else:
            self.sends = [c for c in self.sends if not any(c is other for other in copies)]


def fused(cfg, width, weights, starts, x, g):
    d, db = cfg["D"], cfg["DB"]
    rows = 2 * WINDOW
    anywhere = pl.BlockSpec(memory_space=pl.ANY)
    vmem = pl.BlockSpec(memory_space=pltpu.VMEM)
    keys = ("qkv", "out", "ga", "up", "dn")
    result = (d,) if cfg["whole"] else (SUB, db)
    outs = [("out", (rows, d), BF, vmem), ("in_grad", (rows, d), F32, vmem)]
    outs += [("o_" + key, result + (width[key],), BF, anywhere) for key in keys]
    if cfg["whole"]:
        ins = [("sh_" + key, anywhere) for key in keys]
    else:
        ins = [(name, vmem) for name in ("raw_qkv", "raw_out", "raw_gu", "raw_dn", "gains")]
    ins += [(name, vmem) for name in ("doc_starts", "x_in", "g_in")]
    plane = (SUB, 2, rows)
    scratch = [("w_" + key, (d, width[key]), BF) for key in keys]
    scratch += [("g_" + key, (d, width[key]), BF) for key in ("qkv", "dn")]
    slot = 16 if cfg["whole"] else 2 * db
    scratch += [("slots_" + key, (6, slot, width[key]), BF) for key in keys]
    scratch += [(name, plane + (d,), BF) for name in ("u1", "u2", "g", "d_r")]
    scratch += [(name, plane + (width["out"],), BF) for name in ("heads",)]
    scratch += [(name, plane + (width["dn"],), BF) for name in ("hidden", "d_ga", "d_up")]
    scratch += [(name, (2, 2, rows, d), BF) for name in ("sc", "rc", "so")]
    scratch += [
        ("starts", (SUB + 2, 8, rows), F32),
        ("qkv", (2 * SUB + 2, rows, width["qkv"]), BF),
        ("probs", (2 * SUB, 4, WINDOW, 2 * WINDOW), F32),
        ("carry", (2, rows, 4 * HP), F32),
        ("rim", (2, rows, 4 * HP), BF),
        ("resid", (rows, d), F32),
        ("rd", (rows, d), BF),
        ("rz", (rows, d), BF),
        ("ry", (rows, d), BF),
    ]
    number = 220
    names = [n for n, _ in ins] + [n for n, *_ in outs] + [n for n, *_ in scratch]
    names += ["send_sems", "recv_sems", "local_sems"]

    def kernel(*refs):
        Kernel(cfg, dict(zip(names, refs, strict=True))).run()

    return pl.pallas_call(
        kernel,
        out_shape=[jax.ShapeDtypeStruct(shape, kind) for _, shape, kind, _ in outs],
        in_specs=[spec for _, spec in ins],
        out_specs=[spec for *_, spec in outs],
        scratch_shapes=[pltpu.VMEM(shape, kind) for _, shape, kind in scratch]
        + [
            pltpu.SemaphoreType.DMA((number,)),
            pltpu.SemaphoreType.DMA((number,)),
            pltpu.SemaphoreType.DMA((11,)),
        ],
        compiler_params=pltpu.CompilerParams(
            collective_id=0, has_side_effects=True, vmem_limit_bytes=64 * 2**20
        ),
    )(*weights, starts, x, g)


def assemble(ff, o_qkv, o_out, o_ga, o_up, o_dn, w_qkv, w_gu, gains, g_qkv, g_out, g_gu, g_dn, g_gain):
    db = w_qkv.shape[1]
    lines = gains[...].astype(F32)
    same = eye(db)

    def column(k):
        return jnp.sum(jnp.where(same, jnp.broadcast_to(lines[k : k + 1, :], (db, db)), 0.0), axis=1, keepdims=True)

    sums = []
    gain = column(0)
    total = jnp.zeros((db, 1), F32)
    for k in range(3):
        parts = []
        for s in range(SUB):
            for h in range(2):
                start = (2 * k + h) * HP
                parts.append(o_qkv[s, :, start : start + DH].astype(F32))
        value = jnp.concatenate(parts, axis=1)
        total = total + jnp.sum(value * w_qkv[k].astype(F32), axis=1, keepdims=True)
        g_qkv[k] = value * gain
    sums.append(total)
    gain = column(1)
    total = jnp.zeros((db, 1), F32)
    for k, ref in enumerate((o_ga, o_up)):
        value = jnp.concatenate([ref[s, :, :ff].astype(F32) for s in range(SUB)], axis=1)
        total = total + jnp.sum(value * w_gu[k].astype(F32), axis=1, keepdims=True)
        g_gu[k] = value * gain
    sums.append(total)
    for k, total in enumerate(sums):
        g_gain[k : k + 1, :] = jnp.sum(jnp.where(same, jnp.broadcast_to(total, (db, db)), 0.0), axis=0, keepdims=True)
    parts = [o_out[s, :, h * HP : h * HP + DH].astype(F32) for s in range(SUB) for h in range(2)]
    g_out[...] = jnp.concatenate(parts, axis=1)
    g_dn[...] = jnp.concatenate([o_dn[s, :, :ff].astype(F32) for s in range(SUB)], axis=1)


def body(size, tokens, doc_starts, w_qkv, w_out, w_gate_up, w_down, gains, cotangent):
    batches, rows, d = tokens.shape
    db = w_qkv.shape[1]
    ff = w_gate_up.shape[2] // SUB
    ffp = -(-ff // HP) * HP
    heads = w_qkv.shape[2] // (SUB * DH)
    whole = size != 16 or db % 16 != 0
    cfg = {"D": d, "NH": size // 8, "DB": db, "FF": ff, "whole": whole}
    width = {"qkv": 3 * heads * HP, "out": heads * HP, "ga": ffp, "up": ffp, "dn": ffp}
    acts = [doc_starts, tokens.reshape(batches * rows, d), cotangent.reshape(batches * rows, d)]

    def results(out, in_grad, g_qkv, g_out, g_gu, g_dn, gain_sums):
        gain_sums = gain_sums + lax.ppermute(gain_sums, "tp", [(0, 1), (1, 0)])
        return (out.reshape(tokens.shape), in_grad.reshape(tokens.shape), g_qkv, g_out, g_gu, g_dn, gain_sums)

    if not whole:
        out, in_grad, *grads = fused(cfg, width, [w_qkv, w_out.T, w_gate_up, w_down.T, gains], *acts)
        vmem = pl.BlockSpec(memory_space=pltpu.VMEM)
        grads = pl.pallas_call(
            functools.partial(assemble, ff),
            out_shape=[jax.ShapeDtypeStruct(v.shape, F32) for v in (w_qkv, w_out.T, w_gate_up, w_down.T, gains)],
            in_specs=[vmem] * 8,
            out_specs=[vmem] * 5,
            compiler_params=pltpu.CompilerParams(vmem_limit_bytes=40 * 2**20),
        )(*grads, w_qkv, w_gate_up, gains)
        g_qkv, g_out, g_gu, g_dn, gain_sums = grads
        return results(out, in_grad, g_qkv, g_out.T, g_gu, g_dn.T, gain_sums)

    gain = gains.astype(F32)
    sh_qkv = (w_qkv.astype(F32) * gain[0][None, :, None]).astype(BF).reshape(3, db, SUB, heads, DH)
    sh_qkv = padded(sh_qkv, HP).transpose(2, 1, 0, 3, 4).reshape(SUB, db, 3 * heads * HP)
    sh_out = w_out.T.reshape(db, SUB, heads, DH)
    sh_out = padded(sh_out, HP).transpose(1, 0, 2, 3).reshape(SUB, db, heads * HP)
    scaled = (w_gate_up.astype(F32) * gain[1][None, :, None]).astype(BF).reshape(2, db, SUB, ff)
    sh_ga, sh_up = [padded(scaled[k], ffp).transpose(1, 0, 2) for k in range(2)]
    sh_dn = padded(w_down.T.reshape(db, SUB, ff), ffp).transpose(1, 0, 2)
    f = lax.axis_index("fsdp")
    s = (f // 4) % 2 * 2 + f % 2
    everyone = [lax.all_gather(v, "fsdp", axis=1, tiled=True) for v in (sh_qkv, sh_out, sh_ga, sh_up, sh_dn)]
    shares = [lax.dynamic_index_in_dim(v, s, 0, keepdims=False) for v in everyone]
    out, in_grad, *grads = fused(cfg, width, shares, *acts)
    mine = (jnp.arange(SUB) == s)[:, None, None]
    g_qkv, g_out, g_ga, g_up, g_dn = [
        lax.psum_scatter(jnp.where(mine, v[None], 0).astype(BF), "fsdp", scatter_dimension=1, tiled=True).astype(F32)
        for v in grads
    ]
    g_qkv = g_qkv.reshape(SUB, db, 3, heads, HP)[..., :DH].transpose(2, 1, 0, 3, 4).reshape(w_qkv.shape)
    g_out = g_out.reshape(SUB, db, heads, HP)[..., :DH].transpose(0, 2, 3, 1).reshape(w_out.shape)
    g_gu = jnp.stack([v[..., :ff].transpose(1, 0, 2).reshape(w_gate_up.shape[1:]) for v in (g_ga, g_up)])
    g_dn = g_dn[..., :ff].transpose(0, 2, 1).reshape(w_down.shape)
    gain_sums = jnp.stack(
        [
            jnp.sum(g_qkv * w_qkv.astype(F32), axis=(0, 2)),
            jnp.sum(g_gu * w_gate_up.astype(F32), axis=(0, 2)),
        ]
    )
    g_qkv, g_gu = g_qkv * gain[0][None, :, None], g_gu * gain[1][None, :, None]
    return results(out, in_grad, g_qkv, g_out, g_gu, g_dn, gain_sums)


def solution(mesh):
    in_specs = (
        P(None, ("fsdp", "tp"), None),
        P(None, "fsdp"),
        P(None, "fsdp", "tp"),
        P("tp", "fsdp"),
        P(None, "fsdp", "tp"),
        P("tp", "fsdp"),
        P(None, "fsdp"),
        P(None, ("fsdp", "tp"), None),
    )
    out_specs = (
        P(None, ("fsdp", "tp"), None),
        P(None, ("fsdp", "tp"), None),
        P(None, "fsdp", "tp"),
        P("tp", "fsdp"),
        P(None, "fsdp", "tp"),
        P("tp", "fsdp"),
        P(None, "fsdp"),
    )
    return jax.shard_map(
        functools.partial(body, mesh.shape["fsdp"]), mesh=mesh, in_specs=in_specs, out_specs=out_specs, check_vma=False
    )
```

```python
import functools

import jax
import jax.numpy as jnp
from jax import lax
from jax.experimental import pallas as pl
from jax.experimental.pallas import tpu as pltpu
from jax.sharding import PartitionSpec as P

DH = 112
HP = 128
WINDOW = 64
EPSILON = 1e-06
SUB = 4
BF = jnp.bfloat16
F32 = jnp.float32
NN = (((1,), (0,)), ((), ()))
NT = (((1,), (1,)), ((), ()))
TN = (((0,), (0,)), ((), ()))


def dot(a, b, dims):
    return lax.dot_general(a, b, dims, preferred_element_type=F32)


def flat(value):
    return value.reshape(-1, value.shape[-1])


def eye(size):
    shape = (size, size)
    return lax.broadcasted_iota(jnp.int32, shape, 0) == lax.broadcasted_iota(jnp.int32, shape, 1)


def padded(value, size):
    extra = size - value.shape[-1]
    if not extra:
        return value
    return jnp.concatenate([value, jnp.zeros(value.shape[:-1] + (extra,), value.dtype)], axis=-1)


class Conditional:
    def __init__(self, copy, sent, received):
        self.copy, self.sent, self.received = copy, sent, received

    def wait_send(self):
        pl.when(self.sent)(self.copy.wait_send)

    def wait_recv(self):
        pl.when(self.received)(self.copy.wait_recv)


class Kernel:
    def __init__(self, cfg, refs):
        self.cfg = cfg
        self.__dict__.update(refs)
        self.f = lax.axis_index("fsdp")
        self.y = lax.axis_index("tp")
        core = self.f % 2
        self.x = (self.f // 2) % 2
        self.hi = self.f // 8
        self.z = (self.f // 4) % 2
        self.is_middle = self.hi + self.z == 1
        self.is_end = self.hi + self.z != 1
        self.s = (self.f // 4) % 2 * 2 + core
        self.sib = self.s + 1 - 2 * core
        self.zn = (self.s + 2) % SUB
        self.diag = (self.sib + 2) % SUB
        self.yn = 1 - self.y
        self.next_hi = (self.hi + 1) % cfg["NH"]
        self.last_hi = (self.hi + cfg["NH"] - 1) % cfg["NH"]
        self.count = 0
        self.local_count = 0
        self.sends = []
        self.gathered = []
        self.given = []
        middle = cfg["D"] // 256 * 128
        self.halves = (slice(0, middle), slice(middle, cfg["D"]))

    def index(self, hi, s, x):
        return hi * 8 + s // 2 * 4 + x * 2 + s % 2

    def mate(self, s):
        return {"fsdp": self.index(self.hi, s, self.x), "tp": self.y}

    def other(self, s):
        return {"fsdp": self.index(self.next_hi, s, self.x), "tp": self.y}

    def peer(self, hi, x):
        return {"fsdp": self.index(hi, self.s, x), "tp": self.y}

    def barrier(self):
        sem = pltpu.get_barrier_semaphore()
        partners = [self.mate(s) for s in (self.sib, self.zn, self.diag)]
        partners += [{"fsdp": self.f, "tp": self.yn}, self.peer(self.hi, 1 - self.x)]
        partners += [self.peer(self.next_hi, 1 - self.x)]
        if self.cfg["whole"]:
            partners += [self.peer(self.last_hi, 1 - self.x)]
        else:
            partners += [self.other(s) for s in (self.s, self.sib, self.zn, self.diag)]
        for partner in partners:
            pl.semaphore_signal(sem, inc=1, device_id=partner, device_id_type=pl.DeviceIdType.MESH)
        return lambda: pl.semaphore_wait(sem, len(partners))

    def remote(self, src, dst, device, sent=None, received=None):
        k = self.count
        self.count += 1
        copy = pltpu.make_async_remote_copy(
            src_ref=src,
            dst_ref=dst,
            send_sem=self.send_sems.at[k],
            recv_sem=self.recv_sems.at[k],
            device_id=device,
            device_id_type=pl.DeviceIdType.MESH,
        )
        if sent is None:
            copy.start()
        else:
            pl.when(sent)(copy.start)
            copy = Conditional(copy, sent, received)
        self.sends.append(copy)
        return copy

    def to_sib(self, src, dst):
        return self.remote(src, dst, self.mate(self.sib))

    def to_z(self, src, dst):
        return self.remote(src, dst, self.mate(self.zn))

    def to_y(self, src, dst):
        return self.remote(src, dst, {"fsdp": self.f, "tp": self.yn})

    def to_x(self, src, dst):
        return self.remote(src, dst, self.peer(self.hi, 1 - self.x))

    def to_half(self, src, dst):
        return self.remote(src, dst, self.peer(self.next_hi, self.x))

    def local(self, src, dst):
        k = self.local_count
        self.local_count += 1
        copy = pltpu.make_async_copy(src, dst, self.local_sems.at[k])
        copy.start()
        return copy


    def rows(self, hi, z, x):
        size = 2 * self.cfg["DB"]
        return pl.ds(pl.multiple_of(((hi * 2 + z) * 2 + x) * size, 16), size)

    def share(self, ref, s):
        db = self.cfg["DB"]
        return ref.at[pl.ds(pl.multiple_of(self.index(self.hi, s, self.x) * db, 16), db), :]

    def columns_out(self, key):
        full = getattr(self, "w_" + key)
        if self.cfg["whole"]:
            return {"full": full, "own": self.local(getattr(self, "sh_" + key), full), "here": []}
        if key != "qkv":
            self.prepare(key)
        shares = functools.partial(self.prepared, key)
        mine = self.share(full, self.s)
        here = [self.remote(shares(s), mine, self.mate(s)) for s in (self.zn, self.diag, self.sib)]
        self.given += here
        return {"full": full, "shares": shares, "own": self.local(shares(self.s), mine), "here": here}

    def prepared(self, key, s):
        db = self.cfg["DB"]
        rows = pl.ds(pl.multiple_of(s % 2 * db, 16), db)
        return getattr(self, "slots_" + key).at[s // 2, rows, :]

    def gain_column(self, k):
        db = self.cfg["DB"]
        line = jnp.broadcast_to(self.gains[...].astype(F32)[k : k + 1, :], (db, db))
        return jnp.sum(jnp.where(eye(db), line, 0.0), axis=1, keepdims=True)

    def prepare(self, key):
        db, ff = self.cfg["DB"], self.cfg["FF"]
        slots = getattr(self, "slots_" + key)
        if key in ("qkv", "ga", "up"):
            gain = self.gain_column(0 if key == "qkv" else 1)
        for s in range(SUB):
            if key == "qkv":
                blocks = [(k, 2 * s + h) for k in range(3) for h in range(2)]
                parts = [self.raw_qkv[k, :, n * DH : (n + 1) * DH].astype(F32) * gain for k, n in blocks]
            elif key == "out":
                parts = [self.raw_out[:, n * DH : (n + 1) * DH].astype(F32) for n in (2 * s, 2 * s + 1)]
            elif key == "dn":
                parts = [self.raw_dn[:, s * ff : (s + 1) * ff].astype(F32)]
            else:
                parts = [self.raw_gu[int(key == "up"), :, s * ff : (s + 1) * ff].astype(F32) * gain]
            value = jnp.concatenate([padded(part, -(-part.shape[1] // HP) * HP) for part in parts], axis=1)
            slots[s // 2, s % 2 * db : (s % 2 + 1) * db, :] = value.astype(BF)

    def columns_far(self, g):
        if self.cfg["whole"]:
            return
        mine = self.share(g["full"], self.s)
        g["far"], g["middle"] = [], []
        for s in (self.s, self.sib):
            g["far"].append(self.remote(g["shares"](s), mine, self.other(s)))
        for s in (self.zn, self.diag):
            g["middle"].append(self.remote(g["shares"](s), mine, self.other(s), self.is_middle, self.is_middle))
        self.given += g["far"] + g["middle"]

    def spread(self, g):
        for c in g["here"]:
            c.wait_recv()
        g["own"].wait()
        if self.cfg["whole"]:
            return
        part = g["full"].at[self.rows(self.hi, 1 - self.z, self.x), :]
        g["passed"] = self.remote(part, part, self.other(self.s), self.is_middle, self.is_end)
        parts = [g["full"].at[self.rows(self.hi, z, self.x), :] for z in range(2)]
        g["near"] = [self.to_x(part, part) for part in parts]
        self.gathered += [g["passed"]] + g["near"]

    def onward(self, g, z):
        part = g["full"].at[self.rows(self.next_hi, z, self.x), :]
        copy = self.to_x(part, part)
        g["near"].append(copy)
        self.gathered.append(copy)

    def spread_same(self, g):
        if self.cfg["whole"]:
            return
        for c in g["far"]:
            c.wait_recv()
        self.onward(g, self.z)

    def spread_rest(self, g):
        if self.cfg["whole"]:
            return
        for c in g["middle"] + [g["passed"]]:
            c.wait_recv()
        self.onward(g, 1 - self.z)

    def spread_done(self, g):
        if not self.cfg["whole"]:
            for c in g["near"]:
                c.wait_recv()

    def columns_back(self, full, result):
        if self.cfg["whole"]:
            return self.local(full, result).wait
        copies = [
            self.remote(self.share(full, s), result.at[self.s], self.mate(s)) for s in (self.zn, self.diag, self.sib)
        ]
        own = self.local(self.share(full, self.s), result.at[self.s])

        def wait():
            for c in copies:
                c.wait_recv()
            own.wait()

        return wait

    def add_rows(self, grad, rows, parts):
        size, tile = 2 * self.cfg["DB"], 2 * self.cfg["DB"]
        tile = next(t for t in (112, 32, 16) if size % t == 0)
        for i in range(size // tile):
            place = pl.ds(pl.multiple_of(rows.start + i * tile, 16), tile)
            total = grad[place, :].astype(F32)
            for part in parts:
                total = total + part[i * tile : (i + 1) * tile, :].astype(F32)
            grad[place, :] = total.astype(BF)

    def collect(self, grad, slots):
        if self.cfg["whole"]:
            return None
        near = []
        for k, hi in enumerate((self.next_hi, self.hi)):
            for z in range(2):
                near.append(self.to_x(grad.at[self.rows(hi, z, 1 - self.x), :], slots.at[2 * k + z]))
        return {"grad": grad, "slots": slots, "near": near, "far": []}

    def collect_on(self, g, planes=(0, 1)):
        if g is None:
            return
        for z in planes:
            g["near"][z].wait_recv()
            rows = self.rows(self.next_hi, z, self.x)
            self.add_rows(g["grad"], rows, [g["slots"].at[z]])
            g["far"].append(self.to_half(g["grad"].at[rows, :], g["slots"].at[4 + z]))

    def collect_done(self, g):
        if g is None:
            return
        for z in range(2):
            g["near"][2 + z].wait_recv()
            g["far"][z].wait_recv()
            rows = self.rows(self.hi, z, self.x)
            self.add_rows(g["grad"], rows, [g["slots"].at[2 + z], g["slots"].at[4 + z]])


    def rim_out(self, ends, slots):
        after = self.peer((self.hi + self.x) % self.cfg["NH"], 1 - self.x)
        return [self.to_x(ends[0], slots(self.x)), self.remote(ends[1], slots(1 - self.x), after)]

    def rim_home(self, slots, ends):
        before = self.peer((self.hi + self.cfg["NH"] - 1 + self.x) % self.cfg["NH"], 1 - self.x)
        return [self.to_x(slots(1 - self.x), ends[0]), self.remote(slots(self.x), ends[1], before)]


    def gather_start(self, buf):
        own = buf.at[self.s, self.y]
        halves = [own.at[:, h] for h in self.halves]
        z = [self.to_z(half, half) for half in halves]
        return {"z": z, "y": self.to_y(own, own), "own": self.to_sib(own, own), "buf": buf}

    def gather_relay(self, g):
        buf = g["buf"]
        g["d"], g["fz"] = [], []
        for c, h in zip(g["z"], self.halves, strict=True):
            c.wait_recv()
            part = buf.at[self.zn, self.y, :, h]
            g["d"].append(self.to_y(part, part))
            g["fz"].append(self.to_sib(part, part))
        g["y"].wait_recv()
        part = buf.at[self.s, self.yn]
        g["fy"] = self.to_sib(part, part)
        g["own"].wait_recv()

    def gather_near(self, g):
        g["fy"].wait_recv()

    def gather_finish(self, g, near=False):
        g["fd"] = []
        for c, h in zip(g["d"], self.halves, strict=True):
            c.wait_recv()
            part = g["buf"].at[self.zn, self.yn, :, h]
            g["fd"].append(self.to_sib(part, part))
        for c in ([] if near else [g["fy"]]) + g["fz"] + g["fd"]:
            c.wait_recv()
        g["copies"] = [g["own"], g["y"], g["fy"]] + g["z"] + g["d"] + g["fz"] + g["fd"]

    def scatter_pair(self, st, partial):
        sc, rc = st["sc"], st["rc"]
        copies = []
        for k, pair in enumerate((self.diag, self.sib)):
            sc[k] = partial(pair).astype(BF).reshape(sc.shape[1:])
            copies.append(self.to_sib(sc.at[k], rc.at[k]))
        return {"pair": copies, "st": st}

    def scatter_send(self, g, partial):
        st = g["st"]
        so, rc = st["so"], st["rc"]
        value = partial(self.zn)
        g["pair"][0].wait_recv()
        so[0] = (value + flat(rc[0].astype(F32))).astype(BF).reshape(so.shape[1:])
        g["d"] = [self.to_y(so.at[0, self.yn, :, h], st["rd"].at[:, h]) for h in self.halves]
        value = partial(self.s)
        g["pair"][1].wait_recv()
        so[1] = (value + flat(rc[1].astype(F32))).astype(BF).reshape(so.shape[1:])
        g["y"] = self.to_y(so.at[1, self.yn], st["ry"])

    def scatter_relay(self, g):
        st = g["st"]
        so = st["so"]
        g["z"] = []
        for c, h in zip(g["d"], self.halves, strict=True):
            c.wait_recv()
            so[0, self.y, :, h] = (so[0, self.y, :, h].astype(F32) + st["rd"][:, h].astype(F32)).astype(BF)
            g["z"].append(self.to_z(so.at[0, self.y, :, h], st["rz"].at[:, h]))

    def scatter_finish(self, g):
        st = g["st"]
        for c in g["z"] + [g["y"]]:
            c.wait_recv()
        total = st["so"][1, self.y].astype(F32) + st["rz"][...].astype(F32) + st["ry"][...].astype(F32)
        self.settle(g["pair"] + g["d"] + g["z"] + [g["y"]])
        return total


    def place(self, s):
        return 1 + 2 * s + s // 2

    def project(self, w):
        def step(i, _):
            rows = flat(self.u1[i])
            out = dot(rows, w[...], NN).astype(BF)
            self.qkv[pl.ds(self.place(i), 2)] = out.reshape(2, 2 * WINDOW, out.shape[1])
            return 0

        lax.fori_loop(0, SUB, step, 0)

    def masks(self, s):
        at = 1 + s + s // 2
        before, own = self.starts[at - 1], self.starts[at]
        lane = lax.broadcasted_iota(jnp.int32, before.shape, 1)
        even = jnp.where(lane < WINDOW, pltpu.roll(before, WINDOW, 1), pltpu.roll(own, WINDOW, 1))
        shape = (WINDOW, 2 * WINDOW)
        i = lax.broadcasted_iota(jnp.int32, shape, 0)
        j = lax.broadcasted_iota(jnp.int32, shape, 1)
        square = (2 * WINDOW, 2 * WINDOW)
        later = lax.broadcasted_iota(jnp.int32, square, 0) > lax.broadcasted_iota(jnp.int32, square, 1)
        later = later.astype(F32).astype(BF)
        band = (j <= i + WINDOW) & (j > i)
        result = []
        for rows in (even, own):
            per_batch = []
            for batch in range(2):
                line = jnp.broadcast_to(rows[batch : batch + 1, :], shape)
                line = jnp.where(j <= i + WINDOW, line, 0.0).astype(BF)
                between = dot(line, later, NN)
                per_batch.append(band & (between < 0.5))
            result.append(per_batch)
        return result

    def tile(self, index, batch, part, head):
        cols = slice(part * 2 * HP + head * HP, part * 2 * HP + (head + 1) * HP)
        return self.qkv[index, batch * WINDOW : (batch + 1) * WINDOW, cols]

    def attend(self, first):
        def step(run, _):
            s = 2 * run + first
            allowed = self.masks(s)
            for half in range(2):
                p = self.place(s) + half
                for batch in range(2):
                    for head in range(2):
                        q = self.tile(p, batch, 0, head)
                        k = jnp.concatenate([self.tile(p - 1, batch, 1, head), self.tile(p, batch, 1, head)], axis=0)
                        v = jnp.concatenate([self.tile(p - 1, batch, 2, head), self.tile(p, batch, 2, head)], axis=0)
                        scores = dot(q, k, NT) * DH ** (-0.5)
                        scores = jnp.where(allowed[half][batch], scores, -1e30)
                        top = jnp.max(scores, axis=-1, keepdims=True)
                        weights = jnp.exp(scores - top)
                        probs = weights / jnp.sum(weights, axis=-1, keepdims=True)
                        self.probs[2 * s + half, 2 * batch + head] = probs
                        out = dot(probs.astype(BF), v, NN).astype(BF)
                        self.heads[s, half, batch * WINDOW : (batch + 1) * WINDOW, head * HP : (head + 1) * HP] = out
            return 0

        lax.fori_loop(0, 2, step, 0)

    def attend_back(self, s):
        run = s // 2
        for half in range(2):
            p = self.place(s) + half
            for batch in range(2):
                rows = slice(batch * WINDOW, (batch + 1) * WINDOW)
                for head in range(2):
                    cols = slice(head * HP, (head + 1) * HP)
                    q = self.tile(p, batch, 0, head)
                    k = jnp.concatenate([self.tile(p - 1, batch, 1, head), self.tile(p, batch, 1, head)], axis=0)
                    v = jnp.concatenate([self.tile(p - 1, batch, 2, head), self.tile(p, batch, 2, head)], axis=0)
                    probs = self.probs[2 * s + half, 2 * batch + head]
                    d_out = self.d_heads[s, half, rows, cols]
                    d_probs = dot(d_out, v, NT)
                    inner = jnp.sum(probs * d_probs, axis=-1, keepdims=True)
                    d_scores = (probs * (d_probs - inner)).astype(BF)
                    d_q = dot(d_scores, k, NN) * DH ** (-0.5)
                    d_k = dot(d_scores, q, TN) * DH ** (-0.5)
                    d_v = dot(probs.astype(BF), d_out, TN)
                    self.qkv[p, rows, head * HP : (head + 1) * HP] = d_q.astype(BF)
                    for part, grad in ((1, d_k), (2, d_v)):
                        slot = slice((part - 1) * 2 * HP + head * HP, (part - 1) * 2 * HP + (head + 1) * HP)
                        place = slice(part * 2 * HP + head * HP, part * 2 * HP + (head + 1) * HP)
                        done = self.carry[run, rows, slot] + grad[:WINDOW]
                        self.qkv[p - 1, rows, place] = done.astype(BF)
                        self.carry[run, rows, slot] = grad[WINDOW:]

    def grad_into(self, target, left, right):
        width = 256

        def step(m, _):
            cols = pl.ds(pl.multiple_of(m * width, width), width)
            parts = right()
            each = SUB // len(parts)
            total = 0.0
            for k, part in enumerate(parts):
                total = total + dot(flat(left[k * each : (k + 1) * each, :, :, cols]), part, TN)
            target[cols, :] = total.astype(BF)
            return 0

        lax.fori_loop(0, self.cfg["D"] // width, step, 0)

    def feed_forward(self, plane):
        ff = self.w_dn.shape[1]

        def step(k, _):
            i = 2 * plane + k
            rows = flat(self.u2[i])
            gate = dot(rows, self.w_ga[...], NN)
            upward = dot(rows, self.w_up[...], NN)
            d_hidden = dot(flat(self.g[i]), self.w_dn[...], NN)
            sig = jax.nn.sigmoid(gate)
            silu = gate * sig
            shape = (2, 2 * WINDOW, ff)
            self.hidden[i] = (silu * upward).astype(BF).reshape(shape)
            d_gate = d_hidden * upward * sig * (1.0 + gate * (1.0 - sig))
            self.d_ga[i] = d_gate.astype(BF).reshape(shape)
            self.d_up[i] = (d_hidden * silu).astype(BF).reshape(shape)
            return 0

        lax.fori_loop(0, 2, step, 0)

    def run(self):
        cfg = self.cfg
        me = (self.s, self.y)
        norm = lambda v: lax.rsqrt(jnp.mean(v * v, axis=-1, keepdims=True) + EPSILON)
        whole = lambda ref: [flat(ref[...])]

        everyone_here = self.barrier()
        line = 1 + self.s + self.s // 2
        own_starts = self.doc_starts[...].astype(F32)
        fill = jnp.zeros((self.starts.shape[1] - own_starts.shape[0], own_starts.shape[1]), F32)
        self.starts[line] = jnp.concatenate([own_starts, fill], axis=0)
        own_line = self.starts.at[line]
        x = self.x_in[...].astype(F32)
        self.u1[me] = (x * norm(x)).astype(BF)
        if not cfg["whole"]:
            self.prepare("qkv")
        everyone_here()
        start_copies = [self.remote(own_line, own_line, self.mate(s)) for s in (self.sib, self.zn, self.diag)]
        qkv = self.columns_out("qkv")
        gather_one = self.gather_start(self.u1)
        self.columns_far(qkv)
        self.spread(qkv)
        for c in start_copies:
            c.wait_recv()
        rim_starts = self.rim_out([self.starts.at[2], self.starts.at[5]], lambda run: self.starts.at[3 * run])
        self.spread_same(qkv)
        self.gather_relay(gather_one)
        self.spread_rest(qkv)
        out = self.columns_out("out")
        self.columns_far(out)
        ga = self.columns_out("ga")
        self.gather_finish(gather_one)
        self.spread_done(qkv)

        self.project(self.w_qkv)
        rims = self.rim_out(
            [self.qkv.at[4, :, slice(2 * HP, 6 * HP)], self.qkv.at[9, :, slice(2 * HP, 6 * HP)]],
            lambda run: self.qkv.at[5 * run, :, slice(2 * HP, 6 * HP)],
        )
        self.spread(out)
        self.columns_far(ga)
        up = self.columns_out("up")
        self.attend(1)
        self.spread_same(out)
        self.spread_rest(out)
        for c in rim_starts + rims:
            c.wait_recv()
        self.spread(ga)
        self.columns_far(up)
        self.attend(0)
        self.spread(up)
        dn = self.columns_out("dn")
        self.spread_same(ga)
        self.spread_done(out)

        partial = lambda pair: dot(flat(self.heads[pair]), self.w_out[...], NT)
        stage = {n: getattr(self, n) for n in ("sc", "rc", "so", "rd", "rz", "ry")}
        scatter = self.scatter_pair(stage, partial)
        self.scatter_send(scatter, partial)
        self.scatter_relay(scatter)
        self.spread_rest(ga)
        self.g[me] = self.g_in[...]
        gather_g = self.gather_start(self.g)
        self.columns_far(dn)
        self.spread(dn)
        self.spread_same(up)
        self.resid[...] = self.x_in[...].astype(F32) + self.scatter_finish(scatter)
        resid = self.resid[...]
        self.u2[me] = (resid * norm(resid)).astype(BF)
        gather_two = self.gather_start(self.u2)
        self.spread_rest(up)
        self.spread_same(dn)
        self.gather_relay(gather_g)
        self.settle(self.given)
        self.spread_rest(dn)
        self.gather_relay(gather_two)
        self.gather_finish(gather_g)
        for g in (ga, up, dn):
            self.spread_done(g)
        self.gather_near(gather_two)
        self.feed_forward(self.s // 2)
        self.gather_finish(gather_two, near=True)
        self.feed_forward(1 - self.s // 2)
        self.grad_into(self.g_dn, self.g, lambda: whole(self.hidden))
        sum_dn = self.collect(self.g_dn, self.slots_dn)
        partial = lambda pair: dot(flat(self.d_ga[pair]), self.w_ga[...], NT) + dot(
            flat(self.d_up[pair]), self.w_up[...], NT
        )
        scatter = self.scatter_pair(stage, partial)
        self.scatter_send(scatter, partial)
        self.settle(self.gathered)
        self.grad_into(self.w_ga, self.u2, lambda: whole(self.d_ga))
        sum_ga = self.collect(self.w_ga, self.slots_ga)
        self.scatter_relay(scatter)
        self.collect_on(sum_dn, (0,))
        self.grad_into(self.w_up, self.u2, lambda: whole(self.d_up))
        sum_up = self.collect(self.w_up, self.slots_up)
        d_unit = self.scatter_finish(scatter)
        resid = self.resid[...]
        scale = norm(resid)
        unit = resid * scale
        inner = jnp.mean(d_unit * unit, axis=-1, keepdims=True)
        self.in_grad[...] = self.g_in[...].astype(F32) + scale * (d_unit - unit * inner)
        self.d_r[me] = self.in_grad[...].astype(BF)
        self.settle(gather_g["copies"] + gather_two["copies"] + rims)
        gather_d = self.gather_start(self.d_r)
        self.collect_on(sum_dn, (1,))
        self.gather_relay(gather_d)

        view = {
            "sc": self.u2.at[0:2],
            "so": self.u2.at[2:4],
            "rc": self.g.at[0:2],
            "rd": self.g.at[2, 0],
            "rz": self.g.at[2, 1],
            "ry": self.g.at[3, 0],
        }
        partial = lambda pair: dot(flat(self.hidden[pair]), self.w_dn[...], NT)
        mlp = self.scatter_pair(view, partial)
        self.scatter_send(mlp, partial)
        self.collect_on(sum_ga)
        self.gather_finish(gather_d)

        d_heads = self.d_heads = self.d_ga.at[:, :, :, slice(0, 2 * HP)]

        def heads_back(i, _):
            value = dot(flat(self.d_r[i]), self.w_out[...], NN).astype(BF)
            d_heads[i] = value.reshape(2, 2 * WINDOW, 2 * HP)
            return 0

        lax.fori_loop(0, SUB, heads_back, 0)
        self.collect_done(sum_dn)
        backs = [self.columns_back(self.g_dn, self.o_dn)]

        self.carry[...] = jnp.zeros_like(self.carry)

        def first(run, _):
            self.attend_back(2 * run)
            return 0

        def second(run, _):
            self.attend_back(2 * run + 1)
            return 0

        lax.fori_loop(0, 2, first, 0)
        rim_back = self.rim_home(
            lambda run: self.qkv.at[5 * run, :, slice(2 * HP, 6 * HP)], [self.rim.at[0], self.rim.at[1]]
        )
        self.scatter_relay(mlp)
        lax.fori_loop(0, 2, second, 0)
        of_q, of_kv = slice(0, 2 * HP), slice(2 * HP, 6 * HP)
        g_q, g_kv = self.g_qkv.at[:, of_q], self.g_qkv.at[:, of_kv]
        self.grad_into(g_q, self.u1, lambda: [flat(self.qkv[1:5, :, of_q]), flat(self.qkv[6:10, :, of_q])])
        sum_q = self.collect(g_q, self.slots_qkv.at[:, :, of_q])
        self.collect_on(sum_up)
        self.collect_done(sum_ga)
        backs.append(self.columns_back(self.w_ga, self.o_ga))
        for c in rim_back:
            c.wait_recv()
        for run in range(2):
            done = self.carry[run] + self.rim[run].astype(F32)
            self.qkv[5 * run + 4, :, 2 * HP :] = done.astype(BF)

        self.grad_into(g_kv, self.u1, lambda: [flat(self.qkv[1:5, :, of_kv]), flat(self.qkv[6:10, :, of_kv])])
        sum_kv = self.collect(g_kv, self.slots_qkv.at[:, :, of_kv])
        self.grad_into(self.w_out, self.d_r, lambda: whole(self.heads))
        sum_out = self.collect(self.w_out, self.slots_out)
        partial = lambda pair: dot(flat(self.qkv[pl.ds(self.place(pair), 2)]), self.w_qkv[...], NT)
        scatter = self.scatter_pair(stage, partial)
        self.scatter_send(scatter, partial)
        self.collect_on(sum_q)
        self.scatter_relay(scatter)
        self.collect_done(sum_up)
        backs.append(self.columns_back(self.w_up, self.o_up))
        self.collect_on(sum_kv)
        self.out[...] = (self.resid[...] + self.scatter_finish(mlp)).astype(BF)
        back_to = lambda span: self.o_qkv.at[:, span] if cfg["whole"] else self.o_qkv.at[:, :, span]
        self.collect_done(sum_q)
        backs.append(self.columns_back(g_q, back_to(of_q)))
        d_unit = self.scatter_finish(scatter)
        x = self.x_in[...].astype(F32)
        scale = norm(x)
        unit = x * scale
        inner = jnp.mean(d_unit * unit, axis=-1, keepdims=True)
        self.in_grad[...] += scale * (d_unit - unit * inner)
        self.collect_on(sum_out)
        self.collect_done(sum_kv)
        backs.append(self.columns_back(g_kv, back_to(of_kv)))
        self.collect_done(sum_out)
        backs.append(self.columns_back(self.w_out, self.o_out))
        for wait in backs:
            wait()
        self.settle()

    def settle(self, copies=None):
        for c in self.sends:
            if copies is None or any(c is other for other in copies):
                c.wait_send()
        if copies is None:
            self.sends = []
        else:
            self.sends = [c for c in self.sends if not any(c is other for other in copies)]


def fused(cfg, width, weights, starts, x, g):
    d, db = cfg["D"], cfg["DB"]
    rows = 2 * WINDOW
    anywhere = pl.BlockSpec(memory_space=pl.ANY)
    vmem = pl.BlockSpec(memory_space=pltpu.VMEM)
    keys = ("qkv", "out", "ga", "up", "dn")
    result = (d,) if cfg["whole"] else (SUB, db)
    outs = [("out", (rows, d), BF, vmem), ("in_grad", (rows, d), F32, vmem)]
    outs += [("o_" + key, result + (width[key],), BF, anywhere) for key in keys]
    if cfg["whole"]:
        ins = [("sh_" + key, anywhere) for key in keys]
    else:
        ins = [(name, vmem) for name in ("raw_qkv", "raw_out", "raw_gu", "raw_dn", "gains")]
    ins += [(name, vmem) for name in ("doc_starts", "x_in", "g_in")]
    plane = (SUB, 2, rows)
    scratch = [("w_" + key, (d, width[key]), BF) for key in keys]
    scratch += [("g_" + key, (d, width[key]), BF) for key in ("qkv", "dn")]
    slot = 16 if cfg["whole"] else 2 * db
    scratch += [("slots_" + key, (6, slot, width[key]), BF) for key in keys]
    scratch += [(name, plane + (d,), BF) for name in ("u1", "u2", "g", "d_r")]
    scratch += [(name, plane + (width["out"],), BF) for name in ("heads",)]
    scratch += [(name, plane + (width["dn"],), BF) for name in ("hidden", "d_ga", "d_up")]
    scratch += [(name, (2, 2, rows, d), BF) for name in ("sc", "rc", "so")]
    scratch += [
        ("starts", (SUB + 2, 8, rows), F32),
        ("qkv", (2 * SUB + 2, rows, width["qkv"]), BF),
        ("probs", (2 * SUB, 4, WINDOW, 2 * WINDOW), F32),
        ("carry", (2, rows, 4 * HP), F32),
        ("rim", (2, rows, 4 * HP), BF),
        ("resid", (rows, d), F32),
        ("rd", (rows, d), BF),
        ("rz", (rows, d), BF),
        ("ry", (rows, d), BF),
    ]
    number = 220
    names = [n for n, _ in ins] + [n for n, *_ in outs] + [n for n, *_ in scratch]
    names += ["send_sems", "recv_sems", "local_sems"]

    def kernel(*refs):
        Kernel(cfg, dict(zip(names, refs, strict=True))).run()

    return pl.pallas_call(
        kernel,
        out_shape=[jax.ShapeDtypeStruct(shape, kind) for _, shape, kind, _ in outs],
        in_specs=[spec for _, spec in ins],
        out_specs=[spec for *_, spec in outs],
        scratch_shapes=[pltpu.VMEM(shape, kind) for _, shape, kind in scratch]
        + [
            pltpu.SemaphoreType.DMA((number,)),
            pltpu.SemaphoreType.DMA((number,)),
            pltpu.SemaphoreType.DMA((11,)),
        ],
        compiler_params=pltpu.CompilerParams(
            collective_id=0, has_side_effects=True, vmem_limit_bytes=64 * 2**20
        ),
    )(*weights, starts, x, g)


def assemble(ff, *refs):
    gains, sources, results, g_gain = refs[0], refs[1:10], refs[10:16], refs[16]
    held, made, sems = refs[17:26], refs[26:30], refs[30]
    copies = [pltpu.make_async_copy(a, b, sems.at[k]) for k, (a, b) in enumerate(zip(sources, held, strict=True))]
    for c in copies:
        c.start()
    ready = made + held[7:]
    back = [pltpu.make_async_copy(a, b, sems.at[9 + k]) for k, (a, b) in enumerate(zip(ready, results, strict=True))]
    o_ga, o_up, w_gu, o_dn, o_qkv, w_qkv, o_out = held[:7]
    g_gu, g_dn, g_qkv, g_out = made
    db = w_qkv.shape[1]
    lines = gains[...].astype(F32)
    same = eye(db)

    def column(k):
        return jnp.sum(jnp.where(same, jnp.broadcast_to(lines[k : k + 1, :], (db, db)), 0.0), axis=1, keepdims=True)

    def put(k, total):
        g_gain[k : k + 1, :] = jnp.sum(jnp.where(same, jnp.broadcast_to(total, (db, db)), 0.0), axis=0, keepdims=True)

    gain = column(1)
    total = jnp.zeros((db, 1), F32)
    copies[2].wait()
    for k, ref in enumerate((o_ga, o_up)):
        copies[k].wait()
        value = jnp.concatenate([ref[s, :, :ff].astype(F32) for s in range(SUB)], axis=1)
        total = total + jnp.sum(value * w_gu[k].astype(F32), axis=1, keepdims=True)
        g_gu[k] = value * gain
    back[0].start()
    put(1, total)
    copies[3].wait()
    g_dn[...] = jnp.concatenate([o_dn[s, :, :ff].astype(F32) for s in range(SUB)], axis=1)
    back[1].start()
    gain = column(0)
    total = jnp.zeros((db, 1), F32)
    copies[4].wait()
    copies[5].wait()
    for k in range(3):
        parts = []
        for s in range(SUB):
            for h in range(2):
                start = (2 * k + h) * HP
                parts.append(o_qkv[s, :, start : start + DH].astype(F32))
        value = jnp.concatenate(parts, axis=1)
        total = total + jnp.sum(value * w_qkv[k].astype(F32), axis=1, keepdims=True)
        g_qkv[k] = value * gain
    back[2].start()
    put(0, total)
    copies[6].wait()
    parts = [o_out[s, :, h * HP : h * HP + DH].astype(F32) for s in range(SUB) for h in range(2)]
    g_out[...] = jnp.concatenate(parts, axis=1)
    back[3].start()
    for k in range(2):
        copies[7 + k].wait()
        back[4 + k].start()
    for c in back:
        c.wait()


def body(size, tokens, doc_starts, w_qkv, w_out, w_gate_up, w_down, gains, cotangent):
    batches, rows, d = tokens.shape
    db = w_qkv.shape[1]
    ff = w_gate_up.shape[2] // SUB
    ffp = -(-ff // HP) * HP
    heads = w_qkv.shape[2] // (SUB * DH)
    whole = size != 16 or db % 16 != 0
    cfg = {"D": d, "NH": size // 8, "DB": db, "FF": ff, "whole": whole}
    width = {"qkv": 3 * heads * HP, "out": heads * HP, "ga": ffp, "up": ffp, "dn": ffp}
    acts = [doc_starts, tokens.reshape(batches * rows, d), cotangent.reshape(batches * rows, d)]

    def results(out, in_grad, g_qkv, g_out, g_gu, g_dn, gain_sums):
        gain_sums = gain_sums + lax.ppermute(gain_sums, "tp", [(0, 1), (1, 0)])
        return (out.reshape(tokens.shape), in_grad.reshape(tokens.shape), g_qkv, g_out, g_gu, g_dn, gain_sums)

    if not whole:
        out, in_grad, *grads = fused(cfg, width, [w_qkv, w_out.T, w_gate_up, w_down.T, gains], *acts)
        o_qkv, o_out, o_ga, o_up, o_dn = grads
        sources = [o_ga, o_up, w_gate_up, o_dn, o_qkv, w_qkv, o_out, out, in_grad]
        made = [jax.ShapeDtypeStruct(v.shape, F32) for v in (w_gate_up, w_down.T, w_qkv, w_out.T)]
        shapes = made + [jax.ShapeDtypeStruct(v.shape, v.dtype) for v in (out, in_grad)]
        shapes.append(jax.ShapeDtypeStruct(gains.shape, F32))
        anywhere, vmem = pl.BlockSpec(memory_space=pl.ANY), pl.BlockSpec(memory_space=pltpu.VMEM)
        g_gu, g_dn, g_qkv, g_out, out, in_grad, gain_sums = pl.pallas_call(
            functools.partial(assemble, ff),
            out_shape=shapes,
            in_specs=[vmem] + [anywhere] * 9,
            out_specs=[anywhere] * 6 + [vmem],
            scratch_shapes=[pltpu.VMEM(v.shape, v.dtype) for v in sources + made] + [pltpu.SemaphoreType.DMA((15,))],
            compiler_params=pltpu.CompilerParams(vmem_limit_bytes=63 * 2**20),
        )(gains, *sources)
        return results(out, in_grad, g_qkv, g_out.T, g_gu, g_dn.T, gain_sums)

    gain = gains.astype(F32)
    sh_qkv = (w_qkv.astype(F32) * gain[0][None, :, None]).astype(BF).reshape(3, db, SUB, heads, DH)
    sh_qkv = padded(sh_qkv, HP).transpose(2, 1, 0, 3, 4).reshape(SUB, db, 3 * heads * HP)
    sh_out = w_out.T.reshape(db, SUB, heads, DH)
    sh_out = padded(sh_out, HP).transpose(1, 0, 2, 3).reshape(SUB, db, heads * HP)
    scaled = (w_gate_up.astype(F32) * gain[1][None, :, None]).astype(BF).reshape(2, db, SUB, ff)
    sh_ga, sh_up = [padded(scaled[k], ffp).transpose(1, 0, 2) for k in range(2)]
    sh_dn = padded(w_down.T.reshape(db, SUB, ff), ffp).transpose(1, 0, 2)
    f = lax.axis_index("fsdp")
    s = (f // 4) % 2 * 2 + f % 2
    everyone = [lax.all_gather(v, "fsdp", axis=1, tiled=True) for v in (sh_qkv, sh_out, sh_ga, sh_up, sh_dn)]
    shares = [lax.dynamic_index_in_dim(v, s, 0, keepdims=False) for v in everyone]
    out, in_grad, *grads = fused(cfg, width, shares, *acts)
    mine = (jnp.arange(SUB) == s)[:, None, None]
    g_qkv, g_out, g_ga, g_up, g_dn = [
        lax.psum_scatter(jnp.where(mine, v[None], 0).astype(BF), "fsdp", scatter_dimension=1, tiled=True).astype(F32)
        for v in grads
    ]
    g_qkv = g_qkv.reshape(SUB, db, 3, heads, HP)[..., :DH].transpose(2, 1, 0, 3, 4).reshape(w_qkv.shape)
    g_out = g_out.reshape(SUB, db, heads, HP)[..., :DH].transpose(0, 2, 3, 1).reshape(w_out.shape)
    g_gu = jnp.stack([v[..., :ff].transpose(1, 0, 2).reshape(w_gate_up.shape[1:]) for v in (g_ga, g_up)])
    g_dn = g_dn[..., :ff].transpose(0, 2, 1).reshape(w_down.shape)
    gain_sums = jnp.stack(
        [
            jnp.sum(g_qkv * w_qkv.astype(F32), axis=(0, 2)),
            jnp.sum(g_gu * w_gate_up.astype(F32), axis=(0, 2)),
        ]
    )
    g_qkv, g_gu = g_qkv * gain[0][None, :, None], g_gu * gain[1][None, :, None]
    return results(out, in_grad, g_qkv, g_out, g_gu, g_dn, gain_sums)


def solution(mesh):
    in_specs = (
        P(None, ("fsdp", "tp"), None),
        P(None, "fsdp"),
        P(None, "fsdp", "tp"),
        P("tp", "fsdp"),
        P(None, "fsdp", "tp"),
        P("tp", "fsdp"),
        P(None, "fsdp"),
        P(None, ("fsdp", "tp"), None),
    )
    out_specs = (
        P(None, ("fsdp", "tp"), None),
        P(None, ("fsdp", "tp"), None),
        P(None, "fsdp", "tp"),
        P("tp", "fsdp"),
        P(None, "fsdp", "tp"),
        P("tp", "fsdp"),
        P(None, "fsdp"),
    )
    return jax.shard_map(
        functools.partial(body, mesh.shape["fsdp"]), mesh=mesh, in_specs=in_specs, out_specs=out_specs, check_vma=False
    )
```

```python
import functools

import jax
import jax.numpy as jnp
from jax import lax
from jax.experimental import pallas as pl
from jax.experimental.pallas import tpu as pltpu
from jax.sharding import PartitionSpec as P

DH = 112
HP = 128
WINDOW = 64
EPSILON = 1e-06
SUB = 4
NARROW = 1
BF = jnp.bfloat16
F32 = jnp.float32
NN = (((1,), (0,)), ((), ()))
NT = (((1,), (1,)), ((), ()))
TN = (((0,), (0,)), ((), ()))


def dot(a, b, dims):
    return lax.dot_general(a, b, dims, preferred_element_type=F32)


def flat(value):
    return value.reshape(-1, value.shape[-1])


def eye(size):
    shape = (size, size)
    return lax.broadcasted_iota(jnp.int32, shape, 0) == lax.broadcasted_iota(jnp.int32, shape, 1)


def padded(value, size):
    extra = size - value.shape[-1]
    if not extra:
        return value
    return jnp.concatenate([value, jnp.zeros(value.shape[:-1] + (extra,), value.dtype)], axis=-1)


class Conditional:
    def __init__(self, copy, sent, received, part=None, narrow=None):
        self.copy, self.sent, self.received, self.part, self.narrow = copy, sent, received, part, narrow

    def under(self, condition, k, name):
        if self.part is None:
            pl.when(condition)(getattr(self.copy, name))
            return
        thin = self.narrow[k]
        wide = jnp.logical_not(thin)
        if condition is not None:
            thin, wide = jnp.logical_and(condition, thin), jnp.logical_and(condition, wide)
        pl.when(thin)(getattr(self.part, name))
        pl.when(wide)(getattr(self.copy, name))

    def start(self):
        self.under(self.sent, 0, "start")

    def wait_send(self):
        self.under(self.sent, 0, "wait_send")

    def wait_recv(self):
        self.under(self.received, 1, "wait_recv")


class Kernel:
    def __init__(self, cfg, refs):
        self.cfg = cfg
        self.__dict__.update(refs)
        self.f = lax.axis_index("fsdp")
        self.y = lax.axis_index("tp")
        core = self.f % 2
        self.x = (self.f // 2) % 2
        self.hi = self.f // 8
        self.z = (self.f // 4) % 2
        self.is_middle = self.hi + self.z == 1
        self.is_end = self.hi + self.z != 1
        self.s = (self.f // 4) % 2 * 2 + core
        self.col = self.column_of(self.s)
        self.is_narrow = self.col == NARROW
        self.sib = self.s + 1 - 2 * core
        self.zn = (self.s + 2) % SUB
        self.diag = (self.sib + 2) % SUB
        self.yn = 1 - self.y
        self.next_hi = (self.hi + 1) % cfg["NH"]
        self.last_hi = (self.hi + cfg["NH"] - 1) % cfg["NH"]
        self.count = 0
        self.local_count = 0
        self.sends = []
        self.gathered = []
        self.given = []
        middle = cfg["D"] // 256 * 128
        self.halves = (slice(0, middle), slice(middle, cfg["D"]))

    def column_of(self, s):
        if self.cfg["whole"]:
            return s
        return (s // 2 + self.hi) % 2 * 2 + s % 2

    def index(self, hi, s, x):
        return hi * 8 + s // 2 * 4 + x * 2 + s % 2

    def mate(self, s):
        return {"fsdp": self.index(self.hi, s, self.x), "tp": self.y}

    def other(self, s):
        return {"fsdp": self.index(self.next_hi, s, self.x), "tp": self.y}

    def peer(self, hi, x):
        s = self.s if self.cfg["whole"] else jnp.where(hi == self.hi, self.s, self.zn)
        return {"fsdp": self.index(hi, s, x), "tp": self.y}

    def barrier(self):
        sem = pltpu.get_barrier_semaphore()
        partners = [self.mate(s) for s in (self.sib, self.zn, self.diag)]
        partners += [{"fsdp": self.f, "tp": self.yn}, self.peer(self.hi, 1 - self.x)]
        partners += [self.peer(self.next_hi, 1 - self.x)]
        if self.cfg["whole"]:
            partners += [self.peer(self.last_hi, 1 - self.x)]
        else:
            partners += [self.other(s) for s in (self.s, self.sib, self.zn, self.diag)]
        for partner in partners:
            pl.semaphore_signal(sem, inc=1, device_id=partner, device_id_type=pl.DeviceIdType.MESH)
        return lambda: pl.semaphore_wait(sem, len(partners))

    def remote(self, src, dst, device, sent=None, received=None, narrow=None):
        k = self.count
        self.count += 1

        def describe(src, dst):
            return pltpu.make_async_remote_copy(
                src_ref=src,
                dst_ref=dst,
                send_sem=self.send_sems.at[k],
                recv_sem=self.recv_sems.at[k],
                device_id=device,
                device_id_type=pl.DeviceIdType.MESH,
            )

        copy = describe(src, dst)
        if narrow is not None:
            part = slice(0, src.shape[1] - HP)
            copy = Conditional(copy, sent, received, describe(src.at[:, part], dst.at[:, part]), narrow)
        elif sent is not None:
            copy = Conditional(copy, sent, received)
        copy.start()
        self.sends.append(copy)
        return copy

    def narrow(self, key, sent, received):
        return (sent, received) if key in ("ga", "up", "dn") and self.cfg["uneven"] else None

    def to_sib(self, src, dst):
        return self.remote(src, dst, self.mate(self.sib))

    def to_z(self, src, dst):
        return self.remote(src, dst, self.mate(self.zn))

    def to_y(self, src, dst):
        return self.remote(src, dst, {"fsdp": self.f, "tp": self.yn})

    def to_x(self, src, dst, narrow=None):
        return self.remote(src, dst, self.peer(self.hi, 1 - self.x), narrow=narrow)

    def to_half(self, src, dst, narrow=None):
        return self.remote(src, dst, self.peer(self.next_hi, self.x), narrow=narrow)

    def local(self, src, dst):
        k = self.local_count
        self.local_count += 1
        copy = pltpu.make_async_copy(src, dst, self.local_sems.at[k])
        copy.start()
        return copy


    def rows(self, hi, z, x):
        size = 2 * self.cfg["DB"]
        return pl.ds(pl.multiple_of(((hi * 2 + z) * 2 + x) * size, 16), size)

    def share(self, ref, s):
        db = self.cfg["DB"]
        return ref.at[pl.ds(pl.multiple_of(self.index(self.hi, s, self.x) * db, 16), db), :]

    def columns_out(self, key):
        full = getattr(self, "w_" + key)
        if self.cfg["whole"]:
            return {"full": full, "own": self.local(getattr(self, "sh_" + key), full), "here": []}
        if key != "qkv":
            self.prepare(key)
        shares = functools.partial(self.prepared, key)
        mine = self.share(full, self.s)
        here = []
        for s in (self.zn, self.diag, self.sib):
            col = self.column_of(s)
            narrow = self.narrow(key, col == NARROW, self.is_narrow)
            here.append(self.remote(shares(col), mine, self.mate(s), narrow=narrow))
        self.given += here
        same = self.narrow(key, self.is_narrow, self.is_narrow)
        own = self.local(shares(self.col), mine)
        return {"key": key, "full": full, "shares": shares, "own": own, "here": here, "narrow": same}

    def prepared(self, key, s):
        db = self.cfg["DB"]
        rows = pl.ds(pl.multiple_of(s % 2 * db, 16), db)
        return getattr(self, "slots_" + key).at[s // 2, rows, :]

    def gain_column(self, k):
        db = self.cfg["DB"]
        line = jnp.broadcast_to(self.gains[...].astype(F32)[k : k + 1, :], (db, db))
        return jnp.sum(jnp.where(eye(db), line, 0.0), axis=1, keepdims=True)

    def prepare(self, key):
        db = self.cfg["DB"]
        slots = getattr(self, "slots_" + key)
        if key in ("qkv", "ga", "up"):
            gain = self.gain_column(0 if key == "qkv" else 1)
        for s in range(SUB):
            if key == "qkv":
                blocks = [(k, 2 * s + h) for k in range(3) for h in range(2)]
                parts = [self.raw_qkv[k, :, n * DH : (n + 1) * DH].astype(F32) * gain for k, n in blocks]
            elif key == "out":
                parts = [self.raw_out[:, n * DH : (n + 1) * DH].astype(F32) for n in (2 * s, 2 * s + 1)]
            elif key == "dn":
                parts = [self.raw_dn[:, self.cfg["spans"][s]].astype(F32)]
            else:
                parts = [self.raw_gu[int(key == "up"), :, self.cfg["spans"][s]].astype(F32) * gain]
            value = jnp.concatenate([padded(part, slots.shape[2] // len(parts)) for part in parts], axis=1)
            slots[s // 2, s % 2 * db : (s % 2 + 1) * db, :] = value.astype(BF)

    def columns_far(self, g):
        if self.cfg["whole"]:
            return
        mine = self.share(g["full"], self.s)
        g["far"], g["middle"] = [], []
        for s, col in ((self.zn, self.col), (self.diag, self.column_of(self.sib))):
            narrow = self.narrow(g["key"], col == NARROW, self.is_narrow)
            g["far"].append(self.remote(g["shares"](col), mine, self.other(s), narrow=narrow))
        for s, col in ((self.s, self.column_of(self.zn)), (self.sib, self.column_of(self.diag))):
            narrow = self.narrow(g["key"], col == NARROW, self.is_narrow)
            device = self.other(s)
            g["middle"].append(
                self.remote(g["shares"](col), mine, device, self.is_middle, self.is_end, narrow=narrow)
            )
        self.given += g["far"] + g["middle"]

    def spread(self, g):
        for c in g["here"]:
            c.wait_recv()
        g["own"].wait()
        if self.cfg["whole"]:
            return
        part = g["full"].at[self.rows(self.hi, 1 - self.z, self.x), :]
        device = self.other(self.zn)
        g["passed"] = self.remote(part, part, device, self.is_middle, self.is_middle, narrow=g["narrow"])
        parts = [g["full"].at[self.rows(self.hi, z, self.x), :] for z in range(2)]
        g["near"] = [self.to_x(part, part, g["narrow"]) for part in parts]
        self.gathered += [g["passed"]] + g["near"]

    def onward(self, g, z):
        part = g["full"].at[self.rows(self.next_hi, z, self.x), :]
        copy = self.to_x(part, part, g["narrow"])
        g["near"].append(copy)
        self.gathered.append(copy)

    def spread_same(self, g):
        if self.cfg["whole"]:
            return
        for c in g["far"]:
            c.wait_recv()
        self.onward(g, 1 - self.z)

    def spread_rest(self, g):
        if self.cfg["whole"]:
            return
        for c in g["middle"] + [g["passed"]]:
            c.wait_recv()
        self.onward(g, self.z)

    def spread_done(self, g):
        if not self.cfg["whole"]:
            for c in g["near"]:
                c.wait_recv()

    def columns_back(self, full, result, key=""):
        if self.cfg["whole"]:
            return self.local(full, result).wait
        copies = []
        for s in (self.zn, self.diag, self.sib):
            narrow = self.narrow(key, self.is_narrow, self.column_of(s) == NARROW)
            copies.append(self.remote(self.share(full, s), result.at[self.col], self.mate(s), narrow=narrow))
        own = self.local(self.share(full, self.s), result.at[self.col])

        def wait():
            for c in copies:
                c.wait_recv()
            own.wait()

        return wait

    def add_rows(self, grad, rows, parts):
        size, tile = 2 * self.cfg["DB"], 2 * self.cfg["DB"]
        tile = next(t for t in (112, 32, 16) if size % t == 0)
        for i in range(size // tile):
            place = pl.ds(pl.multiple_of(rows.start + i * tile, 16), tile)
            total = grad[place, :].astype(F32)
            for part in parts:
                total = total + part[i * tile : (i + 1) * tile, :].astype(F32)
            grad[place, :] = total.astype(BF)

    def collect(self, grad, slots, key=""):
        if self.cfg["whole"]:
            return None
        near = []
        narrow = self.narrow(key, self.is_narrow, self.is_narrow)
        for k, hi in enumerate((self.next_hi, self.hi)):
            for z in range(2):
                near.append(self.to_x(grad.at[self.rows(hi, z, 1 - self.x), :], slots.at[2 * k + z], narrow))
        return {"grad": grad, "slots": slots, "near": near, "far": [], "narrow": narrow}

    def collect_on(self, g, planes=(0, 1)):
        if g is None:
            return
        for z in planes:
            g["near"][z].wait_recv()
            rows = self.rows(self.next_hi, z, self.x)
            self.add_rows(g["grad"], rows, [g["slots"].at[z]])
            g["far"].append(self.to_half(g["grad"].at[rows, :], g["slots"].at[4 + z], g["narrow"]))

    def collect_done(self, g):
        if g is None:
            return
        for z in range(2):
            g["near"][2 + z].wait_recv()
            g["far"][z].wait_recv()
            rows = self.rows(self.hi, z, self.x)
            self.add_rows(g["grad"], rows, [g["slots"].at[2 + z], g["slots"].at[4 + z]])


    def rim_out(self, ends, slots):
        after = self.peer((self.hi + self.x) % self.cfg["NH"], 1 - self.x)
        return [self.to_x(ends[0], slots(self.x)), self.remote(ends[1], slots(1 - self.x), after)]

    def rim_home(self, slots, ends):
        before = self.peer((self.hi + self.cfg["NH"] - 1 + self.x) % self.cfg["NH"], 1 - self.x)
        return [self.to_x(slots(1 - self.x), ends[0]), self.remote(slots(self.x), ends[1], before)]


    def gather_start(self, buf):
        own = buf.at[self.s, self.y]
        halves = [own.at[:, h] for h in self.halves]
        z = [self.to_z(half, half) for half in halves]
        return {"z": z, "y": self.to_y(own, own), "own": self.to_sib(own, own), "buf": buf}

    def gather_relay(self, g):
        buf = g["buf"]
        g["d"], g["fz"] = [], []
        for c, h in zip(g["z"], self.halves, strict=True):
            c.wait_recv()
            part = buf.at[self.zn, self.y, :, h]
            g["d"].append(self.to_y(part, part))
            g["fz"].append(self.to_sib(part, part))
        g["y"].wait_recv()
        part = buf.at[self.s, self.yn]
        g["fy"] = self.to_sib(part, part)
        g["own"].wait_recv()

    def gather_near(self, g):
        g["fy"].wait_recv()

    def gather_finish(self, g, near=False):
        g["fd"] = []
        for c, h in zip(g["d"], self.halves, strict=True):
            c.wait_recv()
            part = g["buf"].at[self.zn, self.yn, :, h]
            g["fd"].append(self.to_sib(part, part))
        for c in ([] if near else [g["fy"]]) + g["fz"] + g["fd"]:
            c.wait_recv()
        g["copies"] = [g["own"], g["y"], g["fy"]] + g["z"] + g["d"] + g["fz"] + g["fd"]

    def scatter_pair(self, st, partial):
        sc, rc = st["sc"], st["rc"]
        copies = []
        for k, pair in enumerate((self.diag, self.sib)):
            sc[k] = partial(pair).astype(BF).reshape(sc.shape[1:])
            copies.append(self.to_sib(sc.at[k], rc.at[k]))
        return {"pair": copies, "st": st}

    def scatter_send(self, g, partial):
        st = g["st"]
        so, rc = st["so"], st["rc"]
        value = partial(self.zn)
        g["pair"][0].wait_recv()
        so[0] = (value + flat(rc[0].astype(F32))).astype(BF).reshape(so.shape[1:])
        g["d"] = [self.to_y(so.at[0, self.yn, :, h], st["rd"].at[:, h]) for h in self.halves]
        value = partial(self.s)
        g["pair"][1].wait_recv()
        so[1] = (value + flat(rc[1].astype(F32))).astype(BF).reshape(so.shape[1:])
        g["y"] = self.to_y(so.at[1, self.yn], st["ry"])

    def scatter_relay(self, g):
        st = g["st"]
        so = st["so"]
        g["z"] = []
        for c, h in zip(g["d"], self.halves, strict=True):
            c.wait_recv()
            so[0, self.y, :, h] = (so[0, self.y, :, h].astype(F32) + st["rd"][:, h].astype(F32)).astype(BF)
            g["z"].append(self.to_z(so.at[0, self.y, :, h], st["rz"].at[:, h]))

    def scatter_finish(self, g):
        st = g["st"]
        for c in g["z"] + [g["y"]]:
            c.wait_recv()
        total = st["so"][1, self.y].astype(F32) + st["rz"][...].astype(F32) + st["ry"][...].astype(F32)
        self.settle(g["pair"] + g["d"] + g["z"] + [g["y"]])
        return total


    def place(self, s):
        return 1 + 2 * s + s // 2

    def project(self, w):
        def step(i, _):
            rows = flat(self.u1[i])
            out = dot(rows, w[...], NN).astype(BF)
            self.qkv[pl.ds(self.place(i), 2)] = out.reshape(2, 2 * WINDOW, out.shape[1])
            return 0

        lax.fori_loop(0, SUB, step, 0)

    def masks(self, s):
        at = 1 + s + s // 2
        before, own = self.starts[at - 1], self.starts[at]
        lane = lax.broadcasted_iota(jnp.int32, before.shape, 1)
        even = jnp.where(lane < WINDOW, pltpu.roll(before, WINDOW, 1), pltpu.roll(own, WINDOW, 1))
        shape = (WINDOW, 2 * WINDOW)
        i = lax.broadcasted_iota(jnp.int32, shape, 0)
        j = lax.broadcasted_iota(jnp.int32, shape, 1)
        square = (2 * WINDOW, 2 * WINDOW)
        later = lax.broadcasted_iota(jnp.int32, square, 0) > lax.broadcasted_iota(jnp.int32, square, 1)
        later = later.astype(F32).astype(BF)
        band = (j <= i + WINDOW) & (j > i)
        result = []
        for rows in (even, own):
            per_batch = []
            for batch in range(2):
                line = jnp.broadcast_to(rows[batch : batch + 1, :], shape)
                line = jnp.where(j <= i + WINDOW, line, 0.0).astype(BF)
                between = dot(line, later, NN)
                per_batch.append(band & (between < 0.5))
            result.append(per_batch)
        return result

    def tile(self, index, batch, part, head):
        cols = slice(part * 2 * HP + head * HP, part * 2 * HP + (head + 1) * HP)
        return self.qkv[index, batch * WINDOW : (batch + 1) * WINDOW, cols]

    def attend(self, first):
        def step(run, _):
            s = 2 * run + first
            allowed = self.masks(s)
            for half in range(2):
                p = self.place(s) + half
                for batch in range(2):
                    for head in range(2):
                        q = self.tile(p, batch, 0, head)
                        k = jnp.concatenate([self.tile(p - 1, batch, 1, head), self.tile(p, batch, 1, head)], axis=0)
                        v = jnp.concatenate([self.tile(p - 1, batch, 2, head), self.tile(p, batch, 2, head)], axis=0)
                        scores = dot(q, k, NT) * DH ** (-0.5)
                        scores = jnp.where(allowed[half][batch], scores, -1e30)
                        top = jnp.max(scores, axis=-1, keepdims=True)
                        weights = jnp.exp(scores - top)
                        probs = weights / jnp.sum(weights, axis=-1, keepdims=True)
                        self.probs[2 * s + half, 2 * batch + head] = probs
                        out = dot(probs.astype(BF), v, NN).astype(BF)
                        self.heads[s, half, batch * WINDOW : (batch + 1) * WINDOW, head * HP : (head + 1) * HP] = out
            return 0

        lax.fori_loop(0, 2, step, 0)

    def attend_back(self, s):
        run = s // 2
        for half in range(2):
            p = self.place(s) + half
            for batch in range(2):
                rows = slice(batch * WINDOW, (batch + 1) * WINDOW)
                for head in range(2):
                    cols = slice(head * HP, (head + 1) * HP)
                    q = self.tile(p, batch, 0, head)
                    k = jnp.concatenate([self.tile(p - 1, batch, 1, head), self.tile(p, batch, 1, head)], axis=0)
                    v = jnp.concatenate([self.tile(p - 1, batch, 2, head), self.tile(p, batch, 2, head)], axis=0)
                    probs = self.probs[2 * s + half, 2 * batch + head]
                    d_out = self.d_heads[s, half, rows, cols]
                    d_probs = dot(d_out, v, NT)
                    inner = jnp.sum(probs * d_probs, axis=-1, keepdims=True)
                    d_scores = (probs * (d_probs - inner)).astype(BF)
                    d_q = dot(d_scores, k, NN) * DH ** (-0.5)
                    d_k = dot(d_scores, q, TN) * DH ** (-0.5)
                    d_v = dot(probs.astype(BF), d_out, TN)
                    self.qkv[p, rows, head * HP : (head + 1) * HP] = d_q.astype(BF)
                    for part, grad in ((1, d_k), (2, d_v)):
                        slot = slice((part - 1) * 2 * HP + head * HP, (part - 1) * 2 * HP + (head + 1) * HP)
                        place = slice(part * 2 * HP + head * HP, part * 2 * HP + (head + 1) * HP)
                        done = self.carry[run, rows, slot] + grad[:WINDOW]
                        self.qkv[p - 1, rows, place] = done.astype(BF)
                        self.carry[run, rows, slot] = grad[WINDOW:]

    def grad_into(self, target, left, right):
        width = 256

        def step(m, _):
            cols = pl.ds(pl.multiple_of(m * width, width), width)
            parts = right()
            each = SUB // len(parts)
            total = 0.0
            for k, part in enumerate(parts):
                total = total + dot(flat(left[k * each : (k + 1) * each, :, :, cols]), part, TN)
            target[cols, :] = total.astype(BF)
            return 0

        lax.fori_loop(0, self.cfg["D"] // width, step, 0)

    def feed_forward(self, plane):
        ff = self.w_dn.shape[1]

        def step(k, _):
            i = 2 * plane + k
            rows = flat(self.u2[i])
            gate = dot(rows, self.w_ga[...], NN)
            upward = dot(rows, self.w_up[...], NN)
            d_hidden = dot(flat(self.g[i]), self.w_dn[...], NN)
            sig = jax.nn.sigmoid(gate)
            silu = gate * sig
            shape = (2, 2 * WINDOW, ff)
            self.hidden[i] = (silu * upward).astype(BF).reshape(shape)
            d_gate = d_hidden * upward * sig * (1.0 + gate * (1.0 - sig))
            self.d_ga[i] = d_gate.astype(BF).reshape(shape)
            self.d_up[i] = (d_hidden * silu).astype(BF).reshape(shape)
            return 0

        lax.fori_loop(0, 2, step, 0)

    def run(self):
        cfg = self.cfg
        me = (self.s, self.y)
        norm = lambda v: lax.rsqrt(jnp.mean(v * v, axis=-1, keepdims=True) + EPSILON)
        whole = lambda ref: [flat(ref[...])]

        everyone_here = self.barrier()
        if cfg["uneven"]:

            @pl.when(self.is_narrow)
            def _():
                for w in (self.w_ga, self.w_up, self.w_dn):
                    w[:, w.shape[1] - HP :] = jnp.zeros((w.shape[0], HP), BF)

        line = 1 + self.s + self.s // 2
        own_starts = self.doc_starts[...].astype(F32)
        fill = jnp.zeros((self.starts.shape[1] - own_starts.shape[0], own_starts.shape[1]), F32)
        self.starts[line] = jnp.concatenate([own_starts, fill], axis=0)
        own_line = self.starts.at[line]
        x = self.x_in[...].astype(F32)
        self.u1[me] = (x * norm(x)).astype(BF)
        if not cfg["whole"]:
            self.prepare("qkv")
        everyone_here()
        start_copies = [self.remote(own_line, own_line, self.mate(s)) for s in (self.sib, self.zn, self.diag)]
        qkv = self.columns_out("qkv")
        gather_one = self.gather_start(self.u1)
        self.columns_far(qkv)
        self.spread(qkv)
        for c in start_copies:
            c.wait_recv()
        rim_starts = self.rim_out([self.starts.at[2], self.starts.at[5]], lambda run: self.starts.at[3 * run])
        self.spread_same(qkv)
        self.gather_relay(gather_one)
        self.spread_rest(qkv)
        out = self.columns_out("out")
        self.columns_far(out)
        ga = self.columns_out("ga")
        self.gather_finish(gather_one)
        self.spread_done(qkv)

        self.project(self.w_qkv)
        rims = self.rim_out(
            [self.qkv.at[4, :, slice(2 * HP, 6 * HP)], self.qkv.at[9, :, slice(2 * HP, 6 * HP)]],
            lambda run: self.qkv.at[5 * run, :, slice(2 * HP, 6 * HP)],
        )
        self.spread(out)
        self.columns_far(ga)
        up = self.columns_out("up")
        self.attend(1)
        self.spread_same(out)
        self.spread_rest(out)
        for c in rim_starts + rims:
            c.wait_recv()
        self.spread(ga)
        self.columns_far(up)
        self.attend(0)
        self.spread(up)
        dn = self.columns_out("dn")
        self.spread_same(ga)
        self.spread_done(out)

        partial = lambda pair: dot(flat(self.heads[pair]), self.w_out[...], NT)
        stage = {n: getattr(self, n) for n in ("sc", "rc", "so", "rd", "rz", "ry")}
        scatter = self.scatter_pair(stage, partial)
        self.scatter_send(scatter, partial)
        self.scatter_relay(scatter)
        self.spread_rest(ga)
        self.g[me] = self.g_in[...]
        gather_g = self.gather_start(self.g)
        self.columns_far(dn)
        self.spread(dn)
        self.spread_same(up)
        self.resid[...] = self.x_in[...].astype(F32) + self.scatter_finish(scatter)
        resid = self.resid[...]
        self.u2[me] = (resid * norm(resid)).astype(BF)
        gather_two = self.gather_start(self.u2)
        self.spread_rest(up)
        self.spread_same(dn)
        self.gather_relay(gather_g)
        self.settle(self.given)
        self.spread_rest(dn)
        self.gather_relay(gather_two)
        self.gather_finish(gather_g)
        for g in (ga, up, dn):
            self.spread_done(g)
        self.gather_near(gather_two)
        self.feed_forward(self.s // 2)
        self.gather_finish(gather_two, near=True)
        self.feed_forward(1 - self.s // 2)
        self.grad_into(self.g_dn, self.g, lambda: whole(self.hidden))
        sum_dn = self.collect(self.g_dn, self.slots_dn, "dn")
        partial = lambda pair: dot(flat(self.d_ga[pair]), self.w_ga[...], NT) + dot(
            flat(self.d_up[pair]), self.w_up[...], NT
        )
        scatter = self.scatter_pair(stage, partial)
        self.scatter_send(scatter, partial)
        self.collect_on(sum_dn, (0,))
        self.settle(self.gathered)
        self.grad_into(self.w_ga, self.u2, lambda: whole(self.d_ga))
        sum_ga = self.collect(self.w_ga, self.slots_ga, "ga")
        self.scatter_relay(scatter)
        self.collect_on(sum_dn, (1,))
        self.grad_into(self.w_up, self.u2, lambda: whole(self.d_up))
        sum_up = self.collect(self.w_up, self.slots_up, "up")
        d_unit = self.scatter_finish(scatter)
        resid = self.resid[...]
        scale = norm(resid)
        unit = resid * scale
        inner = jnp.mean(d_unit * unit, axis=-1, keepdims=True)
        self.in_grad[...] = self.g_in[...].astype(F32) + scale * (d_unit - unit * inner)
        self.d_r[me] = self.in_grad[...].astype(BF)
        self.settle(gather_g["copies"] + gather_two["copies"] + rims)
        gather_d = self.gather_start(self.d_r)
        self.collect_on(sum_ga, (0,))
        self.gather_relay(gather_d)
        self.collect_on(sum_ga, (1,))

        view = {
            "sc": self.u2.at[0:2],
            "so": self.u2.at[2:4],
            "rc": self.g.at[0:2],
            "rd": self.g.at[2, 0],
            "rz": self.g.at[2, 1],
            "ry": self.g.at[3, 0],
        }
        partial = lambda pair: dot(flat(self.hidden[pair]), self.w_dn[...], NT)
        mlp = self.scatter_pair(view, partial)
        self.scatter_send(mlp, partial)
        self.gather_finish(gather_d)

        d_heads = self.d_heads = self.d_ga.at[:, :, :, slice(0, 2 * HP)]

        def heads_back(i, _):
            value = dot(flat(self.d_r[i]), self.w_out[...], NN).astype(BF)
            d_heads[i] = value.reshape(2, 2 * WINDOW, 2 * HP)
            return 0

        lax.fori_loop(0, SUB, heads_back, 0)
        self.collect_done(sum_dn)
        backs = [self.columns_back(self.g_dn, self.o_dn, "dn")]

        self.carry[...] = jnp.zeros_like(self.carry)

        def first(run, _):
            self.attend_back(2 * run)
            return 0

        def second(run, _):
            self.attend_back(2 * run + 1)
            return 0

        lax.fori_loop(0, 2, first, 0)
        rim_back = self.rim_home(
            lambda run: self.qkv.at[5 * run, :, slice(2 * HP, 6 * HP)], [self.rim.at[0], self.rim.at[1]]
        )
        self.scatter_relay(mlp)
        self.collect_on(sum_up, (0,))
        lax.fori_loop(0, 2, second, 0)
        of_q, of_kv = slice(0, 2 * HP), slice(2 * HP, 6 * HP)
        g_q, g_kv = self.g_qkv.at[:, of_q], self.g_qkv.at[:, of_kv]
        self.grad_into(g_q, self.u1, lambda: [flat(self.qkv[1:5, :, of_q]), flat(self.qkv[6:10, :, of_q])])
        sum_q = self.collect(g_q, self.slots_qkv.at[:, :, of_q])
        self.collect_on(sum_up, (1,))
        self.collect_done(sum_ga)
        backs.append(self.columns_back(self.w_ga, self.o_ga, "ga"))
        for c in rim_back:
            c.wait_recv()
        for run in range(2):
            done = self.carry[run] + self.rim[run].astype(F32)
            self.qkv[5 * run + 4, :, 2 * HP :] = done.astype(BF)

        self.grad_into(g_kv, self.u1, lambda: [flat(self.qkv[1:5, :, of_kv]), flat(self.qkv[6:10, :, of_kv])])
        sum_kv = self.collect(g_kv, self.slots_qkv.at[:, :, of_kv])
        self.grad_into(self.w_out, self.d_r, lambda: whole(self.heads))
        sum_out = self.collect(self.w_out, self.slots_out)
        self.collect_on(sum_q)
        partial = lambda pair: dot(flat(self.qkv[pl.ds(self.place(pair), 2)]), self.w_qkv[...], NT)
        scatter = self.scatter_pair(stage, partial)
        self.scatter_send(scatter, partial)
        self.collect_on(sum_kv, (0,))
        self.scatter_relay(scatter)
        self.collect_on(sum_kv, (1,))
        self.collect_done(sum_up)
        backs.append(self.columns_back(self.w_up, self.o_up, "up"))
        self.out[...] = (self.resid[...] + self.scatter_finish(mlp)).astype(BF)
        back_to = lambda span: self.o_qkv.at[:, span] if cfg["whole"] else self.o_qkv.at[:, :, span]
        self.collect_done(sum_q)
        backs.append(self.columns_back(g_q, back_to(of_q)))
        self.collect_on(sum_out)
        self.collect_done(sum_kv)
        backs.append(self.columns_back(g_kv, back_to(of_kv)))
        self.collect_done(sum_out)
        backs.append(self.columns_back(self.w_out, self.o_out))
        d_unit = self.scatter_finish(scatter)
        x = self.x_in[...].astype(F32)
        scale = norm(x)
        unit = x * scale
        inner = jnp.mean(d_unit * unit, axis=-1, keepdims=True)
        self.in_grad[...] += scale * (d_unit - unit * inner)
        for wait in backs:
            wait()
        self.settle()

    def settle(self, copies=None):
        for c in self.sends:
            if copies is None or any(c is other for other in copies):
                c.wait_send()
        if copies is None:
            self.sends = []
        else:
            self.sends = [c for c in self.sends if not any(c is other for other in copies)]


def fused(cfg, width, weights, starts, x, g):
    d, db = cfg["D"], cfg["DB"]
    rows = 2 * WINDOW
    anywhere = pl.BlockSpec(memory_space=pl.ANY)
    vmem = pl.BlockSpec(memory_space=pltpu.VMEM)
    keys = ("qkv", "out", "ga", "up", "dn")
    result = (d,) if cfg["whole"] else (SUB, db)
    outs = [("out", (rows, d), BF, vmem), ("in_grad", (rows, d), F32, vmem)]
    outs += [("o_" + key, result + (width[key],), BF, anywhere) for key in keys]
    if cfg["whole"]:
        ins = [("sh_" + key, anywhere) for key in keys]
    else:
        ins = [(name, vmem) for name in ("raw_qkv", "raw_out", "raw_gu", "raw_dn", "gains")]
    ins += [(name, vmem) for name in ("doc_starts", "x_in", "g_in")]
    plane = (SUB, 2, rows)
    scratch = [("w_" + key, (d, width[key]), BF) for key in keys]
    scratch += [("g_" + key, (d, width[key]), BF) for key in ("qkv", "dn")]
    slot = 16 if cfg["whole"] else 2 * db
    scratch += [("slots_" + key, (6, slot, width[key]), BF) for key in keys]
    scratch += [(name, plane + (d,), BF) for name in ("u1", "u2", "g", "d_r")]
    scratch += [(name, plane + (width["out"],), BF) for name in ("heads",)]
    scratch += [(name, plane + (width["dn"],), BF) for name in ("hidden", "d_ga", "d_up")]
    scratch += [(name, (2, 2, rows, d), BF) for name in ("sc", "rc", "so")]
    scratch += [
        ("starts", (SUB + 2, 8, rows), F32),
        ("qkv", (2 * SUB + 2, rows, width["qkv"]), BF),
        ("probs", (2 * SUB, 4, WINDOW, 2 * WINDOW), F32),
        ("carry", (2, rows, 4 * HP), F32),
        ("rim", (2, rows, 4 * HP), BF),
        ("resid", (rows, d), F32),
        ("rd", (rows, d), BF),
        ("rz", (rows, d), BF),
        ("ry", (rows, d), BF),
    ]
    number = 220
    names = [n for n, _ in ins] + [n for n, *_ in outs] + [n for n, *_ in scratch]
    names += ["send_sems", "recv_sems", "local_sems"]

    def kernel(*refs):
        Kernel(cfg, dict(zip(names, refs, strict=True))).run()

    return pl.pallas_call(
        kernel,
        out_shape=[jax.ShapeDtypeStruct(shape, kind) for _, shape, kind, _ in outs],
        in_specs=[spec for _, spec in ins],
        out_specs=[spec for *_, spec in outs],
        scratch_shapes=[pltpu.VMEM(shape, kind) for _, shape, kind in scratch]
        + [
            pltpu.SemaphoreType.DMA((number,)),
            pltpu.SemaphoreType.DMA((number,)),
            pltpu.SemaphoreType.DMA((11,)),
        ],
        compiler_params=pltpu.CompilerParams(
            collective_id=0, has_side_effects=True, vmem_limit_bytes=64 * 2**20
        ),
    )(*weights, starts, x, g)


def assemble(spans, *refs):
    gains, sources, results, g_gain = refs[0], refs[1:10], refs[10:16], refs[16]
    held, made, sems = refs[17:26], refs[26:30], refs[30]
    copies = [pltpu.make_async_copy(a, b, sems.at[k]) for k, (a, b) in enumerate(zip(sources, held, strict=True))]
    for c in copies:
        c.start()
    ready = made + held[7:]
    back = [pltpu.make_async_copy(a, b, sems.at[9 + k]) for k, (a, b) in enumerate(zip(ready, results, strict=True))]
    o_ga, o_up, w_gu, o_dn, o_qkv, w_qkv, o_out = held[:7]
    g_gu, g_dn, g_qkv, g_out = made
    db = w_qkv.shape[1]
    lines = gains[...].astype(F32)
    same = eye(db)

    def column(k):
        return jnp.sum(jnp.where(same, jnp.broadcast_to(lines[k : k + 1, :], (db, db)), 0.0), axis=1, keepdims=True)

    def put(k, total):
        g_gain[k : k + 1, :] = jnp.sum(jnp.where(same, jnp.broadcast_to(total, (db, db)), 0.0), axis=0, keepdims=True)

    gain = column(1)
    total = jnp.zeros((db, 1), F32)
    copies[2].wait()
    for k, ref in enumerate((o_ga, o_up)):
        copies[k].wait()
        value = jnp.concatenate([ref[s, :, : p.stop - p.start].astype(F32) for s, p in enumerate(spans)], axis=1)
        total = total + jnp.sum(value * w_gu[k].astype(F32), axis=1, keepdims=True)
        g_gu[k] = value * gain
    back[0].start()
    put(1, total)
    copies[3].wait()
    g_dn[...] = jnp.concatenate([o_dn[s, :, : p.stop - p.start].astype(F32) for s, p in enumerate(spans)], axis=1)
    back[1].start()
    gain = column(0)
    total = jnp.zeros((db, 1), F32)
    copies[4].wait()
    copies[5].wait()
    for k in range(3):
        parts = []
        for s in range(SUB):
            for h in range(2):
                start = (2 * k + h) * HP
                parts.append(o_qkv[s, :, start : start + DH].astype(F32))
        value = jnp.concatenate(parts, axis=1)
        total = total + jnp.sum(value * w_qkv[k].astype(F32), axis=1, keepdims=True)
        g_qkv[k] = value * gain
    back[2].start()
    put(0, total)
    copies[6].wait()
    parts = [o_out[s, :, h * HP : h * HP + DH].astype(F32) for s in range(SUB) for h in range(2)]
    g_out[...] = jnp.concatenate(parts, axis=1)
    back[3].start()
    for k in range(2):
        copies[7 + k].wait()
        back[4 + k].start()
    for c in back:
        c.wait()


def body(size, tokens, doc_starts, w_qkv, w_out, w_gate_up, w_down, gains, cotangent):
    batches, rows, d = tokens.shape
    db = w_qkv.shape[1]
    ff = w_gate_up.shape[2] // SUB
    ffp = -(-ff // HP) * HP
    heads = w_qkv.shape[2] // (SUB * DH)
    whole = size != 16 or db % 16 != 0
    uneven = not whole and w_gate_up.shape[2] == SUB * ffp - HP
    sizes = [ffp - HP * (uneven and s == NARROW) if uneven else ff for s in range(SUB)]
    spans = [slice(sum(sizes[:s]), sum(sizes[: s + 1])) for s in range(SUB)]
    cfg = {"D": d, "NH": size // 8, "DB": db, "spans": spans, "uneven": uneven, "whole": whole}
    width = {"qkv": 3 * heads * HP, "out": heads * HP, "ga": ffp, "up": ffp, "dn": ffp}
    acts = [doc_starts, tokens.reshape(batches * rows, d), cotangent.reshape(batches * rows, d)]

    def results(out, in_grad, g_qkv, g_out, g_gu, g_dn, gain_sums):
        gain_sums = gain_sums + lax.ppermute(gain_sums, "tp", [(0, 1), (1, 0)])
        return (out.reshape(tokens.shape), in_grad.reshape(tokens.shape), g_qkv, g_out, g_gu, g_dn, gain_sums)

    if not whole:
        out, in_grad, *grads = fused(cfg, width, [w_qkv, w_out.T, w_gate_up, w_down.T, gains], *acts)
        o_qkv, o_out, o_ga, o_up, o_dn = grads
        sources = [o_ga, o_up, w_gate_up, o_dn, o_qkv, w_qkv, o_out, out, in_grad]
        made = [jax.ShapeDtypeStruct(v.shape, F32) for v in (w_gate_up, w_down.T, w_qkv, w_out.T)]
        shapes = made + [jax.ShapeDtypeStruct(v.shape, v.dtype) for v in (out, in_grad)]
        shapes.append(jax.ShapeDtypeStruct(gains.shape, F32))
        anywhere, vmem = pl.BlockSpec(memory_space=pl.ANY), pl.BlockSpec(memory_space=pltpu.VMEM)
        g_gu, g_dn, g_qkv, g_out, out, in_grad, gain_sums = pl.pallas_call(
            functools.partial(assemble, spans),
            out_shape=shapes,
            in_specs=[vmem] + [anywhere] * 9,
            out_specs=[anywhere] * 6 + [vmem],
            scratch_shapes=[pltpu.VMEM(v.shape, v.dtype) for v in sources + made] + [pltpu.SemaphoreType.DMA((15,))],
            compiler_params=pltpu.CompilerParams(vmem_limit_bytes=63 * 2**20),
        )(gains, *sources)
        return results(out, in_grad, g_qkv, g_out.T, g_gu, g_dn.T, gain_sums)

    gain = gains.astype(F32)
    sh_qkv = (w_qkv.astype(F32) * gain[0][None, :, None]).astype(BF).reshape(3, db, SUB, heads, DH)
    sh_qkv = padded(sh_qkv, HP).transpose(2, 1, 0, 3, 4).reshape(SUB, db, 3 * heads * HP)
    sh_out = w_out.T.reshape(db, SUB, heads, DH)
    sh_out = padded(sh_out, HP).transpose(1, 0, 2, 3).reshape(SUB, db, heads * HP)
    scaled = (w_gate_up.astype(F32) * gain[1][None, :, None]).astype(BF).reshape(2, db, SUB, ff)
    sh_ga, sh_up = [padded(scaled[k], ffp).transpose(1, 0, 2) for k in range(2)]
    sh_dn = padded(w_down.T.reshape(db, SUB, ff), ffp).transpose(1, 0, 2)
    f = lax.axis_index("fsdp")
    s = (f // 4) % 2 * 2 + f % 2
    everyone = [lax.all_gather(v, "fsdp", axis=1, tiled=True) for v in (sh_qkv, sh_out, sh_ga, sh_up, sh_dn)]
    shares = [lax.dynamic_index_in_dim(v, s, 0, keepdims=False) for v in everyone]
    out, in_grad, *grads = fused(cfg, width, shares, *acts)
    mine = (jnp.arange(SUB) == s)[:, None, None]
    g_qkv, g_out, g_ga, g_up, g_dn = [
        lax.psum_scatter(jnp.where(mine, v[None], 0).astype(BF), "fsdp", scatter_dimension=1, tiled=True).astype(F32)
        for v in grads
    ]
    g_qkv = g_qkv.reshape(SUB, db, 3, heads, HP)[..., :DH].transpose(2, 1, 0, 3, 4).reshape(w_qkv.shape)
    g_out = g_out.reshape(SUB, db, heads, HP)[..., :DH].transpose(0, 2, 3, 1).reshape(w_out.shape)
    g_gu = jnp.stack([v[..., :ff].transpose(1, 0, 2).reshape(w_gate_up.shape[1:]) for v in (g_ga, g_up)])
    g_dn = g_dn[..., :ff].transpose(0, 2, 1).reshape(w_down.shape)
    gain_sums = jnp.stack(
        [
            jnp.sum(g_qkv * w_qkv.astype(F32), axis=(0, 2)),
            jnp.sum(g_gu * w_gate_up.astype(F32), axis=(0, 2)),
        ]
    )
    g_qkv, g_gu = g_qkv * gain[0][None, :, None], g_gu * gain[1][None, :, None]
    return results(out, in_grad, g_qkv, g_out, g_gu, g_dn, gain_sums)


def solution(mesh):
    in_specs = (
        P(None, ("fsdp", "tp"), None),
        P(None, "fsdp"),
        P(None, "fsdp", "tp"),
        P("tp", "fsdp"),
        P(None, "fsdp", "tp"),
        P("tp", "fsdp"),
        P(None, "fsdp"),
        P(None, ("fsdp", "tp"), None),
    )
    out_specs = (
        P(None, ("fsdp", "tp"), None),
        P(None, ("fsdp", "tp"), None),
        P(None, "fsdp", "tp"),
        P("tp", "fsdp"),
        P(None, "fsdp", "tp"),
        P("tp", "fsdp"),
        P(None, "fsdp"),
    )
    return jax.shard_map(
        functools.partial(body, mesh.shape["fsdp"]), mesh=mesh, in_specs=in_specs, out_specs=out_specs, check_vma=False
    )
```

```python
import functools

import jax
import jax.numpy as jnp
from jax import lax
from jax.experimental import pallas as pl
from jax.experimental.pallas import tpu as pltpu
from jax.sharding import PartitionSpec as P

DH = 112
HP = 128
WINDOW = 64
EPSILON = 1e-06
SUB = 4
NARROW = 1
BF = jnp.bfloat16
F32 = jnp.float32
NN = (((1,), (0,)), ((), ()))
NT = (((1,), (1,)), ((), ()))
TN = (((0,), (0,)), ((), ()))


def dot(a, b, dims):
    return lax.dot_general(a, b, dims, preferred_element_type=F32)


def flat(value):
    return value.reshape(-1, value.shape[-1])


def eye(size):
    shape = (size, size)
    return lax.broadcasted_iota(jnp.int32, shape, 0) == lax.broadcasted_iota(jnp.int32, shape, 1)


def padded(value, size):
    extra = size - value.shape[-1]
    if not extra:
        return value
    return jnp.concatenate([value, jnp.zeros(value.shape[:-1] + (extra,), value.dtype)], axis=-1)


class Conditional:
    def __init__(self, copy, sent, received, part=None, narrow=None):
        self.copy, self.sent, self.received, self.part, self.narrow = copy, sent, received, part, narrow

    def under(self, condition, k, name):
        if self.part is None:
            pl.when(condition)(getattr(self.copy, name))
            return
        thin = self.narrow[k]
        wide = jnp.logical_not(thin)
        if condition is not None:
            thin, wide = jnp.logical_and(condition, thin), jnp.logical_and(condition, wide)
        pl.when(thin)(getattr(self.part, name))
        pl.when(wide)(getattr(self.copy, name))

    def start(self):
        self.under(self.sent, 0, "start")

    def wait_send(self):
        self.under(self.sent, 0, "wait_send")

    def wait_recv(self):
        self.under(self.received, 1, "wait_recv")


class Kernel:
    def __init__(self, cfg, refs):
        self.cfg = cfg
        self.__dict__.update(refs)
        self.f = lax.axis_index("fsdp")
        self.y = lax.axis_index("tp")
        core = self.f % 2
        self.x = (self.f // 2) % 2
        self.hi = self.f // 8
        self.z = (self.f // 4) % 2
        self.is_middle = self.hi + self.z == 1
        self.is_end = self.hi + self.z != 1
        self.s = (self.f // 4) % 2 * 2 + core
        self.col = self.column_of(self.s)
        self.is_narrow = self.col == NARROW
        self.sib = self.s + 1 - 2 * core
        self.zn = (self.s + 2) % SUB
        self.diag = (self.sib + 2) % SUB
        self.yn = 1 - self.y
        self.next_hi = (self.hi + 1) % cfg["NH"]
        self.last_hi = (self.hi + cfg["NH"] - 1) % cfg["NH"]
        self.count = 0
        self.local_count = 0
        self.sends = []
        self.gathered = []
        self.given = []
        middle = cfg["D"] // 256 * 128
        self.halves = (slice(0, middle), slice(middle, cfg["D"]))

    def column_of(self, s):
        if self.cfg["whole"]:
            return s
        return (s // 2 + self.hi) % 2 * 2 + s % 2

    def index(self, hi, s, x):
        return hi * 8 + s // 2 * 4 + x * 2 + s % 2

    def mate(self, s):
        return {"fsdp": self.index(self.hi, s, self.x), "tp": self.y}

    def other(self, s):
        return {"fsdp": self.index(self.next_hi, s, self.x), "tp": self.y}

    def peer(self, hi, x):
        s = self.s if self.cfg["whole"] else jnp.where(hi == self.hi, self.s, self.zn)
        return {"fsdp": self.index(hi, s, x), "tp": self.y}

    def barrier(self):
        sem = pltpu.get_barrier_semaphore()
        partners = [self.mate(s) for s in (self.sib, self.zn, self.diag)]
        partners += [{"fsdp": self.f, "tp": self.yn}, self.peer(self.hi, 1 - self.x)]
        partners += [self.peer(self.next_hi, 1 - self.x)]
        if self.cfg["whole"]:
            partners += [self.peer(self.last_hi, 1 - self.x)]
        else:
            partners += [self.other(s) for s in (self.s, self.sib, self.zn, self.diag)]
        for partner in partners:
            pl.semaphore_signal(sem, inc=1, device_id=partner, device_id_type=pl.DeviceIdType.MESH)
        return lambda: pl.semaphore_wait(sem, len(partners))

    def remote(self, src, dst, device, sent=None, received=None, narrow=None):
        k = self.count
        self.count += 1

        def describe(src, dst):
            return pltpu.make_async_remote_copy(
                src_ref=src,
                dst_ref=dst,
                send_sem=self.send_sems.at[k],
                recv_sem=self.recv_sems.at[k],
                device_id=device,
                device_id_type=pl.DeviceIdType.MESH,
            )

        copy = describe(src, dst)
        if narrow is not None:
            part = slice(0, src.shape[1] - HP)
            copy = Conditional(copy, sent, received, describe(src.at[:, part], dst.at[:, part]), narrow)
        elif sent is not None:
            copy = Conditional(copy, sent, received)
        copy.start()
        self.sends.append(copy)
        return copy

    def narrow(self, key, sent, received):
        return (sent, received) if key in ("ga", "up", "dn") and self.cfg["uneven"] else None

    def to_sib(self, src, dst):
        return self.remote(src, dst, self.mate(self.sib))

    def to_z(self, src, dst):
        return self.remote(src, dst, self.mate(self.zn))

    def to_y(self, src, dst):
        return self.remote(src, dst, {"fsdp": self.f, "tp": self.yn})

    def to_x(self, src, dst, narrow=None):
        return self.remote(src, dst, self.peer(self.hi, 1 - self.x), narrow=narrow)

    def to_half(self, src, dst, narrow=None):
        return self.remote(src, dst, self.peer(self.next_hi, self.x), narrow=narrow)

    def local(self, src, dst):
        k = self.local_count
        self.local_count += 1
        copy = pltpu.make_async_copy(src, dst, self.local_sems.at[k])
        copy.start()
        return copy


    def rows(self, hi, z, x):
        size = 2 * self.cfg["DB"]
        return pl.ds(pl.multiple_of(((hi * 2 + z) * 2 + x) * size, 16), size)

    def share(self, ref, s):
        db = self.cfg["DB"]
        return ref.at[pl.ds(pl.multiple_of(self.index(self.hi, s, self.x) * db, 16), db), :]

    def columns_out(self, key):
        full = getattr(self, "w_" + key)
        if self.cfg["whole"]:
            return {"full": full, "own": self.local(getattr(self, "sh_" + key), full), "here": []}
        if key != "qkv":
            self.prepare(key)
        shares = functools.partial(self.prepared, key)
        mine = self.share(full, self.s)
        here = []
        for s in (self.zn, self.diag, self.sib):
            col = self.column_of(s)
            narrow = self.narrow(key, col == NARROW, self.is_narrow)
            here.append(self.remote(shares(col), mine, self.mate(s), narrow=narrow))
        self.given += here
        same = self.narrow(key, self.is_narrow, self.is_narrow)
        own = self.local(shares(self.col), mine)
        return {"key": key, "full": full, "shares": shares, "own": own, "here": here, "narrow": same}

    def prepared(self, key, s):
        db = self.cfg["DB"]
        rows = pl.ds(pl.multiple_of(s % 2 * db, 16), db)
        return getattr(self, "slots_" + key).at[s // 2, rows, :]

    def gain_column(self, k):
        db = self.cfg["DB"]
        line = jnp.broadcast_to(self.gains[...].astype(F32)[k : k + 1, :], (db, db))
        return jnp.sum(jnp.where(eye(db), line, 0.0), axis=1, keepdims=True)

    def prepare(self, key):
        db = self.cfg["DB"]
        slots = getattr(self, "slots_" + key)
        if key in ("qkv", "ga", "up"):
            gain = self.gain_column(0 if key == "qkv" else 1)
        for s in range(SUB):
            if key == "qkv":
                blocks = [(k, 2 * s + h) for k in range(3) for h in range(2)]
                parts = [self.raw_qkv[k, :, n * DH : (n + 1) * DH].astype(F32) * gain for k, n in blocks]
            elif key == "out":
                parts = [self.raw_out[:, n * DH : (n + 1) * DH].astype(F32) for n in (2 * s, 2 * s + 1)]
            elif key == "dn":
                parts = [self.raw_dn[:, self.cfg["spans"][s]].astype(F32)]
            else:
                parts = [self.raw_gu[int(key == "up"), :, self.cfg["spans"][s]].astype(F32) * gain]
            value = jnp.concatenate([padded(part, slots.shape[2] // len(parts)) for part in parts], axis=1)
            slots[s // 2, s % 2 * db : (s % 2 + 1) * db, :] = value.astype(BF)

    def columns_far(self, g):
        if self.cfg["whole"]:
            return
        mine = self.share(g["full"], self.s)
        g["far"], g["middle"] = [], []
        for s, col in ((self.zn, self.col), (self.diag, self.column_of(self.sib))):
            narrow = self.narrow(g["key"], col == NARROW, self.is_narrow)
            g["far"].append(self.remote(g["shares"](col), mine, self.other(s), narrow=narrow))
        for s, col in ((self.s, self.column_of(self.zn)), (self.sib, self.column_of(self.diag))):
            narrow = self.narrow(g["key"], col == NARROW, self.is_narrow)
            device = self.other(s)
            g["middle"].append(
                self.remote(g["shares"](col), mine, device, self.is_middle, self.is_end, narrow=narrow)
            )
        self.given += g["far"] + g["middle"]

    def spread(self, g):
        for c in g["here"]:
            c.wait_recv()
        g["own"].wait()
        if self.cfg["whole"]:
            return
        part = g["full"].at[self.rows(self.hi, 1 - self.z, self.x), :]
        device = self.other(self.zn)
        g["passed"] = self.remote(part, part, device, self.is_middle, self.is_middle, narrow=g["narrow"])
        parts = [g["full"].at[self.rows(self.hi, z, self.x), :] for z in range(2)]
        g["near"] = [self.to_x(part, part, g["narrow"]) for part in parts]
        self.gathered += [g["passed"]] + g["near"]

    def onward(self, g, z):
        part = g["full"].at[self.rows(self.next_hi, z, self.x), :]
        copy = self.to_x(part, part, g["narrow"])
        g["near"].append(copy)
        self.gathered.append(copy)

    def spread_same(self, g):
        if self.cfg["whole"]:
            return
        for c in g["far"]:
            c.wait_recv()
        self.onward(g, 1 - self.z)

    def spread_rest(self, g):
        if self.cfg["whole"]:
            return
        for c in g["middle"] + [g["passed"]]:
            c.wait_recv()
        self.onward(g, self.z)

    def spread_done(self, g):
        if not self.cfg["whole"]:
            for c in g["near"]:
                c.wait_recv()

    def columns_back(self, full, result, key=""):
        if self.cfg["whole"]:
            return self.local(full, result).wait
        copies = []
        for s in (self.zn, self.diag, self.sib):
            narrow = self.narrow(key, self.is_narrow, self.column_of(s) == NARROW)
            copies.append(self.remote(self.share(full, s), result.at[self.col], self.mate(s), narrow=narrow))
        own = self.local(self.share(full, self.s), result.at[self.col])

        def wait():
            for c in copies:
                c.wait_recv()
            own.wait()

        return wait

    def add_rows(self, grad, rows, parts):
        size, tile = 2 * self.cfg["DB"], 2 * self.cfg["DB"]
        tile = next(t for t in (112, 32, 16) if size % t == 0)
        for i in range(size // tile):
            place = pl.ds(pl.multiple_of(rows.start + i * tile, 16), tile)
            total = grad[place, :].astype(F32)
            for part in parts:
                total = total + part[i * tile : (i + 1) * tile, :].astype(F32)
            grad[place, :] = total.astype(BF)

    def collect(self, grad, slots, key=""):
        if self.cfg["whole"]:
            return None
        near = []
        narrow = self.narrow(key, self.is_narrow, self.is_narrow)
        for k, hi in enumerate((self.next_hi, self.hi)):
            for z in range(2):
                near.append(self.to_x(grad.at[self.rows(hi, z, 1 - self.x), :], slots.at[2 * k + z], narrow))
        return {"grad": grad, "slots": slots, "near": near, "far": [], "narrow": narrow}

    def collect_on(self, g, planes=(0, 1)):
        if g is None:
            return
        for z in planes:
            g["near"][z].wait_recv()
            rows = self.rows(self.next_hi, z, self.x)
            self.add_rows(g["grad"], rows, [g["slots"].at[z]])
            g["far"].append(self.to_half(g["grad"].at[rows, :], g["slots"].at[4 + z], g["narrow"]))

    def collect_done(self, g):
        if g is None:
            return
        for z in range(2):
            g["near"][2 + z].wait_recv()
            g["far"][z].wait_recv()
            rows = self.rows(self.hi, z, self.x)
            self.add_rows(g["grad"], rows, [g["slots"].at[2 + z], g["slots"].at[4 + z]])


    def rim_out(self, ends, slots):
        after = self.peer((self.hi + self.x) % self.cfg["NH"], 1 - self.x)
        return [self.to_x(ends[0], slots(self.x)), self.remote(ends[1], slots(1 - self.x), after)]

    def rim_home(self, slots, ends):
        before = self.peer((self.hi + self.cfg["NH"] - 1 + self.x) % self.cfg["NH"], 1 - self.x)
        return [self.to_x(slots(1 - self.x), ends[0]), self.remote(slots(self.x), ends[1], before)]


    def gather_start(self, buf):
        own = buf.at[self.s, self.y]
        halves = [own.at[:, h] for h in self.halves]
        z = [self.to_z(half, half) for half in halves]
        return {"z": z, "y": self.to_y(own, own), "own": self.to_sib(own, own), "buf": buf}

    def gather_relay(self, g):
        buf = g["buf"]
        g["d"], g["fz"] = [], []
        for c, h in zip(g["z"], self.halves, strict=True):
            c.wait_recv()
            part = buf.at[self.zn, self.y, :, h]
            g["d"].append(self.to_y(part, part))
            g["fz"].append(self.to_sib(part, part))
        g["y"].wait_recv()
        part = buf.at[self.s, self.yn]
        g["fy"] = self.to_sib(part, part)
        g["own"].wait_recv()

    def gather_near(self, g):
        g["fy"].wait_recv()

    def gather_finish(self, g, near=False):
        g["fd"] = []
        for c, h in zip(g["d"], self.halves, strict=True):
            c.wait_recv()
            part = g["buf"].at[self.zn, self.yn, :, h]
            g["fd"].append(self.to_sib(part, part))
        for c in ([] if near else [g["fy"]]) + g["fz"] + g["fd"]:
            c.wait_recv()
        g["copies"] = [g["own"], g["y"], g["fy"]] + g["z"] + g["d"] + g["fz"] + g["fd"]

    def scatter_pair(self, st, partial):
        sc, rc = st["sc"], st["rc"]
        copies = []
        for k, pair in enumerate((self.diag, self.sib)):
            sc[k] = partial(pair).astype(BF).reshape(sc.shape[1:])
            copies.append(self.to_sib(sc.at[k], rc.at[k]))
        return {"pair": copies, "st": st}

    def scatter_send(self, g, partial):
        st = g["st"]
        so, rc = st["so"], st["rc"]
        value = partial(self.zn)
        g["pair"][0].wait_recv()
        so[0] = (value + flat(rc[0].astype(F32))).astype(BF).reshape(so.shape[1:])
        g["d"] = [self.to_y(so.at[0, self.yn, :, h], st["rd"].at[:, h]) for h in self.halves]
        value = partial(self.s)
        g["pair"][1].wait_recv()
        so[1] = (value + flat(rc[1].astype(F32))).astype(BF).reshape(so.shape[1:])
        g["y"] = self.to_y(so.at[1, self.yn], st["ry"])

    def scatter_relay(self, g):
        st = g["st"]
        so = st["so"]
        g["z"] = []
        for c, h in zip(g["d"], self.halves, strict=True):
            c.wait_recv()
            so[0, self.y, :, h] = (so[0, self.y, :, h].astype(F32) + st["rd"][:, h].astype(F32)).astype(BF)
            g["z"].append(self.to_z(so.at[0, self.y, :, h], st["rz"].at[:, h]))

    def scatter_finish(self, g):
        st = g["st"]
        for c in g["z"] + [g["y"]]:
            c.wait_recv()
        total = st["so"][1, self.y].astype(F32) + st["rz"][...].astype(F32) + st["ry"][...].astype(F32)
        self.settle(g["pair"] + g["d"] + g["z"] + [g["y"]])
        return total


    def place(self, s):
        return 1 + 2 * s + s // 2

    def project(self, w):
        def step(i, _):
            rows = flat(self.u1[i])
            out = dot(rows, w[...], NN).astype(BF)
            self.qkv[pl.ds(self.place(i), 2)] = out.reshape(2, 2 * WINDOW, out.shape[1])
            return 0

        lax.fori_loop(0, SUB, step, 0)

    def masks(self, s):
        at = 1 + s + s // 2
        before, own = self.starts[at - 1], self.starts[at]
        lane = lax.broadcasted_iota(jnp.int32, before.shape, 1)
        even = jnp.where(lane < WINDOW, pltpu.roll(before, WINDOW, 1), pltpu.roll(own, WINDOW, 1))
        shape = (WINDOW, 2 * WINDOW)
        i = lax.broadcasted_iota(jnp.int32, shape, 0)
        j = lax.broadcasted_iota(jnp.int32, shape, 1)
        square = (2 * WINDOW, 2 * WINDOW)
        later = lax.broadcasted_iota(jnp.int32, square, 0) > lax.broadcasted_iota(jnp.int32, square, 1)
        later = later.astype(F32).astype(BF)
        band = (j <= i + WINDOW) & (j > i)
        result = []
        for rows in (even, own):
            per_batch = []
            for batch in range(2):
                line = jnp.broadcast_to(rows[batch : batch + 1, :], shape)
                line = jnp.where(j <= i + WINDOW, line, 0.0).astype(BF)
                between = dot(line, later, NN)
                per_batch.append(band & (between < 0.5))
            result.append(per_batch)
        return result

    def tile(self, index, batch, part, head):
        cols = slice(part * 2 * HP + head * HP, part * 2 * HP + (head + 1) * HP)
        return self.qkv[index, batch * WINDOW : (batch + 1) * WINDOW, cols]

    def attend(self, first):
        def step(run, _):
            s = 2 * run + first
            allowed = self.masks(s)
            for half in range(2):
                p = self.place(s) + half
                for batch in range(2):
                    for head in range(2):
                        q = self.tile(p, batch, 0, head)
                        k = jnp.concatenate([self.tile(p - 1, batch, 1, head), self.tile(p, batch, 1, head)], axis=0)
                        v = jnp.concatenate([self.tile(p - 1, batch, 2, head), self.tile(p, batch, 2, head)], axis=0)
                        scores = dot(q, k, NT) * DH ** (-0.5)
                        scores = jnp.where(allowed[half][batch], scores, -1e30)
                        top = jnp.max(scores, axis=-1, keepdims=True)
                        weights = jnp.exp(scores - top)
                        probs = weights / jnp.sum(weights, axis=-1, keepdims=True)
                        self.probs[2 * s + half, 2 * batch + head] = probs
                        out = dot(probs.astype(BF), v, NN).astype(BF)
                        self.heads[s, half, batch * WINDOW : (batch + 1) * WINDOW, head * HP : (head + 1) * HP] = out
            return 0

        lax.fori_loop(0, 2, step, 0)

    def attend_back(self, s):
        run = s // 2
        for half in range(2):
            p = self.place(s) + half
            for batch in range(2):
                rows = slice(batch * WINDOW, (batch + 1) * WINDOW)
                for head in range(2):
                    cols = slice(head * HP, (head + 1) * HP)
                    q = self.tile(p, batch, 0, head)
                    k = jnp.concatenate([self.tile(p - 1, batch, 1, head), self.tile(p, batch, 1, head)], axis=0)
                    v = jnp.concatenate([self.tile(p - 1, batch, 2, head), self.tile(p, batch, 2, head)], axis=0)
                    probs = self.probs[2 * s + half, 2 * batch + head]
                    d_out = self.d_heads[s, half, rows, cols]
                    d_probs = dot(d_out, v, NT)
                    inner = jnp.sum(probs * d_probs, axis=-1, keepdims=True)
                    d_scores = (probs * (d_probs - inner)).astype(BF)
                    d_q = dot(d_scores, k, NN) * DH ** (-0.5)
                    d_k = dot(d_scores, q, TN) * DH ** (-0.5)
                    d_v = dot(probs.astype(BF), d_out, TN)
                    self.qkv[p, rows, head * HP : (head + 1) * HP] = d_q.astype(BF)
                    for part, grad in ((1, d_k), (2, d_v)):
                        slot = slice((part - 1) * 2 * HP + head * HP, (part - 1) * 2 * HP + (head + 1) * HP)
                        place = slice(part * 2 * HP + head * HP, part * 2 * HP + (head + 1) * HP)
                        done = self.carry[run, rows, slot] + grad[:WINDOW]
                        self.qkv[p - 1, rows, place] = done.astype(BF)
                        self.carry[run, rows, slot] = grad[WINDOW:]

    def grad_into(self, target, left, right):
        width = 256

        def step(m, _):
            cols = pl.ds(pl.multiple_of(m * width, width), width)
            parts = right()
            each = SUB // len(parts)
            total = 0.0
            for k, part in enumerate(parts):
                total = total + dot(flat(left[k * each : (k + 1) * each, :, :, cols]), part, TN)
            target[cols, :] = total.astype(BF)
            return 0

        lax.fori_loop(0, self.cfg["D"] // width, step, 0)

    def gate_and_up(self, plane):
        def step(k, _):
            i = 2 * plane + k
            rows = flat(self.u2[i])
            self.d_ga[i] = dot(rows, self.w_ga[...], NN).astype(BF).reshape(self.d_ga.shape[1:])
            self.d_up[i] = dot(rows, self.w_up[...], NN).astype(BF).reshape(self.d_up.shape[1:])
            return 0

        lax.fori_loop(0, 2, step, 0)

    def feed_forward(self, plane, ahead):
        ff = self.w_dn.shape[1]

        def step(k, _):
            i = 2 * plane + k
            if ahead:
                gate = flat(self.d_ga[i]).astype(F32)
                upward = flat(self.d_up[i]).astype(F32)
            else:
                rows = flat(self.u2[i])
                gate = dot(rows, self.w_ga[...], NN)
                upward = dot(rows, self.w_up[...], NN)
            d_hidden = dot(flat(self.g[i]), self.w_dn[...], NN)
            sig = jax.nn.sigmoid(gate)
            silu = gate * sig
            shape = (2, 2 * WINDOW, ff)
            self.hidden[i] = (silu * upward).astype(BF).reshape(shape)
            d_gate = d_hidden * upward * sig * (1.0 + gate * (1.0 - sig))
            self.d_ga[i] = d_gate.astype(BF).reshape(shape)
            self.d_up[i] = (d_hidden * silu).astype(BF).reshape(shape)
            return 0

        lax.fori_loop(0, 2, step, 0)

    def run(self):
        cfg = self.cfg
        me = (self.s, self.y)
        norm = lambda v: lax.rsqrt(jnp.mean(v * v, axis=-1, keepdims=True) + EPSILON)
        whole = lambda ref: [flat(ref[...])]

        everyone_here = self.barrier()
        if cfg["uneven"]:

            @pl.when(self.is_narrow)
            def _():
                for w in (self.w_ga, self.w_up, self.w_dn):
                    w[:, w.shape[1] - HP :] = jnp.zeros((w.shape[0], HP), BF)

        line = 1 + self.s + self.s // 2
        own_starts = self.doc_starts[...].astype(F32)
        fill = jnp.zeros((self.starts.shape[1] - own_starts.shape[0], own_starts.shape[1]), F32)
        self.starts[line] = jnp.concatenate([own_starts, fill], axis=0)
        own_line = self.starts.at[line]
        x = self.x_in[...].astype(F32)
        self.u1[me] = (x * norm(x)).astype(BF)
        if not cfg["whole"]:
            self.prepare("qkv")
        everyone_here()
        start_copies = [self.remote(own_line, own_line, self.mate(s)) for s in (self.sib, self.zn, self.diag)]
        qkv = self.columns_out("qkv")
        gather_one = self.gather_start(self.u1)
        self.columns_far(qkv)
        self.spread(qkv)
        for c in start_copies:
            c.wait_recv()
        rim_starts = self.rim_out([self.starts.at[2], self.starts.at[5]], lambda run: self.starts.at[3 * run])
        self.spread_same(qkv)
        self.gather_relay(gather_one)
        self.spread_rest(qkv)
        out = self.columns_out("out")
        self.columns_far(out)
        ga = self.columns_out("ga")
        self.gather_finish(gather_one)
        self.spread_done(qkv)

        self.project(self.w_qkv)
        rims = self.rim_out(
            [self.qkv.at[4, :, slice(2 * HP, 6 * HP)], self.qkv.at[9, :, slice(2 * HP, 6 * HP)]],
            lambda run: self.qkv.at[5 * run, :, slice(2 * HP, 6 * HP)],
        )
        self.spread(out)
        self.columns_far(ga)
        up = self.columns_out("up")
        self.attend(1)
        self.spread_same(out)
        self.spread_rest(out)
        for c in rim_starts + rims:
            c.wait_recv()
        self.spread(ga)
        self.columns_far(up)
        self.attend(0)
        self.spread(up)
        dn = self.columns_out("dn")
        self.spread_same(ga)
        self.spread_done(out)

        partial = lambda pair: dot(flat(self.heads[pair]), self.w_out[...], NT)
        stage = {n: getattr(self, n) for n in ("sc", "rc", "so", "rd", "rz", "ry")}
        scatter = self.scatter_pair(stage, partial)
        self.scatter_send(scatter, partial)
        self.scatter_relay(scatter)
        self.spread_rest(ga)
        self.g[me] = self.g_in[...]
        gather_g = self.gather_start(self.g)
        self.columns_far(dn)
        self.spread(dn)
        self.spread_same(up)
        self.resid[...] = self.x_in[...].astype(F32) + self.scatter_finish(scatter)
        resid = self.resid[...]
        self.u2[me] = (resid * norm(resid)).astype(BF)
        gather_two = self.gather_start(self.u2)
        self.spread_rest(up)
        self.spread_same(dn)
        self.gather_relay(gather_g)
        self.settle(self.given)
        self.spread_rest(dn)
        self.gather_relay(gather_two)
        for g in (ga, up):
            self.spread_done(g)
        self.gather_near(gather_two)
        self.gate_and_up(self.s // 2)
        self.gather_finish(gather_g)
        self.spread_done(dn)
        self.feed_forward(self.s // 2, True)
        self.gather_finish(gather_two, near=True)
        self.feed_forward(1 - self.s // 2, False)
        self.grad_into(self.g_dn, self.g, lambda: whole(self.hidden))
        sum_dn = self.collect(self.g_dn, self.slots_dn, "dn")
        partial = lambda pair: dot(flat(self.d_ga[pair]), self.w_ga[...], NT) + dot(
            flat(self.d_up[pair]), self.w_up[...], NT
        )
        scatter = self.scatter_pair(stage, partial)
        self.scatter_send(scatter, partial)
        self.collect_on(sum_dn, (0,))
        self.settle(self.gathered)
        self.grad_into(self.w_ga, self.u2, lambda: whole(self.d_ga))
        sum_ga = self.collect(self.w_ga, self.slots_ga, "ga")
        self.collect_on(sum_dn, (1,))
        self.scatter_relay(scatter)
        self.grad_into(self.w_up, self.u2, lambda: whole(self.d_up))
        sum_up = self.collect(self.w_up, self.slots_up, "up")
        d_unit = self.scatter_finish(scatter)
        resid = self.resid[...]
        scale = norm(resid)
        unit = resid * scale
        inner = jnp.mean(d_unit * unit, axis=-1, keepdims=True)
        self.in_grad[...] = self.g_in[...].astype(F32) + scale * (d_unit - unit * inner)
        self.d_r[me] = self.in_grad[...].astype(BF)
        self.settle(gather_g["copies"] + gather_two["copies"] + rims)
        gather_d = self.gather_start(self.d_r)
        self.collect_on(sum_ga, (0,))
        self.gather_relay(gather_d)
        self.collect_on(sum_ga, (1,))

        view = {
            "sc": self.u2.at[0:2],
            "so": self.u2.at[2:4],
            "rc": self.g.at[0:2],
            "rd": self.g.at[2, 0],
            "rz": self.g.at[2, 1],
            "ry": self.g.at[3, 0],
        }
        partial = lambda pair: dot(flat(self.hidden[pair]), self.w_dn[...], NT)
        mlp = self.scatter_pair(view, partial)
        self.scatter_send(mlp, partial)
        self.gather_finish(gather_d)

        d_heads = self.d_heads = self.d_ga.at[:, :, :, slice(0, 2 * HP)]

        def heads_back(i, _):
            value = dot(flat(self.d_r[i]), self.w_out[...], NN).astype(BF)
            d_heads[i] = value.reshape(2, 2 * WINDOW, 2 * HP)
            return 0

        lax.fori_loop(0, SUB, heads_back, 0)
        self.collect_done(sum_dn)
        backs = [self.columns_back(self.g_dn, self.o_dn, "dn")]

        self.carry[...] = jnp.zeros_like(self.carry)

        def first(run, _):
            self.attend_back(2 * run)
            return 0

        def second(run, _):
            self.attend_back(2 * run + 1)
            return 0

        lax.fori_loop(0, 2, first, 0)
        rim_back = self.rim_home(
            lambda run: self.qkv.at[5 * run, :, slice(2 * HP, 6 * HP)], [self.rim.at[0], self.rim.at[1]]
        )
        self.scatter_relay(mlp)
        self.collect_on(sum_up, (0,))
        lax.fori_loop(0, 2, second, 0)
        of_q, of_kv = slice(0, 2 * HP), slice(2 * HP, 6 * HP)
        g_q, g_kv = self.g_qkv.at[:, of_q], self.g_qkv.at[:, of_kv]
        self.grad_into(g_q, self.u1, lambda: [flat(self.qkv[1:5, :, of_q]), flat(self.qkv[6:10, :, of_q])])
        sum_q = self.collect(g_q, self.slots_qkv.at[:, :, of_q])
        self.collect_on(sum_up, (1,))
        self.collect_done(sum_ga)
        backs.append(self.columns_back(self.w_ga, self.o_ga, "ga"))
        for c in rim_back:
            c.wait_recv()
        for run in range(2):
            done = self.carry[run] + self.rim[run].astype(F32)
            self.qkv[5 * run + 4, :, 2 * HP :] = done.astype(BF)

        self.grad_into(g_kv, self.u1, lambda: [flat(self.qkv[1:5, :, of_kv]), flat(self.qkv[6:10, :, of_kv])])
        sum_kv = self.collect(g_kv, self.slots_qkv.at[:, :, of_kv])
        self.grad_into(self.w_out, self.d_r, lambda: whole(self.heads))
        sum_out = self.collect(self.w_out, self.slots_out)
        self.collect_on(sum_q)
        partial = lambda pair: dot(flat(self.qkv[pl.ds(self.place(pair), 2)]), self.w_qkv[...], NT)
        scatter = self.scatter_pair(stage, partial)
        self.scatter_send(scatter, partial)
        self.collect_on(sum_kv, (0,))
        self.scatter_relay(scatter)
        self.collect_on(sum_kv, (1,))
        self.collect_done(sum_up)
        backs.append(self.columns_back(self.w_up, self.o_up, "up"))
        self.out[...] = (self.resid[...] + self.scatter_finish(mlp)).astype(BF)
        back_to = lambda span: self.o_qkv.at[:, span] if cfg["whole"] else self.o_qkv.at[:, :, span]
        self.collect_done(sum_q)
        backs.append(self.columns_back(g_q, back_to(of_q)))
        self.collect_on(sum_out)
        self.collect_done(sum_kv)
        backs.append(self.columns_back(g_kv, back_to(of_kv)))
        self.collect_done(sum_out)
        backs.append(self.columns_back(self.w_out, self.o_out))
        d_unit = self.scatter_finish(scatter)
        x = self.x_in[...].astype(F32)
        scale = norm(x)
        unit = x * scale
        inner = jnp.mean(d_unit * unit, axis=-1, keepdims=True)
        self.in_grad[...] += scale * (d_unit - unit * inner)
        for wait in backs:
            wait()
        self.settle()

    def settle(self, copies=None):
        for c in self.sends:
            if copies is None or any(c is other for other in copies):
                c.wait_send()
        if copies is None:
            self.sends = []
        else:
            self.sends = [c for c in self.sends if not any(c is other for other in copies)]


def fused(cfg, width, weights, starts, x, g):
    d, db = cfg["D"], cfg["DB"]
    rows = 2 * WINDOW
    anywhere = pl.BlockSpec(memory_space=pl.ANY)
    vmem = pl.BlockSpec(memory_space=pltpu.VMEM)
    keys = ("qkv", "out", "ga", "up", "dn")
    result = (d,) if cfg["whole"] else (SUB, db)
    outs = [("out", (rows, d), BF, vmem), ("in_grad", (rows, d), F32, vmem)]
    outs += [("o_" + key, result + (width[key],), BF, anywhere) for key in keys]
    if cfg["whole"]:
        ins = [("sh_" + key, anywhere) for key in keys]
    else:
        ins = [(name, vmem) for name in ("raw_qkv", "raw_out", "raw_gu", "raw_dn", "gains")]
    ins += [(name, vmem) for name in ("doc_starts", "x_in", "g_in")]
    plane = (SUB, 2, rows)
    scratch = [("w_" + key, (d, width[key]), BF) for key in keys]
    scratch += [("g_" + key, (d, width[key]), BF) for key in ("qkv", "dn")]
    slot = 16 if cfg["whole"] else 2 * db
    scratch += [("slots_" + key, (6, slot, width[key]), BF) for key in keys]
    scratch += [(name, plane + (d,), BF) for name in ("u1", "u2", "g", "d_r")]
    scratch += [(name, plane + (width["out"],), BF) for name in ("heads",)]
    scratch += [(name, plane + (width["dn"],), BF) for name in ("hidden", "d_ga", "d_up")]
    scratch += [(name, (2, 2, rows, d), BF) for name in ("sc", "rc", "so")]
    scratch += [
        ("starts", (SUB + 2, 8, rows), F32),
        ("qkv", (2 * SUB + 2, rows, width["qkv"]), BF),
        ("probs", (2 * SUB, 4, WINDOW, 2 * WINDOW), F32),
        ("carry", (2, rows, 4 * HP), F32),
        ("rim", (2, rows, 4 * HP), BF),
        ("resid", (rows, d), F32),
        ("rd", (rows, d), BF),
        ("rz", (rows, d), BF),
        ("ry", (rows, d), BF),
    ]
    number = 220
    names = [n for n, _ in ins] + [n for n, *_ in outs] + [n for n, *_ in scratch]
    names += ["send_sems", "recv_sems", "local_sems"]

    def kernel(*refs):
        Kernel(cfg, dict(zip(names, refs, strict=True))).run()

    return pl.pallas_call(
        kernel,
        out_shape=[jax.ShapeDtypeStruct(shape, kind) for _, shape, kind, _ in outs],
        in_specs=[spec for _, spec in ins],
        out_specs=[spec for *_, spec in outs],
        scratch_shapes=[pltpu.VMEM(shape, kind) for _, shape, kind in scratch]
        + [
            pltpu.SemaphoreType.DMA((number,)),
            pltpu.SemaphoreType.DMA((number,)),
            pltpu.SemaphoreType.DMA((11,)),
        ],
        compiler_params=pltpu.CompilerParams(
            collective_id=0, has_side_effects=True, vmem_limit_bytes=64 * 2**20
        ),
    )(*weights, starts, x, g)


def assemble(spans, *refs):
    gains, sources, results, g_gain = refs[0], refs[1:10], refs[10:16], refs[16]
    held, made, sems = refs[17:26], refs[26:30], refs[30]
    copies = [pltpu.make_async_copy(a, b, sems.at[k]) for k, (a, b) in enumerate(zip(sources, held, strict=True))]
    for c in copies:
        c.start()
    ready = made + held[7:]
    back = [pltpu.make_async_copy(a, b, sems.at[9 + k]) for k, (a, b) in enumerate(zip(ready, results, strict=True))]
    o_ga, o_up, w_gu, o_dn, o_qkv, w_qkv, o_out = held[:7]
    g_gu, g_dn, g_qkv, g_out = made
    db = w_qkv.shape[1]
    lines = gains[...].astype(F32)
    same = eye(db)

    def column(k):
        return jnp.sum(jnp.where(same, jnp.broadcast_to(lines[k : k + 1, :], (db, db)), 0.0), axis=1, keepdims=True)

    def put(k, total):
        g_gain[k : k + 1, :] = jnp.sum(jnp.where(same, jnp.broadcast_to(total, (db, db)), 0.0), axis=0, keepdims=True)

    gain = column(1)
    total = jnp.zeros((db, 1), F32)
    copies[2].wait()
    for k, ref in enumerate((o_ga, o_up)):
        copies[k].wait()
        value = jnp.concatenate([ref[s, :, : p.stop - p.start].astype(F32) for s, p in enumerate(spans)], axis=1)
        total = total + jnp.sum(value * w_gu[k].astype(F32), axis=1, keepdims=True)
        g_gu[k] = value * gain
    back[0].start()
    put(1, total)
    copies[3].wait()
    g_dn[...] = jnp.concatenate([o_dn[s, :, : p.stop - p.start].astype(F32) for s, p in enumerate(spans)], axis=1)
    back[1].start()
    gain = column(0)
    total = jnp.zeros((db, 1), F32)
    copies[4].wait()
    copies[5].wait()
    for k in range(3):
        parts = []
        for s in range(SUB):
            for h in range(2):
                start = (2 * k + h) * HP
                parts.append(o_qkv[s, :, start : start + DH].astype(F32))
        value = jnp.concatenate(parts, axis=1)
        total = total + jnp.sum(value * w_qkv[k].astype(F32), axis=1, keepdims=True)
        g_qkv[k] = value * gain
    back[2].start()
    put(0, total)
    copies[6].wait()
    parts = [o_out[s, :, h * HP : h * HP + DH].astype(F32) for s in range(SUB) for h in range(2)]
    g_out[...] = jnp.concatenate(parts, axis=1)
    back[3].start()
    for k in range(2):
        copies[7 + k].wait()
        back[4 + k].start()
    for c in back:
        c.wait()


def body(size, tokens, doc_starts, w_qkv, w_out, w_gate_up, w_down, gains, cotangent):
    batches, rows, d = tokens.shape
    db = w_qkv.shape[1]
    ff = w_gate_up.shape[2] // SUB
    ffp = -(-ff // HP) * HP
    heads = w_qkv.shape[2] // (SUB * DH)
    whole = size != 16 or db % 16 != 0
    uneven = not whole and w_gate_up.shape[2] == SUB * ffp - HP
    sizes = [ffp - HP * (uneven and s == NARROW) if uneven else ff for s in range(SUB)]
    spans = [slice(sum(sizes[:s]), sum(sizes[: s + 1])) for s in range(SUB)]
    cfg = {"D": d, "NH": size // 8, "DB": db, "spans": spans, "uneven": uneven, "whole": whole}
    width = {"qkv": 3 * heads * HP, "out": heads * HP, "ga": ffp, "up": ffp, "dn": ffp}
    acts = [doc_starts, tokens.reshape(batches * rows, d), cotangent.reshape(batches * rows, d)]

    def results(out, in_grad, g_qkv, g_out, g_gu, g_dn, gain_sums):
        gain_sums = gain_sums + lax.ppermute(gain_sums, "tp", [(0, 1), (1, 0)])
        return (out.reshape(tokens.shape), in_grad.reshape(tokens.shape), g_qkv, g_out, g_gu, g_dn, gain_sums)

    if not whole:
        out, in_grad, *grads = fused(cfg, width, [w_qkv, w_out.T, w_gate_up, w_down.T, gains], *acts)
        o_qkv, o_out, o_ga, o_up, o_dn = grads
        sources = [o_ga, o_up, w_gate_up, o_dn, o_qkv, w_qkv, o_out, out, in_grad]
        made = [jax.ShapeDtypeStruct(v.shape, F32) for v in (w_gate_up, w_down.T, w_qkv, w_out.T)]
        shapes = made + [jax.ShapeDtypeStruct(v.shape, v.dtype) for v in (out, in_grad)]
        shapes.append(jax.ShapeDtypeStruct(gains.shape, F32))
        anywhere, vmem = pl.BlockSpec(memory_space=pl.ANY), pl.BlockSpec(memory_space=pltpu.VMEM)
        g_gu, g_dn, g_qkv, g_out, out, in_grad, gain_sums = pl.pallas_call(
            functools.partial(assemble, spans),
            out_shape=shapes,
            in_specs=[vmem] + [anywhere] * 9,
            out_specs=[anywhere] * 6 + [vmem],
            scratch_shapes=[pltpu.VMEM(v.shape, v.dtype) for v in sources + made] + [pltpu.SemaphoreType.DMA((15,))],
            compiler_params=pltpu.CompilerParams(vmem_limit_bytes=63 * 2**20),
        )(gains, *sources)
        return results(out, in_grad, g_qkv, g_out.T, g_gu, g_dn.T, gain_sums)

    gain = gains.astype(F32)
    sh_qkv = (w_qkv.astype(F32) * gain[0][None, :, None]).astype(BF).reshape(3, db, SUB, heads, DH)
    sh_qkv = padded(sh_qkv, HP).transpose(2, 1, 0, 3, 4).reshape(SUB, db, 3 * heads * HP)
    sh_out = w_out.T.reshape(db, SUB, heads, DH)
    sh_out = padded(sh_out, HP).transpose(1, 0, 2, 3).reshape(SUB, db, heads * HP)
    scaled = (w_gate_up.astype(F32) * gain[1][None, :, None]).astype(BF).reshape(2, db, SUB, ff)
    sh_ga, sh_up = [padded(scaled[k], ffp).transpose(1, 0, 2) for k in range(2)]
    sh_dn = padded(w_down.T.reshape(db, SUB, ff), ffp).transpose(1, 0, 2)
    f = lax.axis_index("fsdp")
    s = (f // 4) % 2 * 2 + f % 2
    everyone = [lax.all_gather(v, "fsdp", axis=1, tiled=True) for v in (sh_qkv, sh_out, sh_ga, sh_up, sh_dn)]
    shares = [lax.dynamic_index_in_dim(v, s, 0, keepdims=False) for v in everyone]
    out, in_grad, *grads = fused(cfg, width, shares, *acts)
    mine = (jnp.arange(SUB) == s)[:, None, None]
    g_qkv, g_out, g_ga, g_up, g_dn = [
        lax.psum_scatter(jnp.where(mine, v[None], 0).astype(BF), "fsdp", scatter_dimension=1, tiled=True).astype(F32)
        for v in grads
    ]
    g_qkv = g_qkv.reshape(SUB, db, 3, heads, HP)[..., :DH].transpose(2, 1, 0, 3, 4).reshape(w_qkv.shape)
    g_out = g_out.reshape(SUB, db, heads, HP)[..., :DH].transpose(0, 2, 3, 1).reshape(w_out.shape)
    g_gu = jnp.stack([v[..., :ff].transpose(1, 0, 2).reshape(w_gate_up.shape[1:]) for v in (g_ga, g_up)])
    g_dn = g_dn[..., :ff].transpose(0, 2, 1).reshape(w_down.shape)
    gain_sums = jnp.stack(
        [
            jnp.sum(g_qkv * w_qkv.astype(F32), axis=(0, 2)),
            jnp.sum(g_gu * w_gate_up.astype(F32), axis=(0, 2)),
        ]
    )
    g_qkv, g_gu = g_qkv * gain[0][None, :, None], g_gu * gain[1][None, :, None]
    return results(out, in_grad, g_qkv, g_out, g_gu, g_dn, gain_sums)


def solution(mesh):
    in_specs = (
        P(None, ("fsdp", "tp"), None),
        P(None, "fsdp"),
        P(None, "fsdp", "tp"),
        P("tp", "fsdp"),
        P(None, "fsdp", "tp"),
        P("tp", "fsdp"),
        P(None, "fsdp"),
        P(None, ("fsdp", "tp"), None),
    )
    out_specs = (
        P(None, ("fsdp", "tp"), None),
        P(None, ("fsdp", "tp"), None),
        P(None, "fsdp", "tp"),
        P("tp", "fsdp"),
        P(None, "fsdp", "tp"),
        P("tp", "fsdp"),
        P(None, "fsdp"),
    )
    return jax.shard_map(
        functools.partial(body, mesh.shape["fsdp"]), mesh=mesh, in_specs=in_specs, out_specs=out_specs, check_vma=False
    )
```

```python
import functools

import jax
import jax.numpy as jnp
from jax import lax
from jax.experimental import pallas as pl
from jax.experimental.pallas import tpu as pltpu
from jax.sharding import PartitionSpec as P

DH = 112
HP = 128
WINDOW = 64
EPSILON = 1e-06
SUB = 4
NARROW = 1
BF = jnp.bfloat16
F32 = jnp.float32
NN = (((1,), (0,)), ((), ()))
NT = (((1,), (1,)), ((), ()))
TN = (((0,), (0,)), ((), ()))


def dot(a, b, dims):
    return lax.dot_general(a, b, dims, preferred_element_type=F32)


def flat(value):
    return value.reshape(-1, value.shape[-1])


def eye(size):
    shape = (size, size)
    return lax.broadcasted_iota(jnp.int32, shape, 0) == lax.broadcasted_iota(jnp.int32, shape, 1)


def padded(value, size):
    extra = size - value.shape[-1]
    if not extra:
        return value
    return jnp.concatenate([value, jnp.zeros(value.shape[:-1] + (extra,), value.dtype)], axis=-1)


class Conditional:
    def __init__(self, copy, sent, received, part=None, narrow=None):
        self.copy, self.sent, self.received, self.part, self.narrow = copy, sent, received, part, narrow

    def under(self, condition, k, name):
        if self.part is None:
            pl.when(condition)(getattr(self.copy, name))
            return
        thin = self.narrow[k]
        wide = jnp.logical_not(thin)
        if condition is not None:
            thin, wide = jnp.logical_and(condition, thin), jnp.logical_and(condition, wide)
        pl.when(thin)(getattr(self.part, name))
        pl.when(wide)(getattr(self.copy, name))

    def start(self):
        self.under(self.sent, 0, "start")

    def wait_send(self):
        self.under(self.sent, 0, "wait_send")

    def wait_recv(self):
        self.under(self.received, 1, "wait_recv")


class Kernel:
    def __init__(self, cfg, refs):
        self.cfg = cfg
        self.__dict__.update(refs)
        self.f = lax.axis_index("fsdp")
        self.y = lax.axis_index("tp")
        core = self.f % 2
        self.x = (self.f // 2) % 2
        self.hi = self.f // 8
        self.z = (self.f // 4) % 2
        self.is_middle = self.hi + self.z == 1
        self.is_end = self.hi + self.z != 1
        self.s = (self.f // 4) % 2 * 2 + core
        self.col = self.column_of(self.s)
        self.is_narrow = self.col == NARROW
        self.sib = self.s + 1 - 2 * core
        self.zn = (self.s + 2) % SUB
        self.diag = (self.sib + 2) % SUB
        self.yn = 1 - self.y
        self.next_hi = (self.hi + 1) % cfg["NH"]
        self.last_hi = (self.hi + cfg["NH"] - 1) % cfg["NH"]
        self.count = 0
        self.local_count = 0
        self.sends = []
        self.gathered = []
        self.given = []
        middle = cfg["D"] // 256 * 128
        self.halves = (slice(0, middle), slice(middle, cfg["D"]))

    def column_of(self, s):
        if self.cfg["whole"]:
            return s
        return (s // 2 + self.hi) % 2 * 2 + s % 2

    def index(self, hi, s, x):
        return hi * 8 + s // 2 * 4 + x * 2 + s % 2

    def mate(self, s):
        return {"fsdp": self.index(self.hi, s, self.x), "tp": self.y}

    def other(self, s):
        return {"fsdp": self.index(self.next_hi, s, self.x), "tp": self.y}

    def peer(self, hi, x):
        s = self.s if self.cfg["whole"] else jnp.where(hi == self.hi, self.s, self.zn)
        return {"fsdp": self.index(hi, s, x), "tp": self.y}

    def barrier(self):
        sem = pltpu.get_barrier_semaphore()
        partners = [self.mate(s) for s in (self.sib, self.zn, self.diag)]
        partners += [{"fsdp": self.f, "tp": self.yn}, self.peer(self.hi, 1 - self.x)]
        partners += [self.peer(self.next_hi, 1 - self.x)]
        if self.cfg["whole"]:
            partners += [self.peer(self.last_hi, 1 - self.x)]
        else:
            partners += [self.other(s) for s in (self.s, self.sib, self.zn, self.diag)]
        for partner in partners:
            pl.semaphore_signal(sem, inc=1, device_id=partner, device_id_type=pl.DeviceIdType.MESH)
        return lambda: pl.semaphore_wait(sem, len(partners))

    def remote(self, src, dst, device, sent=None, received=None, narrow=None):
        k = self.count
        self.count += 1

        def describe(src, dst):
            return pltpu.make_async_remote_copy(
                src_ref=src,
                dst_ref=dst,
                send_sem=self.send_sems.at[k],
                recv_sem=self.recv_sems.at[k],
                device_id=device,
                device_id_type=pl.DeviceIdType.MESH,
            )

        copy = describe(src, dst)
        if narrow is not None:
            part = slice(0, src.shape[1] - HP)
            copy = Conditional(copy, sent, received, describe(src.at[:, part], dst.at[:, part]), narrow)
        elif sent is not None:
            copy = Conditional(copy, sent, received)
        copy.start()
        self.sends.append(copy)
        return copy

    def narrow(self, key, sent, received):
        return (sent, received) if key in ("ga", "up", "dn") and self.cfg["uneven"] else None

    def to_sib(self, src, dst):
        return self.remote(src, dst, self.mate(self.sib))

    def to_z(self, src, dst):
        return self.remote(src, dst, self.mate(self.zn))

    def to_y(self, src, dst):
        return self.remote(src, dst, {"fsdp": self.f, "tp": self.yn})

    def to_x(self, src, dst, narrow=None):
        return self.remote(src, dst, self.peer(self.hi, 1 - self.x), narrow=narrow)

    def to_half(self, src, dst, narrow=None):
        return self.remote(src, dst, self.peer(self.next_hi, self.x), narrow=narrow)

    def local(self, src, dst):
        k = self.local_count
        self.local_count += 1
        copy = pltpu.make_async_copy(src, dst, self.local_sems.at[k])
        copy.start()
        return copy


    def rows(self, hi, z, x):
        size = 2 * self.cfg["DB"]
        return pl.ds(pl.multiple_of(((hi * 2 + z) * 2 + x) * size, 16), size)

    def share(self, ref, s):
        db = self.cfg["DB"]
        return ref.at[pl.ds(pl.multiple_of(self.index(self.hi, s, self.x) * db, 16), db), :]

    def columns_out(self, key):
        full = getattr(self, "w_" + key)
        if self.cfg["whole"]:
            return {"full": full, "own": self.local(getattr(self, "sh_" + key), full), "here": []}
        if key != "qkv":
            self.prepare(key)
        shares = functools.partial(self.prepared, key)
        mine = self.share(full, self.s)
        here = []
        for s in (self.zn, self.diag, self.sib):
            col = self.column_of(s)
            narrow = self.narrow(key, col == NARROW, self.is_narrow)
            here.append(self.remote(shares(col), mine, self.mate(s), narrow=narrow))
        self.given += here
        same = self.narrow(key, self.is_narrow, self.is_narrow)
        own = self.local(shares(self.col), mine)
        return {"key": key, "full": full, "shares": shares, "own": own, "here": here, "narrow": same}

    def prepared(self, key, s):
        db = self.cfg["DB"]
        rows = pl.ds(pl.multiple_of(s % 2 * db, 16), db)
        return getattr(self, "slots_" + key).at[s // 2, rows, :]

    def gain_column(self, k):
        db = self.cfg["DB"]
        line = jnp.broadcast_to(self.gains[...].astype(F32)[k : k + 1, :], (db, db))
        return jnp.sum(jnp.where(eye(db), line, 0.0), axis=1, keepdims=True)

    def prepare(self, key):
        db = self.cfg["DB"]
        slots = getattr(self, "slots_" + key)
        if key in ("qkv", "ga", "up"):
            gain = self.gain_column(0 if key == "qkv" else 1)
        for s in range(SUB):
            if key == "qkv":
                blocks = [(k, 2 * s + h) for k in range(3) for h in range(2)]
                parts = [self.raw_qkv[k, :, n * DH : (n + 1) * DH].astype(F32) * gain for k, n in blocks]
            elif key == "out":
                parts = [self.raw_out[:, n * DH : (n + 1) * DH].astype(F32) for n in (2 * s, 2 * s + 1)]
            elif key == "dn":
                parts = [self.raw_dn[:, self.cfg["spans"][s]].astype(F32)]
            else:
                parts = [self.raw_gu[int(key == "up"), :, self.cfg["spans"][s]].astype(F32) * gain]
            value = jnp.concatenate([padded(part, slots.shape[2] // len(parts)) for part in parts], axis=1)
            slots[s // 2, s % 2 * db : (s % 2 + 1) * db, :] = value.astype(BF)

    def columns_far(self, g):
        if self.cfg["whole"]:
            return
        mine = self.share(g["full"], self.s)
        g["far"], g["middle"] = [], []
        for s, col in ((self.zn, self.col), (self.diag, self.column_of(self.sib))):
            narrow = self.narrow(g["key"], col == NARROW, self.is_narrow)
            g["far"].append(self.remote(g["shares"](col), mine, self.other(s), narrow=narrow))
        for s, col in ((self.s, self.column_of(self.zn)), (self.sib, self.column_of(self.diag))):
            narrow = self.narrow(g["key"], col == NARROW, self.is_narrow)
            device = self.other(s)
            g["middle"].append(
                self.remote(g["shares"](col), mine, device, self.is_middle, self.is_end, narrow=narrow)
            )
        self.given += g["far"] + g["middle"]

    def spread(self, g):
        for c in g["here"]:
            c.wait_recv()
        g["own"].wait()
        if self.cfg["whole"]:
            return
        part = g["full"].at[self.rows(self.hi, 1 - self.z, self.x), :]
        device = self.other(self.zn)
        g["passed"] = self.remote(part, part, device, self.is_middle, self.is_middle, narrow=g["narrow"])
        parts = [g["full"].at[self.rows(self.hi, z, self.x), :] for z in range(2)]
        g["near"] = [self.to_x(part, part, g["narrow"]) for part in parts]
        self.gathered += [g["passed"]] + g["near"]

    def onward(self, g, z):
        part = g["full"].at[self.rows(self.next_hi, z, self.x), :]
        copy = self.to_x(part, part, g["narrow"])
        g["near"].append(copy)
        self.gathered.append(copy)

    def spread_same(self, g):
        if self.cfg["whole"]:
            return
        for c in g["far"]:
            c.wait_recv()
        self.onward(g, 1 - self.z)

    def spread_rest(self, g):
        if self.cfg["whole"]:
            return
        for c in g["middle"] + [g["passed"]]:
            c.wait_recv()
        self.onward(g, self.z)

    def spread_done(self, g):
        if not self.cfg["whole"]:
            for c in g["near"]:
                c.wait_recv()

    def columns_back(self, full, result, key=""):
        if self.cfg["whole"]:
            return self.local(full, result).wait
        copies = []
        for s in (self.zn, self.diag, self.sib):
            narrow = self.narrow(key, self.is_narrow, self.column_of(s) == NARROW)
            copies.append(self.remote(self.share(full, s), result.at[self.col], self.mate(s), narrow=narrow))
        own = self.local(self.share(full, self.s), result.at[self.col])

        def wait():
            for c in copies:
                c.wait_recv()
            own.wait()

        return wait

    def add_rows(self, grad, rows, parts):
        size, tile = 2 * self.cfg["DB"], 2 * self.cfg["DB"]
        tile = next(t for t in (112, 32, 16) if size % t == 0)
        for i in range(size // tile):
            place = pl.ds(pl.multiple_of(rows.start + i * tile, 16), tile)
            total = grad[place, :].astype(F32)
            for part in parts:
                total = total + part[i * tile : (i + 1) * tile, :].astype(F32)
            grad[place, :] = total.astype(BF)

    def collect(self, grad, slots, key=""):
        if self.cfg["whole"]:
            return None
        near = []
        narrow = self.narrow(key, self.is_narrow, self.is_narrow)
        for k, hi in enumerate((self.next_hi, self.hi)):
            for z in range(2):
                near.append(self.to_x(grad.at[self.rows(hi, z, 1 - self.x), :], slots.at[2 * k + z], narrow))
        return {"grad": grad, "slots": slots, "near": near, "far": [], "narrow": narrow}

    def collect_on(self, g, planes=(0, 1)):
        if g is None:
            return
        for z in planes:
            g["near"][z].wait_recv()
            rows = self.rows(self.next_hi, z, self.x)
            self.add_rows(g["grad"], rows, [g["slots"].at[z]])
            g["far"].append(self.to_half(g["grad"].at[rows, :], g["slots"].at[4 + z], g["narrow"]))

    def collect_done(self, g):
        if g is None:
            return
        for z in range(2):
            g["near"][2 + z].wait_recv()
            g["far"][z].wait_recv()
            rows = self.rows(self.hi, z, self.x)
            self.add_rows(g["grad"], rows, [g["slots"].at[2 + z], g["slots"].at[4 + z]])


    def rim_out(self, ends, slots):
        after = self.peer((self.hi + self.x) % self.cfg["NH"], 1 - self.x)
        return [self.to_x(ends[0], slots(self.x)), self.remote(ends[1], slots(1 - self.x), after)]

    def rim_home(self, slots, ends):
        before = self.peer((self.hi + self.cfg["NH"] - 1 + self.x) % self.cfg["NH"], 1 - self.x)
        return [self.to_x(slots(1 - self.x), ends[0]), self.remote(slots(self.x), ends[1], before)]


    def gather_start(self, buf):
        own = buf.at[self.s, self.y]
        halves = [own.at[:, h] for h in self.halves]
        z = [self.to_z(half, half) for half in halves]
        return {"z": z, "y": self.to_y(own, own), "own": self.to_sib(own, own), "buf": buf}

    def gather_relay(self, g):
        buf = g["buf"]
        g["d"], g["fz"] = [], []
        for c, h in zip(g["z"], self.halves, strict=True):
            c.wait_recv()
            part = buf.at[self.zn, self.y, :, h]
            g["d"].append(self.to_y(part, part))
            g["fz"].append(self.to_sib(part, part))
        g["y"].wait_recv()
        part = buf.at[self.s, self.yn]
        g["fy"] = self.to_sib(part, part)
        g["own"].wait_recv()

    def gather_near(self, g):
        g["fy"].wait_recv()

    def gather_finish(self, g, near=False):
        g["fd"] = []
        for c, h in zip(g["d"], self.halves, strict=True):
            c.wait_recv()
            part = g["buf"].at[self.zn, self.yn, :, h]
            g["fd"].append(self.to_sib(part, part))
        for c in ([] if near else [g["fy"]]) + g["fz"] + g["fd"]:
            c.wait_recv()
        g["copies"] = [g["own"], g["y"], g["fy"]] + g["z"] + g["d"] + g["fz"] + g["fd"]

    def scatter_pair(self, st, partial):
        sc, rc = st["sc"], st["rc"]
        self.settle(st.get("left", []))
        copies = []
        for k, pair in enumerate((self.diag, self.sib)):
            sc[k] = partial(pair).astype(BF).reshape(sc.shape[1:])
            copies.append(self.to_sib(sc.at[k], rc.at[k]))
        return {"pair": copies, "st": st}

    def scatter_send(self, g, partial):
        st = g["st"]
        so, rc = st["so"], st["rc"]
        value = partial(self.zn)
        g["pair"][0].wait_recv()
        so[0] = (value + flat(rc[0].astype(F32))).astype(BF).reshape(so.shape[1:])
        g["d"] = [self.to_y(so.at[0, self.yn, :, h], st["rd"].at[:, h]) for h in self.halves]
        value = partial(self.s)
        g["pair"][1].wait_recv()
        so[1] = (value + flat(rc[1].astype(F32))).astype(BF).reshape(so.shape[1:])
        g["y"] = self.to_y(so.at[1, self.yn], st["ry"])

    def scatter_relay(self, g):
        st = g["st"]
        so = st["so"]
        g["z"] = []
        for c, h in zip(g["d"], self.halves, strict=True):
            c.wait_recv()
            so[0, self.y, :, h] = (so[0, self.y, :, h].astype(F32) + st["rd"][:, h].astype(F32)).astype(BF)
            g["z"].append(self.to_z(so.at[0, self.y, :, h], st["rz"].at[:, h]))

    def scatter_finish(self, g):
        st = g["st"]
        for c in g["z"] + [g["y"]]:
            c.wait_recv()
        total = st["so"][1, self.y].astype(F32) + st["rz"][...].astype(F32) + st["ry"][...].astype(F32)
        st["left"] = g["pair"] + g["d"] + g["z"] + [g["y"]]
        return total


    def place(self, s):
        return 1 + 2 * s + s // 2

    def project(self, w):
        def step(i, _):
            rows = flat(self.u1[i])
            out = dot(rows, w[...], NN).astype(BF)
            self.qkv[pl.ds(self.place(i), 2)] = out.reshape(2, 2 * WINDOW, out.shape[1])
            return 0

        lax.fori_loop(0, SUB, step, 0)

    def masks(self, s):
        at = 1 + s + s // 2
        before, own = self.starts[at - 1], self.starts[at]
        lane = lax.broadcasted_iota(jnp.int32, before.shape, 1)
        even = jnp.where(lane < WINDOW, pltpu.roll(before, WINDOW, 1), pltpu.roll(own, WINDOW, 1))
        shape = (WINDOW, 2 * WINDOW)
        i = lax.broadcasted_iota(jnp.int32, shape, 0)
        j = lax.broadcasted_iota(jnp.int32, shape, 1)
        square = (2 * WINDOW, 2 * WINDOW)
        later = lax.broadcasted_iota(jnp.int32, square, 0) > lax.broadcasted_iota(jnp.int32, square, 1)
        later = later.astype(F32).astype(BF)
        band = (j <= i + WINDOW) & (j > i)
        result = []
        for rows in (even, own):
            per_batch = []
            for batch in range(2):
                line = jnp.broadcast_to(rows[batch : batch + 1, :], shape)
                line = jnp.where(j <= i + WINDOW, line, 0.0).astype(BF)
                between = dot(line, later, NN)
                per_batch.append(band & (between < 0.5))
            result.append(per_batch)
        return result

    def tile(self, index, batch, part, head):
        cols = slice(part * 2 * HP + head * HP, part * 2 * HP + (head + 1) * HP)
        return self.qkv[index, batch * WINDOW : (batch + 1) * WINDOW, cols]

    def attend(self, first):
        def step(run, _):
            s = 2 * run + first
            allowed = self.masks(s)
            for half in range(2):
                p = self.place(s) + half
                for batch in range(2):
                    for head in range(2):
                        q = self.tile(p, batch, 0, head)
                        k = jnp.concatenate([self.tile(p - 1, batch, 1, head), self.tile(p, batch, 1, head)], axis=0)
                        v = jnp.concatenate([self.tile(p - 1, batch, 2, head), self.tile(p, batch, 2, head)], axis=0)
                        scores = dot(q, k, NT) * DH ** (-0.5)
                        scores = jnp.where(allowed[half][batch], scores, -1e30)
                        top = jnp.max(scores, axis=-1, keepdims=True)
                        weights = jnp.exp(scores - top)
                        probs = weights / jnp.sum(weights, axis=-1, keepdims=True)
                        self.probs[2 * s + half, 2 * batch + head] = probs
                        out = dot(probs.astype(BF), v, NN).astype(BF)
                        self.heads[s, half, batch * WINDOW : (batch + 1) * WINDOW, head * HP : (head + 1) * HP] = out
            return 0

        lax.fori_loop(0, 2, step, 0)

    def attend_back(self, s):
        run = s // 2
        for half in range(2):
            p = self.place(s) + half
            for batch in range(2):
                rows = slice(batch * WINDOW, (batch + 1) * WINDOW)
                for head in range(2):
                    cols = slice(head * HP, (head + 1) * HP)
                    q = self.tile(p, batch, 0, head)
                    k = jnp.concatenate([self.tile(p - 1, batch, 1, head), self.tile(p, batch, 1, head)], axis=0)
                    v = jnp.concatenate([self.tile(p - 1, batch, 2, head), self.tile(p, batch, 2, head)], axis=0)
                    probs = self.probs[2 * s + half, 2 * batch + head]
                    d_out = self.d_heads[s, half, rows, cols]
                    d_probs = dot(d_out, v, NT)
                    inner = jnp.sum(probs * d_probs, axis=-1, keepdims=True)
                    d_scores = (probs * (d_probs - inner)).astype(BF)
                    d_q = dot(d_scores, k, NN) * DH ** (-0.5)
                    d_k = dot(d_scores, q, TN) * DH ** (-0.5)
                    d_v = dot(probs.astype(BF), d_out, TN)
                    self.qkv[p, rows, head * HP : (head + 1) * HP] = d_q.astype(BF)
                    for part, grad in ((1, d_k), (2, d_v)):
                        slot = slice((part - 1) * 2 * HP + head * HP, (part - 1) * 2 * HP + (head + 1) * HP)
                        place = slice(part * 2 * HP + head * HP, part * 2 * HP + (head + 1) * HP)
                        done = self.carry[run, rows, slot] + grad[:WINDOW]
                        self.qkv[p - 1, rows, place] = done.astype(BF)
                        self.carry[run, rows, slot] = grad[WINDOW:]

    def grad_into(self, target, left, right):
        width = 256

        def step(m, _):
            cols = pl.ds(pl.multiple_of(m * width, width), width)
            parts = right()
            each = SUB // len(parts)
            total = 0.0
            for k, part in enumerate(parts):
                total = total + dot(flat(left[k * each : (k + 1) * each, :, :, cols]), part, TN)
            target[cols, :] = total.astype(BF)
            return 0

        lax.fori_loop(0, self.cfg["D"] // width, step, 0)

    def gate_and_up(self, plane):
        def step(k, _):
            i = 2 * plane + k
            rows = flat(self.u2[i])
            self.d_ga[i] = dot(rows, self.w_ga[...], NN).astype(BF).reshape(self.d_ga.shape[1:])
            self.d_up[i] = dot(rows, self.w_up[...], NN).astype(BF).reshape(self.d_up.shape[1:])
            return 0

        lax.fori_loop(0, 2, step, 0)

    def feed_forward(self, plane, ahead):
        ff = self.w_dn.shape[1]

        def step(k, _):
            i = 2 * plane + k
            if ahead:
                gate = flat(self.d_ga[i]).astype(F32)
                upward = flat(self.d_up[i]).astype(F32)
            else:
                rows = flat(self.u2[i])
                gate = dot(rows, self.w_ga[...], NN)
                upward = dot(rows, self.w_up[...], NN)
            d_hidden = dot(flat(self.g[i]), self.w_dn[...], NN)
            sig = jax.nn.sigmoid(gate)
            silu = gate * sig
            shape = (2, 2 * WINDOW, ff)
            self.hidden[i] = (silu * upward).astype(BF).reshape(shape)
            d_gate = d_hidden * upward * sig * (1.0 + gate * (1.0 - sig))
            self.d_ga[i] = d_gate.astype(BF).reshape(shape)
            self.d_up[i] = (d_hidden * silu).astype(BF).reshape(shape)
            return 0

        lax.fori_loop(0, 2, step, 0)

    def run(self):
        cfg = self.cfg
        me = (self.s, self.y)
        norm = lambda v: lax.rsqrt(jnp.mean(v * v, axis=-1, keepdims=True) + EPSILON)
        whole = lambda ref: [flat(ref[...])]

        everyone_here = self.barrier()
        if cfg["uneven"]:

            @pl.when(self.is_narrow)
            def _():
                for w in (self.w_ga, self.w_up, self.w_dn):
                    w[:, w.shape[1] - HP :] = jnp.zeros((w.shape[0], HP), BF)

        line = 1 + self.s + self.s // 2
        own_starts = self.doc_starts[...].astype(F32)
        fill = jnp.zeros((self.starts.shape[1] - own_starts.shape[0], own_starts.shape[1]), F32)
        self.starts[line] = jnp.concatenate([own_starts, fill], axis=0)
        own_line = self.starts.at[line]
        x = self.x_in[...].astype(F32)
        self.u1[me] = (x * norm(x)).astype(BF)
        if not cfg["whole"]:
            self.prepare("qkv")
        everyone_here()
        start_copies = [self.remote(own_line, own_line, self.mate(s)) for s in (self.sib, self.zn, self.diag)]
        qkv = self.columns_out("qkv")
        gather_one = self.gather_start(self.u1)
        self.columns_far(qkv)
        self.spread(qkv)
        for c in start_copies:
            c.wait_recv()
        rim_starts = self.rim_out([self.starts.at[2], self.starts.at[5]], lambda run: self.starts.at[3 * run])
        self.spread_same(qkv)
        self.gather_relay(gather_one)
        self.spread_rest(qkv)
        out = self.columns_out("out")
        self.columns_far(out)
        ga = self.columns_out("ga")
        self.gather_finish(gather_one)
        self.spread_done(qkv)

        self.project(self.w_qkv)
        rims = self.rim_out(
            [self.qkv.at[4, :, slice(2 * HP, 6 * HP)], self.qkv.at[9, :, slice(2 * HP, 6 * HP)]],
            lambda run: self.qkv.at[5 * run, :, slice(2 * HP, 6 * HP)],
        )
        self.spread(out)
        self.columns_far(ga)
        up = self.columns_out("up")
        self.attend(1)
        self.spread_same(out)
        self.spread_rest(out)
        for c in rim_starts + rims:
            c.wait_recv()
        self.spread(ga)
        self.columns_far(up)
        self.attend(0)
        self.spread(up)
        dn = self.columns_out("dn")
        self.spread_same(ga)
        self.spread_done(out)

        partial = lambda pair: dot(flat(self.heads[pair]), self.w_out[...], NT)
        stage = {n: getattr(self, n) for n in ("sc", "rc", "so", "rd", "rz", "ry")}
        scatter = self.scatter_pair(stage, partial)
        self.scatter_send(scatter, partial)
        self.scatter_relay(scatter)
        self.spread_rest(ga)
        self.g[me] = self.g_in[...]
        gather_g = self.gather_start(self.g)
        self.columns_far(dn)
        self.spread(dn)
        self.spread_same(up)
        self.resid[...] = self.x_in[...].astype(F32) + self.scatter_finish(scatter)
        resid = self.resid[...]
        self.u2[me] = (resid * norm(resid)).astype(BF)
        gather_two = self.gather_start(self.u2)
        self.spread_rest(up)
        self.spread_same(dn)
        self.gather_relay(gather_g)
        self.settle(self.given)
        self.spread_rest(dn)
        self.gather_relay(gather_two)
        for g in (ga, up):
            self.spread_done(g)
        self.gather_near(gather_two)
        self.gate_and_up(self.s // 2)
        self.gather_finish(gather_g)
        self.spread_done(dn)
        self.feed_forward(self.s // 2, True)
        self.gather_finish(gather_two, near=True)
        self.feed_forward(1 - self.s // 2, False)
        self.grad_into(self.g_dn, self.g, lambda: whole(self.hidden))
        sum_dn = self.collect(self.g_dn, self.slots_dn, "dn")
        partial = lambda pair: dot(flat(self.d_ga[pair]), self.w_ga[...], NT) + dot(
            flat(self.d_up[pair]), self.w_up[...], NT
        )
        scatter = self.scatter_pair(stage, partial)
        self.scatter_send(scatter, partial)
        self.collect_on(sum_dn, (0,))
        self.settle(self.gathered)
        self.grad_into(self.w_ga, self.u2, lambda: whole(self.d_ga))
        sum_ga = self.collect(self.w_ga, self.slots_ga, "ga")
        self.collect_on(sum_dn, (1,))
        self.scatter_relay(scatter)
        self.grad_into(self.w_up, self.u2, lambda: whole(self.d_up))
        sum_up = self.collect(self.w_up, self.slots_up, "up")
        d_unit = self.scatter_finish(scatter)
        resid = self.resid[...]
        scale = norm(resid)
        unit = resid * scale
        inner = jnp.mean(d_unit * unit, axis=-1, keepdims=True)
        self.in_grad[...] = self.g_in[...].astype(F32) + scale * (d_unit - unit * inner)
        self.d_r[me] = self.in_grad[...].astype(BF)
        self.settle(gather_g["copies"] + gather_two["copies"] + rims)
        gather_d = self.gather_start(self.d_r)
        self.collect_on(sum_ga, (0,))
        self.gather_relay(gather_d)
        self.collect_on(sum_ga, (1,))

        view = {
            "sc": self.u2.at[0:2],
            "so": self.u2.at[2:4],
            "rc": self.g.at[0:2],
            "rd": self.g.at[2, 0],
            "rz": self.g.at[2, 1],
            "ry": self.g.at[3, 0],
        }
        partial = lambda pair: dot(flat(self.hidden[pair]), self.w_dn[...], NT)
        mlp = self.scatter_pair(view, partial)
        self.scatter_send(mlp, partial)
        self.gather_finish(gather_d)

        d_heads = self.d_heads = self.d_ga.at[:, :, :, slice(0, 2 * HP)]

        def heads_back(i, _):
            value = dot(flat(self.d_r[i]), self.w_out[...], NN).astype(BF)
            d_heads[i] = value.reshape(2, 2 * WINDOW, 2 * HP)
            return 0

        lax.fori_loop(0, SUB, heads_back, 0)
        self.collect_done(sum_dn)
        backs = [self.columns_back(self.g_dn, self.o_dn, "dn")]

        self.carry[...] = jnp.zeros_like(self.carry)

        def first(run, _):
            self.attend_back(2 * run)
            return 0

        def second(run, _):
            self.attend_back(2 * run + 1)
            return 0

        lax.fori_loop(0, 2, first, 0)
        rim_back = self.rim_home(
            lambda run: self.qkv.at[5 * run, :, slice(2 * HP, 6 * HP)], [self.rim.at[0], self.rim.at[1]]
        )
        self.scatter_relay(mlp)
        self.collect_on(sum_up, (0,))
        lax.fori_loop(0, 2, second, 0)
        of_q, of_kv = slice(0, 2 * HP), slice(2 * HP, 6 * HP)
        g_q, g_kv = self.g_qkv.at[:, of_q], self.g_qkv.at[:, of_kv]
        self.grad_into(g_q, self.u1, lambda: [flat(self.qkv[1:5, :, of_q]), flat(self.qkv[6:10, :, of_q])])
        sum_q = self.collect(g_q, self.slots_qkv.at[:, :, of_q])
        self.collect_on(sum_up, (1,))
        self.collect_done(sum_ga)
        backs.append(self.columns_back(self.w_ga, self.o_ga, "ga"))
        for c in rim_back:
            c.wait_recv()
        for run in range(2):
            done = self.carry[run] + self.rim[run].astype(F32)
            self.qkv[5 * run + 4, :, 2 * HP :] = done.astype(BF)

        self.grad_into(g_kv, self.u1, lambda: [flat(self.qkv[1:5, :, of_kv]), flat(self.qkv[6:10, :, of_kv])])
        sum_kv = self.collect(g_kv, self.slots_qkv.at[:, :, of_kv])
        self.grad_into(self.w_out, self.d_r, lambda: whole(self.heads))
        sum_out = self.collect(self.w_out, self.slots_out)
        self.collect_on(sum_q)
        partial = lambda pair: dot(flat(self.qkv[pl.ds(self.place(pair), 2)]), self.w_qkv[...], NT)
        scatter = self.scatter_pair(stage, partial)
        self.scatter_send(scatter, partial)
        self.collect_on(sum_kv, (0,))
        self.scatter_relay(scatter)
        self.collect_on(sum_kv, (1,))
        self.collect_done(sum_up)
        backs.append(self.columns_back(self.w_up, self.o_up, "up"))
        self.out[...] = (self.resid[...] + self.scatter_finish(mlp)).astype(BF)
        back_to = lambda span: self.o_qkv.at[:, span] if cfg["whole"] else self.o_qkv.at[:, :, span]
        self.collect_done(sum_q)
        backs.append(self.columns_back(g_q, back_to(of_q)))
        self.collect_on(sum_out)
        self.collect_done(sum_kv)
        backs.append(self.columns_back(g_kv, back_to(of_kv)))
        self.collect_done(sum_out)
        backs.append(self.columns_back(self.w_out, self.o_out))
        d_unit = self.scatter_finish(scatter)
        x = self.x_in[...].astype(F32)
        scale = norm(x)
        unit = x * scale
        inner = jnp.mean(d_unit * unit, axis=-1, keepdims=True)
        self.in_grad[...] += scale * (d_unit - unit * inner)
        for wait in backs:
            wait()
        self.settle()

    def settle(self, copies=None):
        for c in self.sends:
            if copies is None or any(c is other for other in copies):
                c.wait_send()
        if copies is None:
            self.sends = []
        else:
            self.sends = [c for c in self.sends if not any(c is other for other in copies)]


def fused(cfg, width, weights, starts, x, g):
    d, db = cfg["D"], cfg["DB"]
    rows = 2 * WINDOW
    anywhere = pl.BlockSpec(memory_space=pl.ANY)
    vmem = pl.BlockSpec(memory_space=pltpu.VMEM)
    keys = ("qkv", "out", "ga", "up", "dn")
    result = (d,) if cfg["whole"] else (SUB, db)
    outs = [("out", (rows, d), BF, vmem), ("in_grad", (rows, d), F32, vmem)]
    outs += [("o_" + key, result + (width[key],), BF, anywhere) for key in keys]
    if cfg["whole"]:
        ins = [("sh_" + key, anywhere) for key in keys]
    else:
        ins = [(name, vmem) for name in ("raw_qkv", "raw_out", "raw_gu", "raw_dn", "gains")]
    ins += [(name, vmem) for name in ("doc_starts", "x_in", "g_in")]
    plane = (SUB, 2, rows)
    scratch = [("w_" + key, (d, width[key]), BF) for key in keys]
    scratch += [("g_" + key, (d, width[key]), BF) for key in ("qkv", "dn")]
    slot = 16 if cfg["whole"] else 2 * db
    scratch += [("slots_" + key, (6, slot, width[key]), BF) for key in keys]
    scratch += [(name, plane + (d,), BF) for name in ("u1", "u2", "g", "d_r")]
    scratch += [(name, plane + (width["out"],), BF) for name in ("heads",)]
    scratch += [(name, plane + (width["dn"],), BF) for name in ("hidden", "d_ga", "d_up")]
    scratch += [(name, (2, 2, rows, d), BF) for name in ("sc", "rc", "so")]
    scratch += [
        ("starts", (SUB + 2, 8, rows), F32),
        ("qkv", (2 * SUB + 2, rows, width["qkv"]), BF),
        ("probs", (2 * SUB, 4, WINDOW, 2 * WINDOW), F32),
        ("carry", (2, rows, 4 * HP), F32),
        ("rim", (2, rows, 4 * HP), BF),
        ("resid", (rows, d), F32),
        ("rd", (rows, d), BF),
        ("rz", (rows, d), BF),
        ("ry", (rows, d), BF),
    ]
    number = 220
    names = [n for n, _ in ins] + [n for n, *_ in outs] + [n for n, *_ in scratch]
    names += ["send_sems", "recv_sems", "local_sems"]

    def kernel(*refs):
        Kernel(cfg, dict(zip(names, refs, strict=True))).run()

    return pl.pallas_call(
        kernel,
        out_shape=[jax.ShapeDtypeStruct(shape, kind) for _, shape, kind, _ in outs],
        in_specs=[spec for _, spec in ins],
        out_specs=[spec for *_, spec in outs],
        scratch_shapes=[pltpu.VMEM(shape, kind) for _, shape, kind in scratch]
        + [
            pltpu.SemaphoreType.DMA((number,)),
            pltpu.SemaphoreType.DMA((number,)),
            pltpu.SemaphoreType.DMA((11,)),
        ],
        compiler_params=pltpu.CompilerParams(
            collective_id=0, has_side_effects=True, vmem_limit_bytes=64 * 2**20
        ),
    )(*weights, starts, x, g)


def assemble(spans, *refs):
    gains, sources, results, g_gain = refs[0], refs[1:10], refs[10:16], refs[16]
    held, made, sems = refs[17:26], refs[26:30], refs[30]
    copies = [pltpu.make_async_copy(a, b, sems.at[k]) for k, (a, b) in enumerate(zip(sources, held, strict=True))]
    for c in copies:
        c.start()
    ready = made + held[7:]
    back = [pltpu.make_async_copy(a, b, sems.at[9 + k]) for k, (a, b) in enumerate(zip(ready, results, strict=True))]
    o_ga, o_up, w_gu, o_dn, o_qkv, w_qkv, o_out = held[:7]
    g_gu, g_dn, g_qkv, g_out = made
    db = w_qkv.shape[1]
    lines = gains[...].astype(F32)
    same = eye(db)

    def column(k):
        return jnp.sum(jnp.where(same, jnp.broadcast_to(lines[k : k + 1, :], (db, db)), 0.0), axis=1, keepdims=True)

    def put(k, total):
        g_gain[k : k + 1, :] = jnp.sum(jnp.where(same, jnp.broadcast_to(total, (db, db)), 0.0), axis=0, keepdims=True)

    gain = column(1)
    total = jnp.zeros((db, 1), F32)
    copies[2].wait()
    for k, ref in enumerate((o_ga, o_up)):
        copies[k].wait()
        value = jnp.concatenate([ref[s, :, : p.stop - p.start].astype(F32) for s, p in enumerate(spans)], axis=1)
        total = total + jnp.sum(value * w_gu[k].astype(F32), axis=1, keepdims=True)
        g_gu[k] = value * gain
    back[0].start()
    put(1, total)
    copies[3].wait()
    g_dn[...] = jnp.concatenate([o_dn[s, :, : p.stop - p.start].astype(F32) for s, p in enumerate(spans)], axis=1)
    back[1].start()
    gain = column(0)
    total = jnp.zeros((db, 1), F32)
    copies[4].wait()
    copies[5].wait()
    for k in range(3):
        parts = []
        for s in range(SUB):
            for h in range(2):
                start = (2 * k + h) * HP
                parts.append(o_qkv[s, :, start : start + DH].astype(F32))
        value = jnp.concatenate(parts, axis=1)
        total = total + jnp.sum(value * w_qkv[k].astype(F32), axis=1, keepdims=True)
        g_qkv[k] = value * gain
    back[2].start()
    put(0, total)
    copies[6].wait()
    parts = [o_out[s, :, h * HP : h * HP + DH].astype(F32) for s in range(SUB) for h in range(2)]
    g_out[...] = jnp.concatenate(parts, axis=1)
    back[3].start()
    for k in range(2):
        copies[7 + k].wait()
        back[4 + k].start()
    for c in back:
        c.wait()


def body(size, tokens, doc_starts, w_qkv, w_out, w_gate_up, w_down, gains, cotangent):
    batches, rows, d = tokens.shape
    db = w_qkv.shape[1]
    ff = w_gate_up.shape[2] // SUB
    ffp = -(-ff // HP) * HP
    heads = w_qkv.shape[2] // (SUB * DH)
    whole = size != 16 or db % 16 != 0
    uneven = not whole and w_gate_up.shape[2] == SUB * ffp - HP
    sizes = [ffp - HP * (uneven and s == NARROW) if uneven else ff for s in range(SUB)]
    spans = [slice(sum(sizes[:s]), sum(sizes[: s + 1])) for s in range(SUB)]
    cfg = {"D": d, "NH": size // 8, "DB": db, "spans": spans, "uneven": uneven, "whole": whole}
    width = {"qkv": 3 * heads * HP, "out": heads * HP, "ga": ffp, "up": ffp, "dn": ffp}
    acts = [doc_starts, tokens.reshape(batches * rows, d), cotangent.reshape(batches * rows, d)]

    def results(out, in_grad, g_qkv, g_out, g_gu, g_dn, gain_sums):
        gain_sums = gain_sums + lax.ppermute(gain_sums, "tp", [(0, 1), (1, 0)])
        return (out.reshape(tokens.shape), in_grad.reshape(tokens.shape), g_qkv, g_out, g_gu, g_dn, gain_sums)

    if not whole:
        out, in_grad, *grads = fused(cfg, width, [w_qkv, w_out.T, w_gate_up, w_down.T, gains], *acts)
        o_qkv, o_out, o_ga, o_up, o_dn = grads
        sources = [o_ga, o_up, w_gate_up, o_dn, o_qkv, w_qkv, o_out, out, in_grad]
        made = [jax.ShapeDtypeStruct(v.shape, F32) for v in (w_gate_up, w_down.T, w_qkv, w_out.T)]
        shapes = made + [jax.ShapeDtypeStruct(v.shape, v.dtype) for v in (out, in_grad)]
        shapes.append(jax.ShapeDtypeStruct(gains.shape, F32))
        anywhere, vmem = pl.BlockSpec(memory_space=pl.ANY), pl.BlockSpec(memory_space=pltpu.VMEM)
        g_gu, g_dn, g_qkv, g_out, out, in_grad, gain_sums = pl.pallas_call(
            functools.partial(assemble, spans),
            out_shape=shapes,
            in_specs=[vmem] + [anywhere] * 9,
            out_specs=[anywhere] * 6 + [vmem],
            scratch_shapes=[pltpu.VMEM(v.shape, v.dtype) for v in sources + made] + [pltpu.SemaphoreType.DMA((15,))],
            compiler_params=pltpu.CompilerParams(vmem_limit_bytes=63 * 2**20),
        )(gains, *sources)
        return results(out, in_grad, g_qkv, g_out.T, g_gu, g_dn.T, gain_sums)

    gain = gains.astype(F32)
    sh_qkv = (w_qkv.astype(F32) * gain[0][None, :, None]).astype(BF).reshape(3, db, SUB, heads, DH)
    sh_qkv = padded(sh_qkv, HP).transpose(2, 1, 0, 3, 4).reshape(SUB, db, 3 * heads * HP)
    sh_out = w_out.T.reshape(db, SUB, heads, DH)
    sh_out = padded(sh_out, HP).transpose(1, 0, 2, 3).reshape(SUB, db, heads * HP)
    scaled = (w_gate_up.astype(F32) * gain[1][None, :, None]).astype(BF).reshape(2, db, SUB, ff)
    sh_ga, sh_up = [padded(scaled[k], ffp).transpose(1, 0, 2) for k in range(2)]
    sh_dn = padded(w_down.T.reshape(db, SUB, ff), ffp).transpose(1, 0, 2)
    f = lax.axis_index("fsdp")
    s = (f // 4) % 2 * 2 + f % 2
    everyone = [lax.all_gather(v, "fsdp", axis=1, tiled=True) for v in (sh_qkv, sh_out, sh_ga, sh_up, sh_dn)]
    shares = [lax.dynamic_index_in_dim(v, s, 0, keepdims=False) for v in everyone]
    out, in_grad, *grads = fused(cfg, width, shares, *acts)
    mine = (jnp.arange(SUB) == s)[:, None, None]
    g_qkv, g_out, g_ga, g_up, g_dn = [
        lax.psum_scatter(jnp.where(mine, v[None], 0).astype(BF), "fsdp", scatter_dimension=1, tiled=True).astype(F32)
        for v in grads
    ]
    g_qkv = g_qkv.reshape(SUB, db, 3, heads, HP)[..., :DH].transpose(2, 1, 0, 3, 4).reshape(w_qkv.shape)
    g_out = g_out.reshape(SUB, db, heads, HP)[..., :DH].transpose(0, 2, 3, 1).reshape(w_out.shape)
    g_gu = jnp.stack([v[..., :ff].transpose(1, 0, 2).reshape(w_gate_up.shape[1:]) for v in (g_ga, g_up)])
    g_dn = g_dn[..., :ff].transpose(0, 2, 1).reshape(w_down.shape)
    gain_sums = jnp.stack(
        [
            jnp.sum(g_qkv * w_qkv.astype(F32), axis=(0, 2)),
            jnp.sum(g_gu * w_gate_up.astype(F32), axis=(0, 2)),
        ]
    )
    g_qkv, g_gu = g_qkv * gain[0][None, :, None], g_gu * gain[1][None, :, None]
    return results(out, in_grad, g_qkv, g_out, g_gu, g_dn, gain_sums)


def solution(mesh):
    in_specs = (
        P(None, ("fsdp", "tp"), None),
        P(None, "fsdp"),
        P(None, "fsdp", "tp"),
        P("tp", "fsdp"),
        P(None, "fsdp", "tp"),
        P("tp", "fsdp"),
        P(None, "fsdp"),
        P(None, ("fsdp", "tp"), None),
    )
    out_specs = (
        P(None, ("fsdp", "tp"), None),
        P(None, ("fsdp", "tp"), None),
        P(None, "fsdp", "tp"),
        P("tp", "fsdp"),
        P(None, "fsdp", "tp"),
        P("tp", "fsdp"),
        P(None, "fsdp"),
    )
    return jax.shard_map(
        functools.partial(body, mesh.shape["fsdp"]), mesh=mesh, in_specs=in_specs, out_specs=out_specs, check_vma=False
    )
```
